32 devices in a mesh: section: 2 (over x), expert: 4 (over z), hidden: 4 (over y, core).
Axes of the slice: x: 2, y: 2, z: 4, core: 2. Of those that a mesh axis runs over, the one named last changes fastest.
Arguments:
- tokens: bfloat16 [4, 64, 7168], P(None, 'expert', 'hidden'), may hold values from -12 to 12
- gate_up: bfloat16 [2, 7168, 2, 16384], P('section', 'hidden', None, 'expert'), may hold values from -0.0625 to 0.0625
- down_proj: bfloat16 [2, 16384, 7168], P('section', 'expert', 'hidden'), may hold values from -0.1875 to 0.1875
- routes: int32 [2, 4, 64, 2], P('section', None, 'expert'), may hold values from 0 to 15, all different within a row; in each aligned block of 16 rows (0 to 15, 16 to 31, ..., all dimensions but the last counted through in order) at most 3 rows name the same one
- gate_weights: bfloat16 [2, 4, 64, 2], P('section', None, 'expert'), may hold values from 0.099609375 to 0.59765625
Outputs:
- layer_outputs: bfloat16 [2, 4, 64, 7168], P('section', None, 'expert', 'hidden')
The draws below stay inside these ranges and needn't reach their ends.
Inputs may be any that keep to these rules, and one draw needn't show every extreme that they name: `routes`: in every layer and micro-batch a token names 2 different experts, and the 16 tokens of one device (aligned blocks of 16 rows) name any one expert at most 3 times; some expert is named exactly 3 times in some block.
All inputs are finite; a program needn't handle non-finite values.
Results may differ from the reference program's by a relative error of at most 0.008.
Values may be sent and summed in bfloat16 or wider, within the bound.
No kernel may reach another device: no remote copies, remote signals or barrier semaphores. Data moves between devices by JAX's collectives and lax.ppermute only.
A program may use at most 192 MiB of HBM per device.

```python
import math
import jax
import jax.numpy as jnp
import numpy as np
from jax import lax

D = 7168
FFE = 1024
EXPERTS = 16
TOP = 2
TOK_DEV = 16
MICRO = 4
LAYERS = 2
TOKENS = 64
CAP = 3
N_EXPERT = 4


def draw_tokens(key, part):
    key_base, key_rough = jax.random.split(key, 2)
    position = jnp.arange(D, dtype=jnp.float32) / D
    feature_ramp = 0.5 * jnp.exp(position * jnp.log(3.0))
    feature_rough = jax.random.uniform(key_rough, (D,), jnp.float32, 0.6, 1.6)
    base_values = jax.random.truncated_normal(key_base, -5.0, 5.0, (MICRO, TOKENS, D), jnp.float32)
    return (base_values * feature_ramp * feature_rough).astype(jnp.bfloat16)


def block_scale(stream_key, shape, cuts, least, largest):
    def one(dim, shards_of):
        steps = jax.random.uniform(jax.random.fold_in(jax.random.fold_in(stream_key, 6), dim), (shards_of,), jnp.float32, least / len(cuts), largest / len(cuts))
        return jnp.repeat(jnp.exp(steps), shape[dim] // shards_of).reshape((-1,) + (1,) * (len(shape) - dim - 1))

    factor_of = one(*cuts[0])
    for cut in cuts[1:]:
        factor_of = factor_of * one(*cut)
    return factor_of


def assign_block(rng, own, number, rows, amount, top, most, lean):
    ranking = jax.random.permutation(rng, amount)
    heavy_load, ordinary = load_shares(amount, rows * top, most, lean, True), load_shares(amount, rows * top, most, lean, False)
    places = jnp.arange(amount)

    def named(lengths, rotation):
        used = int((lengths > 0).sum())
        fixed = max(1, used // 4)
        moved = fixed + (places - fixed + rotation * (used - fixed)) % max(1, amount - fixed)
        return jnp.zeros((amount,), jnp.int32).at[ranking[jnp.where(places < fixed, places, moved)]].set(jnp.asarray(lengths, jnp.int32))

    lengths = jnp.where(number % 4 == 0, named(heavy_load, number // 4), named(ordinary, number - number // 4 - 1))
    mixed = jax.random.permutation(jax.random.fold_in(own, 3), amount)
    source_of, sink = mixed[0:amount // 2 * 2:2], mixed[1:amount // 2 * 2:2]
    slack = jnp.minimum(lengths[source_of] - 1, most - lengths[sink]) // 2
    slack = jnp.where((source_of == ranking[0]) | (sink == ranking[0]) | (lengths[sink] == 0), 0, jnp.maximum(slack, 0))
    moved = jax.random.randint(jax.random.fold_in(own, 4), (amount // 2,), 0, 1 << 20) % (slack + 1)
    lengths = lengths.at[source_of].add(-moved).at[sink].add(moved)
    items = jnp.searchsorted(jnp.cumsum(lengths), jnp.arange(rows * top), side="right").astype(jnp.int32)
    listing = items.reshape(top, rows).T
    listing = listing[jax.random.permutation(jax.random.fold_in(own, 1), rows)]
    rotation = jax.random.randint(jax.random.fold_in(own, 2), (rows, 1), 0, top)
    return jnp.take_along_axis(listing, (jnp.arange(top)[None, :] + rotation) % top, axis=1)


def load_shares(number_of, total, reach, skew, full):
    weights = [(1 << 20) // math.isqrt(grade ** skew) + 1 for grade in range(1, number_of + 1)]
    largest = reach if full else min(reach, max(-(-total // number_of), total * weights[0] // sum(weights)))
    least = 1 if total - largest >= number_of - 1 else 0
    given, rest = [largest] + [least] * (number_of - 1), total - largest - least * (number_of - 1)
    while rest > 0:
        candidates = [i for i in range(1, number_of) if given[i] < largest] or [i for i in range(1, number_of) if given[i] < reach]
        mass, budget = sum([weights[i] for i in candidates]), rest
        for i in candidates:
            extra = min(reach - given[i], max(1, budget * weights[i] // mass), rest)
            given[i] = given[i] + extra
            rest = rest - extra
    return np.array(given)


def bell_draw(key, shape, deviation, bound, cuts=(), kind=jnp.bfloat16):
    level = block_scale(key, shape, cuts, -0.22, 0.18) if cuts else 1.0
    result = jax.random.normal(key, shape, jnp.float32) * deviation * level
    return jnp.minimum(jnp.maximum(result, -bound), bound).astype(kind)


def setup_inputs(seed: int = 0) -> dict:
    key_of = jax.random.split(jax.random.key(seed), 6)
    tokens = draw_tokens(jax.random.fold_in(key_of[5], 71), 0)
    gate_up = bell_draw(key_of[1], (LAYERS, D, 2, EXPERTS * FFE), D ** -0.5, 0.0625, ((0, 2), (1, 4), (3, 4)))
    down_proj = bell_draw(key_of[2], (LAYERS, EXPERTS * FFE, D), FFE ** -0.5, 0.1875, ((0, 2), (1, 4), (2, 4)))
    routes_keys = jax.random.split(jax.random.fold_in(key_of[3], 1), LAYERS * MICRO * TOKENS // TOK_DEV)
    routes_turns = jax.random.permutation(jax.random.fold_in(key_of[3], 3), LAYERS * MICRO * TOKENS // TOK_DEV)
    routes = jax.vmap(lambda own, number: assign_block(jax.random.fold_in(key_of[3], 2), own, number, TOK_DEV, EXPERTS, TOP, CAP, 1))(routes_keys, routes_turns).reshape((LAYERS, MICRO, TOKENS, TOP))
    gate_weights = jnp.clip(0.099609375 + 0.49804688 * jax.random.uniform(key_of[4], (LAYERS, MICRO, TOKENS, TOP), jnp.float32) ** block_scale(key_of[4], (LAYERS, MICRO, TOKENS, TOP), ((0, 2), (2, 4)), -0.2, 0.2), 0.099609375, 0.59765625).astype(jnp.bfloat16)
    return {"tokens": tokens, "gate_up": gate_up, "down_proj": down_proj, "routes": routes, "gate_weights": gate_weights}


EPS = 1e-06

def slot_tables(route_rows, gate_rows):
    expert_ids = jnp.arange(EXPERTS, dtype=jnp.int32)
    matches = route_rows[:, :, None] == expert_ids[None, None, :]
    chosen = lax.optimization_barrier(jnp.sum(matches.astype(jnp.int32), axis=1, dtype=jnp.int32))
    weight_dense = lax.optimization_barrier(jnp.sum(jnp.where(matches, gate_rows.astype(jnp.float32)[:, :, None], jnp.float32(0.0)), axis=1))
    blocked = chosen.reshape(N_EXPERT, TOK_DEV, EXPERTS)
    rank = (jnp.cumsum(blocked, axis=1, dtype=jnp.int32) - blocked).reshape(TOKENS, EXPERTS)
    source = jnp.arange(TOKENS, dtype=jnp.int32) // TOK_DEV
    slot_index = source[:, None] * CAP + rank
    return (chosen, slot_index, weight_dense)

def moe_layer(hidden_state, gate_up, down_proj, route_rows, gate_rows):
    chosen, slot_index, weight_dense = slot_tables(route_rows, gate_rows)
    slot_total = N_EXPERT * CAP
    unit_block = min(FFE, EXPERTS * FFE // N_EXPERT)
    up_table = gate_up.reshape(D, 2, EXPERTS, FFE)
    down_table = down_proj.reshape(EXPERTS, FFE, D)
    token_ids = jnp.arange(TOKENS, dtype=jnp.int32)

    def one_expert(running_sum, expert):
        column_slot = lax.dynamic_index_in_dim(slot_index, expert, 1, keepdims=False)
        column_hit = lax.dynamic_index_in_dim(chosen, expert, 1, keepdims=False)
        column_weight = lax.dynamic_index_in_dim(weight_dense, expert, 1, keepdims=False)
        target = jnp.where(column_hit == 1, column_slot, slot_total).astype(jnp.int32)
        slot_token = jnp.zeros((slot_total,), jnp.int32).at[target].set(token_ids, mode='drop')
        filled = jnp.zeros((slot_total,), jnp.float32).at[target].set(jnp.float32(1.0), mode='drop')
        slot_rows = (hidden_state[slot_token].astype(jnp.float32) * filled[:, None]).astype(jnp.bfloat16)
        slot_weight = column_weight[slot_token] * filled
        w_in = lax.dynamic_index_in_dim(up_table, expert, 2, keepdims=False).reshape(D, 2 * FFE)
        projected = jnp.dot(slot_rows, w_in, preferred_element_type=jnp.float32)
        widened = slot_rows.astype(jnp.float32)
        norm_scale = lax.rsqrt(lax.optimization_barrier(jnp.sum(widened * widened, axis=1, keepdims=True)) / D + EPS)
        activated = (jax.nn.silu(norm_scale * projected[:, :FFE]) * (norm_scale * projected[:, FFE:])).astype(jnp.bfloat16)
        w_out = lax.dynamic_index_in_dim(down_table, expert, 0, keepdims=False)
        for piece_index in range(FFE // unit_block):
            low = piece_index * unit_block
            partial_value = jnp.dot(activated[:, low:low + unit_block], w_out[low:low + unit_block], preferred_element_type=jnp.float32).astype(jnp.bfloat16)
            running_sum = running_sum.at[slot_token].add(slot_weight[:, None] * partial_value.astype(jnp.float32))
        return (running_sum, None)
    start_sum = jnp.zeros((TOKENS, D), jnp.float32)
    mixed, _ = lax.scan(one_expert, start_sum, jnp.arange(EXPERTS, dtype=jnp.int32))
    return (hidden_state.astype(jnp.float32) + mixed).astype(jnp.bfloat16)

def reference(tokens, gate_up, down_proj, routes, gate_weights):
    batch_outputs = []
    for batch_index in range(MICRO):
        hidden_state = tokens[batch_index]
        layer_list = []
        for layer_index in range(LAYERS):
            hidden_state = moe_layer(hidden_state, gate_up[layer_index], down_proj[layer_index], routes[layer_index, batch_index], gate_weights[layer_index, batch_index])
            layer_list.append(hidden_state)
        batch_outputs.append(jnp.stack(layer_list))
    return jnp.stack(batch_outputs, axis=1)
```

```python
import functools

import jax
import jax.numpy as jnp
import numpy as np
from jax import lax
from jax.experimental import pallas as pl
from jax.experimental.pallas import tpu as pltpu
from jax.sharding import PartitionSpec as P

D = 7168
FFE = 1024
CAP = 3
EPS = 1e-06
TILE = 16
SMEM = pl.BlockSpec(memory_space=pltpu.SMEM)
VMEM = pl.BlockSpec(memory_space=pltpu.VMEM)
HBM = pl.BlockSpec(memory_space=pl.ANY)
BF16 = jnp.bfloat16
F32 = jnp.float32


def padded(count, unit=TILE):
    return -(-count // unit) * unit


def dot(a, b):
    return jnp.dot(a, b, preferred_element_type=F32)


def swap(value, axis, step):
    count = lax.axis_size(axis)
    return lax.ppermute(value, axis, [(i, i ^ step) for i in range(count)])


class Sizes:
    def __init__(self, tokens, gate_up, peers, splits):
        self.peers, self.splits = peers, splits
        self.micro, self.tok, self.width = tokens.shape
        self.rows = self.micro * self.tok
        units_dev = gate_up.shape[3]
        self.units_dev = units_dev
        self.units = min(FFE, units_dev)
        self.local = units_dev // self.units
        self.share = self.units // splits
        self.slots = self.micro * CAP
        self.pay = padded(self.local * self.slots)
        self.all_pay = peers * self.pay
        self.pieces = peers if peers <= 8 else 1
        self.piece = self.all_pay // self.pieces
        self.each = padded(peers * self.slots)
        self.all_each = self.local * self.each
        self.lanes = 2 * self.share
        self.square_rows = padded(2 * -(-self.all_each // self.lanes))

    def slot_table(self):
        row = np.arange(self.all_pay)
        step, place = row // self.pay, row % self.pay
        expert, batch, rank = place // self.slots, place // CAP % self.micro, place % CAP
        rank = np.where(place < self.local * self.slots, rank, -1)
        return np.stack([step, expert, batch, rank], axis=1).astype(np.int32)

    def reorder(self):
        matrix = np.zeros((self.all_each, self.all_pay), np.float32)
        for expert in range(self.local):
            for step in range(self.peers):
                for slot in range(self.slots):
                    matrix[
                        expert * self.each + step * self.slots + slot,
                        step * self.pay + expert * self.slots + slot,
                    ] = 1.0
        return matrix


def pack_kernel(z, me_ref, table_ref, routes_ref, gates_ref, rows_ref, *outs):
    table = table_ref[...]
    owner = table[:, 0:1] ^ me_ref[0] if z.pieces > 1 else table[:, 0:1]
    if z.units_dev >= FFE:
        expert = owner * z.local + table[:, 1:2]
    else:
        expert = lax.shift_right_logical(owner, (FFE // z.units_dev).bit_length() - 1)
    batch, rank = table[:, 2:3], table[:, 3:4]
    shape = (z.all_pay, z.rows)
    token = lax.broadcasted_iota(jnp.int32, shape, 1)
    start = batch * z.tok
    same = (token >= start) & (token < start + z.tok)
    first = (routes_ref[0:1, :] == expert) & same
    second = (routes_ref[1:2, :] == expert) & same
    chosen = jnp.where(first | second, F32(1.0), F32(0.0))
    square = (z.rows, z.rows)
    before = lax.broadcasted_iota(jnp.int32, square, 0) < lax.broadcasted_iota(jnp.int32, square, 1)
    before = jnp.where(before, F32(1.0), F32(0.0)).astype(BF16)
    count = dot(chosen.astype(BF16), before)
    hits = jnp.where(count == rank.astype(F32), chosen, F32(0.0))
    weight = jnp.where(first, gates_ref[0:1, :], F32(0.0)) + jnp.where(second, gates_ref[1:2, :], F32(0.0))
    outs[z.pieces][...] = (hits * weight).astype(BF16)
    hits = hits.astype(BF16)
    rows = rows_ref[...]
    for step in range(z.pieces):
        outs[step][...] = dot(hits[step * z.piece:(step + 1) * z.piece], rows).astype(BF16)


def up_kernel(z, parts, h_ref, order_ref, *refs):
    received, weights = refs[:z.pieces], refs[z.pieces]
    outs = refs[z.pieces + 1:z.pieces + 1 + z.splits]
    stacked, spread, held, staged, sems = refs[z.pieces + 1 + z.splits:]
    flat = weights.reshape(2 * z.width, z.units_dev)
    depth = 2 * z.width // parts

    def fetch(expert, part):
        return pltpu.make_async_copy(
            flat.at[pl.ds(part * depth, depth), pl.ds(expert * z.units, z.units)],
            held.at[expert * parts + part],
            sems.at[expert * parts + part],
        )

    for expert in range(z.local):
        for part in range(parts):
            fetch(expert, part).start()
    for step in range(z.pieces):
        stacked[step * z.piece:(step + 1) * z.piece, :] = received[step][...]
    rows = dot(order_ref[...], stacked[...])
    squares = rows * rows
    high = squares.astype(BF16)
    low = (squares - high.astype(F32)).astype(BF16)
    ones = jnp.ones((TILE, z.width), BF16)
    across = (((1,), (1,)), ((), ()))
    sums = lax.dot_general(ones, high, across, preferred_element_type=F32) + lax.dot_general(
        ones, low, across, preferred_element_type=F32
    )
    rows = rows.astype(BF16)
    block = 128
    shape = (block, 2 * block)
    target = lax.broadcasted_iota(jnp.int32, shape, 1) - 2 * lax.broadcasted_iota(jnp.int32, shape, 0)
    for side in range(2):
        placing = jnp.where(target == side, F32(1.0), F32(0.0)).astype(BF16)
        for piece in range(z.width // block):
            low_col = 2 * block * piece
            part, offset = low_col // depth, low_col % depth
            wide = dot(rows[:, piece * block:(piece + 1) * block], placing).astype(BF16)
            for expert in range(z.local):
                spread[
                    expert * parts + part,
                    side * z.each:(side + 1) * z.each,
                    offset:offset + 2 * block,
                ] = wide[expert * z.each:(expert + 1) * z.each]
    sum_high = sums.astype(BF16).astype(F32)
    sum_low = sums - sum_high
    row_id = lax.broadcasted_iota(jnp.int32, (z.square_rows, z.lanes), 0)
    extra = jnp.zeros((z.square_rows, z.lanes), F32)
    for piece in range(-(-z.all_each // z.lanes)):
        begin = piece * z.lanes
        end = min(z.all_each, begin + z.lanes)
        both = []
        for value in (sum_high, sum_low):
            value = value[0:1, begin:end]
            if end - begin < z.lanes:
                value = jnp.concatenate([value, jnp.zeros((1, z.lanes - end + begin), F32)], axis=1)
            both.append(value)
        extra = jnp.where(row_id == 2 * piece, both[0], jnp.where(row_id == 2 * piece + 1, both[1], extra))
    for piece in range(z.splits):
        staged[piece, z.all_each:, :] = extra.astype(BF16)
    for expert in range(z.local):
        total = None
        for part in range(parts):
            fetch(expert, part).wait()
            value = dot(spread[expert * parts + part], held[expert * parts + part])
            total = value if total is None else total + value
        total = total.astype(BF16)
        for piece in range(z.splits):
            columns = slice(piece * z.share, (piece + 1) * z.share)
            here = slice(expert * z.each, (expert + 1) * z.each)
            staged[piece, here, 0:z.share] = total[:z.each, columns]
            staged[piece, here, z.share:2 * z.share] = total[z.each:, columns]
    for step in range(z.splits):
        outs[step][...] = staged[h_ref[0] ^ step]


def act_kernel(z, *refs):
    out = refs[z.splits]
    total = refs[0][...].astype(F32)
    for step in range(1, z.splits):
        total = total + refs[step][...].astype(F32)
    extra = total[z.all_each:, :]
    for piece in range(-(-z.all_each // z.lanes)):
        begin = piece * z.lanes
        end = min(z.all_each, begin + z.lanes)
        shape = (end - begin, end - begin)
        line = (extra[2 * piece:2 * piece + 1, :] + extra[2 * piece + 1:2 * piece + 2, :])[:, :end - begin]
        diagonal = lax.broadcasted_iota(jnp.int32, shape, 0) == lax.broadcasted_iota(jnp.int32, shape, 1)
        sums = jnp.sum(jnp.where(diagonal, line, F32(0.0)), axis=1, keepdims=True)
        scale = lax.rsqrt(sums / D + EPS)
        gate = scale * total[begin:end, :z.share]
        up = scale * total[begin:end, z.share:]
        out[begin:end, :] = (gate / (F32(1.0) + jnp.exp(-gate)) * up).astype(BF16)


def down_kernel(z, h_ref, order_ref, *refs):
    units, weights = refs[:z.splits], refs[z.splits]
    outs = refs[z.splits + 1:z.splits + 1 + z.pieces]
    held, result, sems = refs[z.splits + 1 + z.pieces:]

    def fetch(expert):
        return pltpu.make_async_copy(
            weights.at[0, pl.ds(expert * z.units, z.units), :], held.at[expert], sems.at[expert]
        )

    for expert in range(z.local):
        fetch(expert).start()
    for expert in range(z.local):
        fetch(expert).wait()
        here = slice(expert * z.each, (expert + 1) * z.each)
        total = None
        for step in range(z.splits):
            low = pl.multiple_of((h_ref[0] ^ step) * z.share, z.share)
            value = dot(units[step][here, :], held[expert, pl.ds(low, z.share), :])
            total = value if total is None else total + value
        result[here, :] = total.astype(BF16)
    for step in range(z.pieces):
        rows = order_ref[step * z.piece:(step + 1) * z.piece, :]
        outs[step][...] = dot(rows, result[...]).astype(BF16)


def combine_kernel(z, own_ref, weight_ref, rows_ref, kept_ref, *refs):
    returned, out, stacked = refs[:z.pieces], refs[z.pieces], refs[z.pieces + 1]
    for step in range(z.pieces):
        stacked[step * z.piece:(step + 1) * z.piece, :] = returned[step][...]
    mixed = lax.dot_general(
        weight_ref[...], stacked[...], (((0,), (0,)), ((), ())), preferred_element_type=F32
    )
    value = (rows_ref[...].astype(F32) + mixed).astype(BF16)
    out[...] = jnp.where(own_ref[0] == 1, value, kept_ref[...])


def call(kernel, z, megabytes, outs, in_specs, scratch, *args):
    z = z if isinstance(z, tuple) else (z,)
    results = pl.pallas_call(
        functools.partial(kernel, *z),
        out_shape=outs,
        in_specs=in_specs,
        out_specs=[VMEM] * len(outs),
        scratch_shapes=scratch,
        compiler_params=pltpu.CompilerParams(vmem_limit_bytes=megabytes * 2**20),
    )(*args)
    return list(results)


def on_device(tokens, gate_up, down_proj, routes, gate_weights):
    sections = lax.axis_size("section")
    section_id = lax.axis_index("section")
    z = Sizes(tokens, gate_up, lax.axis_size("expert"), lax.axis_size("hidden"))
    me = lax.axis_index("expert").astype(jnp.int32).reshape(1)
    h = lax.axis_index("hidden").astype(jnp.int32).reshape(1)
    table = jnp.asarray(z.slot_table())
    order = z.reorder()
    back = jnp.asarray(order.T, BF16)
    order = jnp.asarray(order, BF16)
    routes2 = routes[0].transpose(2, 0, 1).reshape(2, z.rows)
    gates2 = gate_weights[0].astype(F32).transpose(2, 0, 1).reshape(2, z.rows)
    parts = 2 if z.width % 256 == 0 else 1
    shape = jax.ShapeDtypeStruct
    pay = shape((z.piece, z.width), BF16)
    partial = shape((z.all_each + z.square_rows, z.lanes), BF16)

    def exchanged(pieces):
        if z.pieces == 1:
            return [lax.all_to_all(pieces[0], "expert", split_axis=0, concat_axis=0, tiled=True)]
        return pieces[:1] + [swap(pieces[step], "expert", step) for step in range(1, z.pieces)]

    def layer(rows, kept, tick):
        *sent, weight = call(
            pack_kernel, z, 6,
            [pay] * z.pieces + [shape((z.all_pay, z.rows), BF16)],
            [SMEM] + [VMEM] * 4, [],
            me, table, routes2, gates2, rows,
        )
        received = exchanged(sent)
        sums = call(
            up_kernel, (z, parts), 40,
            [partial] * z.splits,
            [SMEM, VMEM] + [VMEM] * z.pieces + [HBM],
            [
                pltpu.VMEM((z.all_pay, z.width), BF16),
                pltpu.VMEM((z.local * parts, 2 * z.each, 2 * z.width // parts), BF16),
                pltpu.VMEM((z.local * parts, 2 * z.width // parts, z.units), BF16),
                pltpu.VMEM((z.splits,) + partial.shape, BF16),
                pltpu.SemaphoreType.DMA((z.local * parts,)),
            ],
            h, order, *received, gate_up,
        )
        sums = sums[:1] + [swap(sums[step], "hidden", step) for step in range(1, z.splits)]
        units = call(
            act_kernel, z, 6, [shape((z.all_each, z.share), BF16)], [VMEM] * z.splits, [], *sums
        )[0]
        units = [units] + [swap(units, "hidden", step) for step in range(1, z.splits)]
        outgoing = call(
            down_kernel, z, 22,
            [pay] * z.pieces,
            [SMEM, VMEM] + [VMEM] * z.splits + [HBM],
            [
                pltpu.VMEM((z.local, z.units, z.width), BF16),
                pltpu.VMEM((z.all_each, z.width), BF16),
                pltpu.SemaphoreType.DMA((z.local,)),
            ],
            h, back, *units, down_proj,
        )
        returned = exchanged(outgoing)
        own = (section_id == tick).astype(jnp.int32).reshape(1)
        return call(
            combine_kernel, z, 6,
            [shape((z.rows, z.width), BF16)],
            [SMEM] + [VMEM] * (3 + z.pieces),
            [pltpu.VMEM((z.all_pay, z.width), BF16)],
            own, weight, rows, kept, *returned,
        )[0]

    rows = tokens.reshape(z.rows, z.width)
    kept = rows
    for tick in range(sections):
        if tick:
            rows = lax.ppermute(kept, "section", [(tick - 1, tick)])
        kept = layer(rows, kept, tick)
    return kept.reshape(1, z.micro, z.tok, z.width)


def solution(mesh):
    placed = (
        P(None, "expert", "hidden"),
        P("section", "hidden", None, "expert"),
        P("section", "expert", "hidden"),
        P("section", None, "expert", None),
        P("section", None, "expert", None),
    )
    return jax.shard_map(
        on_device,
        mesh=mesh,
        in_specs=placed,
        out_specs=P("section", None, "expert", "hidden"),
        check_vma=False,
    )
```

```python
import functools

import jax
import jax.numpy as jnp
import numpy as np
from jax import lax
from jax.experimental import pallas as pl
from jax.experimental.pallas import tpu as pltpu
from jax.sharding import PartitionSpec as P

D = 7168
FFE = 1024
CAP = 3
EPS = 1e-06
TILE = 16
SMEM = pl.BlockSpec(memory_space=pltpu.SMEM)
VMEM = pl.BlockSpec(memory_space=pltpu.VMEM)
HBM = pl.BlockSpec(memory_space=pl.ANY)
BF16 = jnp.bfloat16
F32 = jnp.float32


def padded(count, unit=TILE):
    return -(-count // unit) * unit


def dot(a, b):
    return jnp.dot(a, b, preferred_element_type=F32)


def swap(value, axis, step):
    count = lax.axis_size(axis)
    return lax.ppermute(value, axis, [(i, i ^ step) for i in range(count)])


class Sizes:
    def __init__(self, tokens, gate_up, micro, peers, splits):
        self.peers, self.splits = peers, splits
        self.micro, self.tok, self.width = micro, tokens.shape[1], tokens.shape[2]
        self.rows = self.micro * self.tok
        units_dev = gate_up.shape[3]
        self.units_dev = units_dev
        self.units = min(FFE, units_dev)
        self.local = units_dev // self.units
        self.share = self.units // splits
        self.slots = self.micro * CAP
        self.pay = padded(self.local * self.slots, 8)
        self.all_pay = peers * self.pay
        self.pieces = peers if peers <= 8 else 1
        self.piece = self.all_pay // self.pieces
        self.each = padded(peers * self.slots, 8)
        self.all_each = self.local * self.each
        self.lanes = 2 * self.share
        self.square_rows = padded(2 * -(-self.all_each // self.lanes))

    def slot_table(self):
        row = np.arange(self.all_pay)
        step, place = row // self.pay, row % self.pay
        expert, batch, rank = place // self.slots, place // CAP % self.micro, place % CAP
        rank = np.where(place < self.local * self.slots, rank, -1)
        return np.stack([step, expert, batch, rank], axis=1).astype(np.int32)

    def reorder(self):
        matrix = np.zeros((self.all_each, self.all_pay), np.float32)
        for expert in range(self.local):
            for step in range(self.peers):
                for slot in range(self.slots):
                    matrix[
                        expert * self.each + step * self.slots + slot,
                        step * self.pay + expert * self.slots + slot,
                    ] = 1.0
        return matrix


def pack_kernel(z, table_ref, routes_ref, gates_ref, rows_ref, *outs):
    table = table_ref[...]
    owner = table[:, 0:1] ^ lax.axis_index("expert") if z.pieces > 1 else table[:, 0:1]
    if z.units_dev >= FFE:
        expert = owner * z.local + table[:, 1:2]
    else:
        expert = lax.shift_right_logical(owner, (FFE // z.units_dev).bit_length() - 1)
    batch, rank = table[:, 2:3], table[:, 3:4]
    shape = (z.all_pay, z.rows)
    token = lax.broadcasted_iota(jnp.int32, shape, 1)
    start = batch * z.tok
    same = (token >= start) & (token < start + z.tok)
    first = (routes_ref[0:1, :] == expert) & same
    second = (routes_ref[1:2, :] == expert) & same
    chosen = jnp.where(first | second, F32(1.0), F32(0.0))
    square = (z.rows, z.rows)
    before = lax.broadcasted_iota(jnp.int32, square, 0) < lax.broadcasted_iota(jnp.int32, square, 1)
    before = jnp.where(before, F32(1.0), F32(0.0)).astype(BF16)
    count = dot(chosen.astype(BF16), before)
    hits = jnp.where(count == rank.astype(F32), chosen, F32(0.0))
    weight = jnp.where(first, gates_ref[0:1, :], F32(0.0)) + jnp.where(second, gates_ref[1:2, :], F32(0.0))
    outs[z.pieces][...] = (hits * weight).astype(BF16)
    hits = hits.astype(BF16)
    rows = rows_ref[...]
    value = dot(hits, rows)
    for step in range(z.pieces):
        outs[step][...] = value[step * z.piece:(step + 1) * z.piece].astype(BF16)


def load_kernel(z, parts, after, gate_up, down_proj, *refs):
    wide, tall = refs[:z.local], refs[z.local:2 * z.local]
    wide_sems, tall_sems = refs[2 * z.local:]
    flat = gate_up.reshape(2 * z.width, z.units_dev)
    depth = 2 * z.width // parts
    copies = []
    for expert in range(z.local):
        for part in range(parts):
            copies.append(
                pltpu.make_async_copy(
                    flat.at[pl.ds(part * depth, depth), pl.ds(expert * z.units, z.units)],
                    wide[expert].at[pl.ds(part * depth, depth)],
                    wide_sems.at[expert * parts + part],
                )
            )
    for expert in range(z.local):
        copies.append(
            pltpu.make_async_copy(
                down_proj.at[0, pl.ds(expert * z.units, z.units), :], tall[expert], tall_sems.at[expert]
            )
        )
    for copy in copies:
        copy.start()
    for copy in copies:
        copy.wait()


def up_kernel(z, order_ref, *refs):
    weights, refs = refs[:z.local], refs[z.local:]
    received, refs = refs[:z.pieces], refs[z.pieces:]
    outs, (spread, staged) = refs[:z.splits], refs[z.splits:]
    stacked = jnp.concatenate([piece[...].astype(F32) for piece in received], axis=0).astype(BF16)
    rows = dot(order_ref[...], stacked)
    squares = rows * rows
    high = squares.astype(BF16)
    low = (squares - high.astype(F32)).astype(BF16)
    ones = jnp.ones((TILE, z.width), BF16)
    across = (((1,), (1,)), ((), ()))
    sums = lax.dot_general(ones, high, across, preferred_element_type=F32) + lax.dot_general(
        ones, low, across, preferred_element_type=F32
    )
    rows = rows.astype(BF16)
    block = 128
    shape = (block, 2 * block)
    target = lax.broadcasted_iota(jnp.int32, shape, 1) - 2 * lax.broadcasted_iota(jnp.int32, shape, 0)
    placing = [jnp.where(target == side, F32(1.0), F32(0.0)).astype(BF16) for side in range(2)]
    for piece in range(z.width // block):
        columns = slice(piece * block, (piece + 1) * block)
        gate, up = dot(rows[:, columns], placing[0]), dot(rows[:, columns], placing[1])
        for expert in range(z.local):
            here = slice(expert * z.each, (expert + 1) * z.each)
            both = jnp.concatenate([gate[here], up[here]], axis=0).astype(BF16)
            spread[expert, :, 2 * piece * block:2 * (piece + 1) * block] = both
    sum_high = sums.astype(BF16).astype(F32)
    sum_low = sums - sum_high
    row_id = lax.broadcasted_iota(jnp.int32, (z.square_rows, z.lanes), 0)
    extra = jnp.zeros((z.square_rows, z.lanes), F32)
    for piece in range(-(-z.all_each // z.lanes)):
        begin = piece * z.lanes
        end = min(z.all_each, begin + z.lanes)
        both = []
        for value in (sum_high, sum_low):
            value = value[0:1, begin:end]
            if end - begin < z.lanes:
                value = jnp.concatenate([value, jnp.zeros((1, z.lanes - end + begin), F32)], axis=1)
            both.append(value)
        extra = jnp.where(row_id == 2 * piece, both[0], jnp.where(row_id == 2 * piece + 1, both[1], extra))
    totals = [dot(spread[expert], weights[expert][...]) for expert in range(z.local)]
    for piece in range(z.splits):
        columns = slice(piece * z.share, (piece + 1) * z.share)
        gate = jnp.concatenate([total[:z.each, columns] for total in totals], axis=0)
        up = jnp.concatenate([total[z.each:, columns] for total in totals], axis=0)
        staged[piece, :z.all_each, :] = jnp.concatenate([gate, up], axis=1).astype(BF16)
        staged[piece, z.all_each:, :] = extra.astype(BF16)
    for step in range(z.splits):
        outs[step][...] = staged[lax.axis_index("hidden") ^ step]


def act_kernel(z, *refs):
    out = refs[z.splits]
    total = refs[0][...].astype(F32)
    for step in range(1, z.splits):
        total = total + refs[step][...].astype(F32)
    extra = total[z.all_each:, :]
    for piece in range(-(-z.all_each // z.lanes)):
        begin = piece * z.lanes
        end = min(z.all_each, begin + z.lanes)
        shape = (end - begin, end - begin)
        line = (extra[2 * piece:2 * piece + 1, :] + extra[2 * piece + 1:2 * piece + 2, :])[:, :end - begin]
        diagonal = lax.broadcasted_iota(jnp.int32, shape, 0) == lax.broadcasted_iota(jnp.int32, shape, 1)
        sums = jnp.sum(jnp.where(diagonal, line, F32(0.0)), axis=1, keepdims=True)
        scale = lax.rsqrt(sums / D + EPS)
        gate = scale * total[begin:end, :z.share]
        up = scale * total[begin:end, z.share:]
        out[begin:end, :] = (gate / (F32(1.0) + jnp.exp(-gate)) * up).astype(BF16)


def down_kernel(z, order_ref, *refs):
    weights, refs = refs[:z.local], refs[z.local:]
    units, outs = refs[:z.splits], refs[z.splits:]
    units = [unit[...].astype(F32) for unit in units]
    results = []
    for expert in range(z.local):
        here = slice(expert * z.each, (expert + 1) * z.each)
        total = None
        for step in range(z.splits):
            low = pl.multiple_of((lax.axis_index("hidden") ^ step) * z.share, z.share)
            value = dot(units[step][here].astype(BF16), weights[expert][pl.ds(low, z.share), :])
            total = value if total is None else total + value
        results.append(total)
    result = jnp.concatenate(results, axis=0).astype(BF16)
    value = dot(order_ref[...], result)
    for step in range(z.pieces):
        outs[step][...] = value[step * z.piece:(step + 1) * z.piece].astype(BF16)


def combine_kernel(z, tick, weight_ref, rows_ref, kept_ref, *refs):
    returned, out = refs[:z.pieces], refs[z.pieces]
    stacked = jnp.concatenate([piece[...].astype(F32) for piece in returned], axis=0).astype(BF16)
    mixed = lax.dot_general(
        weight_ref[...], stacked, (((0,), (0,)), ((), ())), preferred_element_type=F32
    )
    value = (rows_ref[...].astype(F32) + mixed).astype(BF16)
    out[...] = jnp.where(lax.axis_index("section") == tick, value, kept_ref[...])


def call(kernel, sizes, megabytes, cost, outs, in_specs, scratch, *args):
    flops, moved = cost
    results = pl.pallas_call(
        functools.partial(kernel, *sizes),
        out_shape=outs,
        in_specs=in_specs,
        out_specs=[VMEM] * len(outs),
        scratch_shapes=scratch,
        compiler_params=pltpu.CompilerParams(vmem_limit_bytes=megabytes * 2**20),
        cost_estimate=pl.CostEstimate(flops=flops, bytes_accessed=moved, transcendentals=0),
    )(*args)
    return list(results)


def on_device(tokens, gate_up, down_proj, routes, gate_weights):
    sections = lax.axis_size("section")
    micro = tokens.shape[0]
    streams = 2 if micro % 2 == 0 else 1
    z = Sizes(tokens, gate_up, micro // streams, lax.axis_size("expert"), lax.axis_size("hidden"))
    table = jnp.asarray(z.slot_table())
    order = z.reorder()
    back = jnp.asarray(np.ascontiguousarray(order.T).astype(BF16))
    order = jnp.asarray(order.astype(BF16))
    routes = routes[0].transpose(2, 0, 1).reshape(2, streams, z.rows)
    gates = gate_weights[0].astype(F32).transpose(2, 0, 1).reshape(2, streams, z.rows)
    parts = 2 if z.width % 256 == 0 else 1
    shape = jax.ShapeDtypeStruct
    pay = shape((z.piece, z.width), BF16)
    partial = shape((z.all_each + z.square_rows, z.lanes), BF16)
    weight_bytes = 6 * z.width * z.units_dev

    def exchanged(pieces):
        if z.pieces == 1:
            return [lax.all_to_all(pieces[0], "expert", split_axis=0, concat_axis=0, tiled=True)]
        return pieces[:1] + [swap(pieces[step], "expert", step) for step in range(1, z.pieces)]

    def packs(rows):
        return [
            call(
                pack_kernel, (z,), 2, (0, 2**21),
                [pay] * z.pieces + [shape((z.all_pay, z.rows), BF16)],
                [VMEM] * 4, [],
                table, routes[:, stream], gates[:, stream], rows[stream],
            )
            for stream in range(streams)
        ]

    def layer(packed, rows, kept, tick):
        *sent, weight = packed
        received = exchanged(sent)
        sums = call(
            up_kernel, (z,), 6, (0, 2**24),
            [partial] * z.splits,
            [VMEM] * (1 + z.local + z.pieces),
            [
                pltpu.VMEM((z.local, 2 * z.each, 2 * z.width), BF16),
                pltpu.VMEM((z.splits,) + partial.shape, BF16),
            ],
            order, *held[:z.local], *received,
        )
        sums = sums[:1] + [swap(sums[step], "hidden", step) for step in range(1, z.splits)]
        units = call(
            act_kernel, (z,), 2, (0, 2**20),
            [shape((z.all_each, z.share), BF16)], [VMEM] * z.splits, [], *sums
        )[0]
        units = [units] + [swap(units, "hidden", step) for step in range(1, z.splits)]
        outgoing = call(
            down_kernel, (z,), 4, (0, 2**23),
            [pay] * z.pieces,
            [VMEM] * (1 + z.local + z.splits), [],
            back, *held[z.local:], *units,
        )
        returned = exchanged(outgoing)
        return call(
            combine_kernel, (z, tick), 2, (0, 2**20),
            [shape((z.rows, z.width), BF16)],
            [VMEM] * (3 + z.pieces), [],
            weight, rows, kept, *returned,
        )[0]

    rows = list(tokens.reshape(streams, z.rows, z.width))
    kept = rows
    packed = packs(rows)
    held = call(
        load_kernel, (z, parts), 1, (0, 2 * weight_bytes),
        [pltpu.VMEM((2 * z.width, z.units), BF16)] * z.local
        + [pltpu.VMEM((z.units, z.width), BF16)] * z.local,
        [HBM] * 3,
        [pltpu.SemaphoreType.DMA((z.local * parts,)), pltpu.SemaphoreType.DMA((z.local,))],
        packed[-1][-1], gate_up, down_proj,
    )
    for tick in range(sections):
        if tick:
            rows = [lax.ppermute(value, "section", [(tick - 1, tick)]) for value in kept]
            packed = packs(rows)
        kept = [layer(packed[stream], rows[stream], kept[stream], tick) for stream in range(streams)]
    return jnp.stack(kept).reshape(1, micro, z.tok, z.width)


def solution(mesh):
    placed = (
        P(None, "expert", "hidden"),
        P("section", "hidden", None, "expert"),
        P("section", "expert", "hidden"),
        P("section", None, "expert", None),
        P("section", None, "expert", None),
    )
    return jax.shard_map(
        on_device,
        mesh=mesh,
        in_specs=placed,
        out_specs=P("section", None, "expert", "hidden"),
        check_vma=False,
    )
```

```python
import functools

import jax
import jax.numpy as jnp
from jax import lax
from jax.experimental import pallas as pl
from jax.experimental.pallas import tpu as pltpu
from jax.sharding import PartitionSpec as P

D = 7168
FFE = 1024
CAP = 3
EPS = 1e-06
EXTRA = 16
VMEM = pl.BlockSpec(memory_space=pltpu.VMEM)
HBM = pl.BlockSpec(memory_space=pltpu.HBM)
BF16 = jnp.bfloat16
F32 = jnp.float32
I32 = jnp.int32
ACROSS = (((1,), (1,)), ((), ()))
DOWN = (((0,), (0,)), ((), ()))


def padded(count, unit):
    return -(-count // unit) * unit


def dot(a, b, dims=(((1,), (0,)), ((), ()))):
    return lax.dot_general(a, b, dims, preferred_element_type=F32)


def one_hot(mask):
    return jnp.where(mask, F32(1.0), F32(0.0))


def divided(value, divisor):
    if divisor == 1:
        return value, jnp.zeros_like(value)
    quotient = lax.shift_right_logical(value * (2**20 // divisor + 1), 20)
    return quotient, value - quotient * divisor


class Sizes:
    def __init__(self, tokens, gate_up, peers, splits):
        self.peers, self.splits = peers, splits
        self.micro, self.tok, self.width = tokens.shape
        self.rows = self.micro * self.tok
        self.units_dev = gate_up.shape[3]
        self.units = min(FFE, self.units_dev)
        self.half = self.units // 2
        self.local = self.units_dev // self.units
        self.groups = 2 if self.local % 2 == 0 else 1
        self.members = self.local // self.groups
        self.slots = self.micro * CAP
        self.pay = padded(self.members * self.slots, 8)
        self.pieces = peers if peers <= 8 else 1
        self.group_pay = peers * self.pay
        self.piece = self.group_pay // self.pieces
        self.all_pay = self.groups * self.group_pay
        self.each = padded(peers * self.slots, 8)
        self.group_each = self.members * self.each
        self.partial = (self.group_each + EXTRA, 2 * self.half)

    def order(self):
        shape = (self.group_each, self.group_pay)
        row = lax.broadcasted_iota(I32, (self.group_each, 1), 0)
        expert, rest = divided(row, self.each)
        step, slot = divided(rest, self.slots)
        target = jnp.where(step < self.peers, step * self.pay + expert * self.slots + slot, -1)
        return one_hot(lax.broadcasted_iota(I32, shape, 1) == target).astype(BF16)


def line_up(z, ref):
    total = None
    for batch in range(z.micro):
        shape = (z.tok, z.rows)
        place = lax.broadcasted_iota(I32, shape, 1) == lax.broadcasted_iota(I32, shape, 0) + batch * z.tok
        value = dot(ref[batch].astype(F32).astype(BF16), one_hot(place).astype(BF16))
        total = value if total is None else total + value
    return total


def slot_hits(z, routes_ref):
    row = lax.broadcasted_iota(I32, (z.all_pay, 1), 0)
    group, rest = divided(row, z.group_pay)
    step, place = divided(rest, z.pay)
    member, inside = divided(place, z.slots)
    batch, rank = divided(inside, CAP)
    rank = jnp.where(member < z.members, rank, -1)
    owner = step ^ lax.axis_index("expert") if z.pieces > 1 else step
    if z.units_dev >= FFE:
        expert = owner * z.local + group * z.members + member
    else:
        expert = lax.shift_right_logical(owner, (FFE // z.units_dev).bit_length() - 1)
    routes = line_up(z, routes_ref)
    token = lax.broadcasted_iota(I32, (z.all_pay, z.rows), 1)
    start = batch * z.tok
    same = (token >= start) & (token < start + z.tok)
    expert = expert.astype(F32)
    first = (routes[0:1, :] == expert) & same
    second = (routes[1:2, :] == expert) & same
    chosen = one_hot(first | second)
    shape = (z.rows, z.rows)
    before = lax.broadcasted_iota(I32, shape, 0) < lax.broadcasted_iota(I32, shape, 1)
    count = dot(chosen.astype(BF16), one_hot(before).astype(BF16))
    hits = jnp.where(count == rank.astype(F32), chosen, F32(0.0))
    return hits, first, second


def send_rows(z, hits, rows, outs):
    value = dot(hits.astype(BF16), rows)
    for index, out in enumerate(outs):
        out[...] = value[index * z.piece:(index + 1) * z.piece].astype(BF16)


def pack_kernel(z, routes_ref, gates_ref, rows_ref, *outs):
    hits, first, second = slot_hits(z, routes_ref)
    gates = line_up(z, gates_ref)
    weight = jnp.where(first, gates[0:1, :], F32(0.0)) + jnp.where(second, gates[1:2, :], F32(0.0))
    outs[-1][...] = (hits * weight).astype(BF16)
    send_rows(z, hits, rows_ref[...], outs[:-1])


def load_kernel(z, parts, experts, after, gate_up, *refs):
    outs, sems = refs[:-1], refs[-1]
    flat = gate_up.reshape(2 * z.width, z.units_dev)
    depth = 2 * z.width // parts
    copies = []
    for index, expert in enumerate(experts):
        for part in range(parts):
            copies.append(
                pltpu.make_async_copy(
                    flat.at[pl.ds(part * depth, depth), pl.ds(expert * z.units, z.units)],
                    outs[index].at[pl.ds(part * depth, depth)],
                    sems.at[index * parts + part],
                )
            )
    for copy in copies:
        copy.start()
    for copy in copies:
        copy.wait()


def load_down_kernel(z, experts, after, down_proj, *refs):
    outs, sems = refs[:-1], refs[-1]
    copies = [
        pltpu.make_async_copy(
            down_proj.at[0, pl.ds(expert * z.units, z.units), :], outs[index], sems.at[index]
        )
        for index, expert in enumerate(experts)
    ]
    for copy in copies:
        copy.start()
    for copy in copies:
        copy.wait()


def split_sums(sums, lanes):
    high = sums.astype(BF16).astype(F32)
    row = lax.broadcasted_iota(I32, sums.shape, 0)
    both = jnp.where(row == 0, high, jnp.where(row == 1, sums - high, F32(0.0)))
    if both.shape[1] < lanes:
        both = jnp.concatenate([both, jnp.zeros((EXTRA, lanes - both.shape[1]), F32)], axis=1)
    return both


def up_kernel(z, *refs):
    weights, refs = refs[:z.members], refs[z.members:]
    received, refs = refs[:z.pieces], refs[z.pieces:]
    own, sent, spread, staged = refs
    stacked = jnp.concatenate([piece[...].astype(F32) for piece in received], axis=0).astype(BF16)
    rows = dot(z.order(), stacked)
    squares = rows * rows
    high = squares.astype(BF16)
    low = (squares - high.astype(F32)).astype(BF16)
    ones = jnp.ones((EXTRA, z.width), BF16)
    sums = dot(ones, high, ACROSS) + dot(ones, low, ACROSS)
    rows = rows.astype(BF16)
    block = 128
    shape = (block, 2 * block)
    target = lax.broadcasted_iota(I32, shape, 1) - 2 * lax.broadcasted_iota(I32, shape, 0)
    placing = [one_hot(target == side).astype(BF16) for side in range(2)]
    for piece in range(z.width // block):
        columns = slice(piece * block, (piece + 1) * block)
        gate, up = dot(rows[:, columns], placing[0]), dot(rows[:, columns], placing[1])
        for expert in range(z.members):
            here = slice(expert * z.each, (expert + 1) * z.each)
            both = jnp.concatenate([gate[here], up[here]], axis=0).astype(BF16)
            spread[expert, :, 2 * piece * block:2 * (piece + 1) * block] = both
    totals = [dot(spread[expert], weights[expert][...]) for expert in range(z.members)]
    extra = split_sums(sums, 2 * z.half)
    for side in range(2):
        columns = slice(side * z.half, (side + 1) * z.half)
        gate = jnp.concatenate([total[:z.each, columns] for total in totals], axis=0)
        up = jnp.concatenate([total[z.each:, columns] for total in totals], axis=0)
        staged[side, :z.group_each, :] = jnp.concatenate([gate, up], axis=1)
        staged[side, z.group_each:, :] = extra
    core = lax.axis_index("hidden") & 1
    own[...] = staged[core]
    sent[...] = staged[1 - core].astype(BF16)


def joined(z, refs):
    total = refs[0][...].astype(F32)
    for ref in refs[1:]:
        total = total + ref[...].astype(F32)
    products, extra = total[:z.group_each], total[z.group_each:]
    row = lax.broadcasted_iota(I32, extra.shape, 0)
    sums = jnp.sum(jnp.where(row < 2, extra, F32(0.0)), axis=0, keepdims=True)
    return products, sums


def pair_kernel(z, own, other, out):
    products, sums = joined(z, (own, other))
    out[:z.group_each, :] = products.astype(BF16)
    sums = jnp.broadcast_to(sums, (EXTRA, 2 * z.half))
    out[z.group_each:, :] = split_sums(sums, 2 * z.half).astype(BF16)


def act_kernel(z, *refs):
    out = refs[-1]
    products, sums = joined(z, refs[:-1])
    shape = (z.group_each, z.group_each)
    diagonal = lax.broadcasted_iota(I32, shape, 0) == lax.broadcasted_iota(I32, shape, 1)
    sums = jnp.sum(jnp.where(diagonal, sums[:, :z.group_each], F32(0.0)), axis=1, keepdims=True)
    scale = lax.rsqrt(sums / D + EPS)
    gate = scale * products[:, :z.half]
    up = scale * products[:, z.half:]
    out[...] = (gate / (F32(1.0) + jnp.exp(-gate)) * up).astype(BF16)


def down_kernel(z, *refs):
    weights, refs = refs[:z.members], refs[z.members:]
    halves, outs = refs[:2], refs[2:]
    core = lax.axis_index("hidden") & 1
    results = []
    for expert in range(z.members):
        total = None
        for step in range(2):
            units = halves[step][...].astype(F32)[expert * z.each:(expert + 1) * z.each].astype(BF16)
            low = pl.multiple_of((core ^ step) * z.half, z.half)
            value = dot(units, weights[expert][pl.ds(low, z.half), :])
            total = value if total is None else total + value
        results.append(total)
    value = dot(z.order(), jnp.concatenate(results, axis=0).astype(BF16), DOWN)
    for index, out in enumerate(outs):
        out[...] = value[index * z.piece:(index + 1) * z.piece].astype(BF16)


def combine_kernel(z, tick, last, weight_ref, rows_ref, kept_ref, *refs):
    count = z.groups * z.pieces
    returned, refs = refs[:count], refs[count:]
    stacked = jnp.concatenate([piece[...].astype(F32) for piece in returned], axis=0).astype(BF16)
    mixed = dot(weight_ref[...], stacked, DOWN)
    value = (rows_ref[...].astype(F32) + mixed).astype(BF16)
    if last:
        refs[0][...] = jnp.where(lax.axis_index("section") == tick, value, kept_ref[...])
        return
    routes_ref, out, outs = refs[0], refs[1], refs[2:]
    out[...] = jnp.where(lax.axis_index("section") == tick, value, kept_ref[...])
    hits, _, _ = slot_hits(z, routes_ref)
    send_rows(z, hits, value, outs)


def call(kernel, sizes, megabytes, cost, outs, in_specs, scratch, *args):
    flops, moved = cost
    results = pl.pallas_call(
        functools.partial(kernel, *sizes),
        out_shape=outs,
        in_specs=in_specs,
        out_specs=[VMEM] * len(outs),
        scratch_shapes=scratch,
        compiler_params=pltpu.CompilerParams(vmem_limit_bytes=megabytes * 2**20),
        cost_estimate=pl.CostEstimate(flops=flops, bytes_accessed=moved, transcendentals=0),
    )(*args)
    return list(results)


def on_device(tokens, gate_up, down_proj, routes, gate_weights):
    sections = lax.axis_size("section")
    z = Sizes(tokens, gate_up, lax.axis_size("expert"), lax.axis_size("hidden"))
    parts = 2 if z.width % 256 == 0 else 1
    shape = jax.ShapeDtypeStruct
    pay = shape((z.piece, z.width), BF16)
    whole = shape((z.rows, z.width), BF16)
    steps = sorted(range(z.peers), key=lambda step: -step.bit_length())
    second = 10**6

    def swap(value, step):
        pairs = [(i, i ^ step) for i in range(z.splits)]
        return lax.ppermute(value, "hidden", pairs)

    def exchanged(pieces):
        if z.pieces == 1:
            return [lax.all_to_all(pieces[0], "expert", split_axis=0, concat_axis=0, tiled=True)]
        result = list(pieces)
        for step in steps[:-1]:
            pairs = [(i, i ^ step) for i in range(z.peers)]
            result[step] = lax.ppermute(pieces[step], "expert", pairs)
        return result

    def relayed(pieces, tick):
        if z.pieces == 1:
            return [lax.ppermute(exchanged(pieces)[0], "section", [(tick, tick + 1)])]
        result = list(pieces)
        for step in steps:
            pairs = [(tick * z.peers + i, (tick + 1) * z.peers + (i ^ step)) for i in range(z.peers)]
            result[step] = lax.ppermute(pieces[step], ("section", "expert"), pairs)
        return result

    def grouped(pieces):
        return [pieces[group * z.pieces:(group + 1) * z.pieces] for group in range(z.groups)]

    def middle(received, wide):
        own, sent = call(
            up_kernel, (z,), 6, (0, 3 * second * 3),
            [shape(z.partial, F32), shape(z.partial, BF16)],
            [VMEM] * (z.members + z.pieces),
            [
                pltpu.VMEM((z.members, 2 * z.each, 2 * z.width), BF16),
                pltpu.VMEM((2,) + z.partial, F32),
            ],
            *wide, *received,
        )
        pair = call(
            pair_kernel, (z,), 2, (0, second), [shape(z.partial, BF16)], [VMEM] * 2, [],
            own, swap(sent, 1),
        )[0]
        pairs = [pair] + [swap(pair, step) for step in range(2, z.splits, 2)]
        units = call(
            act_kernel, (z,), 2, (0, second),
            [shape((z.group_each, z.half), BF16)], [VMEM] * len(pairs), [], *pairs,
        )[0]
        return units, swap(units, 1)

    def after(halves, tall):
        return call(
            down_kernel, (z,), 4, (0, 3 * second * 2), [pay] * z.pieces, [VMEM] * (z.members + 2), [],
            *tall, *halves,
        )

    routes = routes[0].transpose(0, 2, 1)
    gates = gate_weights[0].transpose(0, 2, 1)
    rows = tokens.reshape(z.rows, z.width)
    kept = rows
    *sent, weight = call(
        pack_kernel, (z,), 3, (0, second),
        [pay] * (z.groups * z.pieces) + [shape((z.all_pay, z.rows), BF16)],
        [VMEM] * 3, [], routes, gates, rows,
    )
    received = [exchanged(pieces) for pieces in grouped(sent)]
    following = lax.ppermute(routes, "section", [(i + 1, i) for i in range(sections - 1)])
    gate_up = pltpu.with_memory_space_constraint(gate_up, pltpu.HBM)
    down_proj = pltpu.with_memory_space_constraint(down_proj, pltpu.HBM)
    wide, tall = [], []
    for group in range(z.groups):
        experts = range(group * z.members, (group + 1) * z.members)
        wide.append(call(
            load_kernel, (z, parts, experts), 1, (0, 5 * second * 3),
            [pltpu.VMEM((2 * z.width, z.units), BF16)] * z.members, [VMEM, HBM],
            [pltpu.SemaphoreType.DMA((z.members * parts,))],
            weight, gate_up,
        ))
    for group in range(z.groups):
        experts = range(group * z.members, (group + 1) * z.members)
        tall.append(call(
            load_down_kernel, (z, experts), 1, (0, 2 * second * 3),
            [pltpu.VMEM((z.units, z.width), BF16)] * z.members, [VMEM, HBM],
            [pltpu.SemaphoreType.DMA((z.members,))],
            weight, down_proj,
        ))
    for tick in range(sections):
        halves = [middle(received[group], wide[group]) for group in range(z.groups)]
        returned = []
        for group in range(z.groups):
            returned += exchanged(after(halves[group], tall[group]))
        last = tick == sections - 1
        kept, *sent = call(
            combine_kernel, (z, tick, last), 4, (0, second),
            [whole] if last else [whole] + [pay] * (z.groups * z.pieces),
            [VMEM] * (3 + len(returned) + (not last)), [],
            weight, rows, kept, *returned, *([] if last else [following]),
        )
        if not last:
            received = [relayed(pieces, tick) for pieces in grouped(sent)]
            rows = lax.ppermute(kept, "section", [(tick, tick + 1)])
    return kept.reshape(1, z.micro, z.tok, z.width)


def solution(mesh):
    placed = (
        P(None, "expert", "hidden"),
        P("section", "hidden", None, "expert"),
        P("section", "expert", "hidden"),
        P("section", None, "expert", None),
        P("section", None, "expert", None),
    )
    return jax.shard_map(
        on_device,
        mesh=mesh,
        in_specs=placed,
        out_specs=P("section", None, "expert", "hidden"),
        check_vma=False,
    )
```

```python
import functools

import jax
import jax.numpy as jnp
from jax import lax
from jax.experimental import pallas as pl
from jax.experimental.pallas import tpu as pltpu
from jax.sharding import PartitionSpec as P

D = 7168
FFE = 1024
CAP = 3
EPS = 1e-06
EXTRA = 16
VMEM = pl.BlockSpec(memory_space=pltpu.VMEM)
HBM = pl.BlockSpec(memory_space=pltpu.HBM)
BF16 = jnp.bfloat16
F32 = jnp.float32
I32 = jnp.int32
ACROSS = (((1,), (1,)), ((), ()))
DOWN = (((0,), (0,)), ((), ()))


def padded(count, unit):
    return -(-count // unit) * unit


def dot(a, b, dims=(((1,), (0,)), ((), ()))):
    return lax.dot_general(a, b, dims, preferred_element_type=F32)


def one_hot(mask):
    return jnp.where(mask, F32(1.0), F32(0.0))


def divided(value, divisor):
    if divisor == 1:
        return value, jnp.zeros_like(value)
    quotient = lax.shift_right_logical(value * (2**20 // divisor + 1), 20)
    return quotient, value - quotient * divisor


class Sizes:
    def __init__(self, tokens, gate_up, peers, splits):
        self.peers, self.splits = peers, splits
        self.micro, self.tok, self.width = tokens.shape
        self.rows = self.micro * self.tok
        self.units_dev = gate_up.shape[3]
        self.units = min(FFE, self.units_dev)
        self.half = self.units // 2
        self.local = self.units_dev // self.units
        self.groups = 2 if self.local % 2 == 0 else 1
        self.members = self.local // self.groups
        self.slots = self.micro * CAP
        self.pay = padded(self.members * self.slots, 8)
        self.pieces = peers if peers <= 8 else 1
        self.group_pay = peers * self.pay
        self.piece = self.group_pay // self.pieces
        self.all_pay = self.groups * self.group_pay
        self.all_piece = self.groups * self.piece
        self.each = padded(peers * self.slots, 8)
        self.group_each = self.members * self.each
        self.partial = (self.group_each + EXTRA, 2 * self.half)

    def order(self):
        shape = (self.group_each, self.group_pay)
        row = lax.broadcasted_iota(I32, (self.group_each, 1), 0)
        expert, rest = divided(row, self.each)
        step, slot = divided(rest, self.slots)
        target = jnp.where(step < self.peers, step * self.pay + expert * self.slots + slot, -1)
        return one_hot(lax.broadcasted_iota(I32, shape, 1) == target).astype(BF16)


def line_up(z, ref):
    total = None
    for batch in range(z.micro):
        shape = (z.tok, z.rows)
        place = lax.broadcasted_iota(I32, shape, 1) == lax.broadcasted_iota(I32, shape, 0) + batch * z.tok
        value = dot(ref[batch].astype(F32).astype(BF16), one_hot(place).astype(BF16))
        total = value if total is None else total + value
    return total


def slot_hits(z, routes_ref):
    row = lax.broadcasted_iota(I32, (z.all_pay, 1), 0)
    step, rest = divided(row, z.groups * z.pay)
    group, place = divided(rest, z.pay)
    member, inside = divided(place, z.slots)
    batch, rank = divided(inside, CAP)
    rank = jnp.where(member < z.members, rank, -1)
    owner = step ^ lax.axis_index("expert") if z.pieces > 1 else step
    if z.units_dev >= FFE:
        expert = owner * z.local + group * z.members + member
    else:
        expert = lax.shift_right_logical(owner, (FFE // z.units_dev).bit_length() - 1)
    routes = line_up(z, routes_ref)
    token = lax.broadcasted_iota(I32, (z.all_pay, z.rows), 1)
    start = batch * z.tok
    same = (token >= start) & (token < start + z.tok)
    expert = expert.astype(F32)
    first = (routes[0:1, :] == expert) & same
    second = (routes[1:2, :] == expert) & same
    chosen = one_hot(first | second)
    shape = (z.rows, z.rows)
    before = lax.broadcasted_iota(I32, shape, 0) < lax.broadcasted_iota(I32, shape, 1)
    count = dot(chosen.astype(BF16), one_hot(before).astype(BF16))
    hits = jnp.where(count == rank.astype(F32), chosen, F32(0.0))
    return hits, first, second


def send_rows(z, hits, rows, outs):
    value = dot(hits.astype(BF16), rows)
    for index, out in enumerate(outs):
        out[...] = value[index * z.all_piece:(index + 1) * z.all_piece].astype(BF16)


def group_rows(z, group, pieces):
    result = []
    for piece in pieces:
        value = piece[...].astype(F32)
        for step in range(z.peers // z.pieces):
            low = (step * z.groups + group) * z.pay
            result.append(value[low:low + z.pay])
    return jnp.concatenate(result, axis=0)


def pack_kernel(z, *refs):
    sources, outs = refs[:3], refs[3:-4]
    routes_ref, gates_ref, rows_ref, sems = refs[-4:]
    copies = [
        pltpu.make_async_copy(source, target, sems.at[index])
        for index, (source, target) in enumerate(zip(sources, refs[-4:-1]))
    ]
    for copy in copies:
        copy.start()
    for copy in copies:
        copy.wait()
    hits, first, second = slot_hits(z, routes_ref)
    gates = line_up(z, gates_ref)
    weight = jnp.where(first, gates[0:1, :], F32(0.0)) + jnp.where(second, gates[1:2, :], F32(0.0))
    outs[-1][...] = (hits * weight).astype(BF16)
    send_rows(z, hits, rows_ref[...], outs[:-1])


def load_kernel(z, parts, after, gate_up, *refs):
    outs, sems = refs[:-1], refs[-1]
    flat = gate_up.reshape(2 * z.width, z.units_dev)
    depth = 2 * z.width // parts
    copies = []
    for expert in range(z.local):
        for part in range(parts):
            copies.append(
                pltpu.make_async_copy(
                    flat.at[pl.ds(part * depth, depth), pl.ds(expert * z.units, z.units)],
                    outs[expert].at[pl.ds(part * depth, depth)],
                    sems.at[expert * parts + part],
                )
            )
    for copy in copies:
        copy.start()
    for copy in copies:
        copy.wait()


def load_down_kernel(z, group, after, routes_ref, down_proj, *refs):
    outs, routes_out, sems = refs[:z.members], refs[z.members], refs[-1]
    copies = []
    for index in range(z.members):
        low = (group * z.members + index) * z.units
        copies.append(
            pltpu.make_async_copy(down_proj.at[0, pl.ds(low, z.units), :], outs[index], sems.at[index])
        )
    for copy in copies:
        copy.start()
    routes_out[...] = routes_ref[...]
    for copy in copies:
        copy.wait()


def split_sums(sums, lanes):
    high = sums.astype(BF16).astype(F32)
    row = lax.broadcasted_iota(I32, sums.shape, 0)
    both = jnp.where(row == 0, high, jnp.where(row == 1, sums - high, F32(0.0)))
    if both.shape[1] < lanes:
        both = jnp.concatenate([both, jnp.zeros((EXTRA, lanes - both.shape[1]), F32)], axis=1)
    return both


def up_kernel(z, group, *refs):
    weights, refs = refs[:z.members], refs[z.members:]
    received, refs = refs[:z.pieces], refs[z.pieces:]
    own, sent, spread, staged = refs
    rows = dot(z.order(), group_rows(z, group, received).astype(BF16))
    squares = rows * rows
    high = squares.astype(BF16)
    low = (squares - high.astype(F32)).astype(BF16)
    ones = jnp.ones((EXTRA, z.width), BF16)
    sums = dot(ones, high, ACROSS) + dot(ones, low, ACROSS)
    rows = rows.astype(BF16)
    block = 128
    shape = (block, 2 * block)
    target = lax.broadcasted_iota(I32, shape, 1) - 2 * lax.broadcasted_iota(I32, shape, 0)
    placing = [one_hot(target == side).astype(BF16) for side in range(2)]
    for piece in range(z.width // block):
        columns = slice(piece * block, (piece + 1) * block)
        gate, up = dot(rows[:, columns], placing[0]), dot(rows[:, columns], placing[1])
        for expert in range(z.members):
            here = slice(expert * z.each, (expert + 1) * z.each)
            both = jnp.concatenate([gate[here], up[here]], axis=0).astype(BF16)
            spread[expert, :, 2 * piece * block:2 * (piece + 1) * block] = both
    totals = [dot(spread[expert], weights[expert][...]) for expert in range(z.members)]
    extra = split_sums(sums, 2 * z.half)
    for side in range(2):
        columns = slice(side * z.half, (side + 1) * z.half)
        gate = jnp.concatenate([total[:z.each, columns] for total in totals], axis=0)
        up = jnp.concatenate([total[z.each:, columns] for total in totals], axis=0)
        staged[side, :z.group_each, :] = jnp.concatenate([gate, up], axis=1)
        staged[side, z.group_each:, :] = extra
    core = lax.axis_index("hidden") & 1
    own[...] = staged[core]
    sent[...] = staged[1 - core].astype(BF16)


def joined(z, refs):
    total = refs[0][...].astype(F32)
    for ref in refs[1:]:
        total = total + ref[...].astype(F32)
    products, extra = total[:z.group_each], total[z.group_each:]
    row = lax.broadcasted_iota(I32, extra.shape, 0)
    sums = jnp.sum(jnp.where(row < 2, extra, F32(0.0)), axis=0, keepdims=True)
    return products, sums


def pair_kernel(z, own, other, out):
    products, sums = joined(z, (own, other))
    out[:z.group_each, :] = products.astype(BF16)
    sums = jnp.broadcast_to(sums, (EXTRA, 2 * z.half))
    out[z.group_each:, :] = split_sums(sums, 2 * z.half).astype(BF16)


def act_kernel(z, count, *refs):
    out = refs[-1]
    products, sums = joined(z, refs[:count])
    shape = (z.group_each, z.group_each)
    diagonal = lax.broadcasted_iota(I32, shape, 0) == lax.broadcasted_iota(I32, shape, 1)
    sums = jnp.sum(jnp.where(diagonal, sums[:, :z.group_each], F32(0.0)), axis=1, keepdims=True)
    scale = lax.rsqrt(sums / D + EPS)
    gate = scale * products[:, :z.half]
    up = scale * products[:, z.half:]
    out[...] = (gate / (F32(1.0) + jnp.exp(-gate)) * up).astype(BF16)


def down_kernel(z, *refs):
    weights, refs = refs[:z.members], refs[z.members:]
    halves, outs = refs[:2], refs[2:]
    core = lax.axis_index("hidden") & 1
    results = []
    for expert in range(z.members):
        total = None
        for step in range(2):
            units = halves[step][...].astype(F32)[expert * z.each:(expert + 1) * z.each].astype(BF16)
            low = pl.multiple_of((core ^ step) * z.half, z.half)
            value = dot(units, weights[expert][pl.ds(low, z.half), :])
            total = value if total is None else total + value
        results.append(total)
    value = dot(z.order(), jnp.concatenate(results, axis=0).astype(BF16), DOWN)
    for index, out in enumerate(outs):
        out[...] = value[index * z.piece:(index + 1) * z.piece].astype(BF16)


def combine_kernel(z, tick, last, weight_ref, rows_ref, kept_ref, *refs):
    count = z.groups * z.pieces
    returned, refs = refs[:count], refs[count:]
    stacked = []
    for piece in range(z.pieces):
        values = [returned[group * z.pieces + piece][...].astype(F32) for group in range(z.groups)]
        for step in range(z.peers // z.pieces):
            stacked += [value[step * z.pay:(step + 1) * z.pay] for value in values]
    stacked = jnp.concatenate(stacked, axis=0).astype(BF16)
    mixed = dot(weight_ref[...], stacked, DOWN)
    value = (rows_ref[...].astype(F32) + mixed).astype(BF16)
    if last:
        refs[0][...] = jnp.where(lax.axis_index("section") == tick, value, kept_ref[...])
        return
    routes_ref, out, outs = refs[0], refs[1], refs[2:]
    out[...] = jnp.where(lax.axis_index("section") == tick, value, kept_ref[...])
    hits, _, _ = slot_hits(z, routes_ref)
    send_rows(z, hits, value, outs)


def call(kernel, sizes, megabytes, cost, outs, in_specs, scratch, *args):
    flops, moved = cost
    results = pl.pallas_call(
        functools.partial(kernel, *sizes),
        out_shape=outs,
        in_specs=in_specs,
        out_specs=[VMEM] * len(outs),
        scratch_shapes=scratch,
        compiler_params=pltpu.CompilerParams(vmem_limit_bytes=megabytes * 2**20),
        cost_estimate=pl.CostEstimate(flops=flops, bytes_accessed=moved, transcendentals=0),
    )(*args)
    return list(results)


def on_device(tokens, gate_up, down_proj, routes, gate_weights):
    sections = lax.axis_size("section")
    z = Sizes(tokens, gate_up, lax.axis_size("expert"), lax.axis_size("hidden"))
    parts = 2 if z.width % 256 == 0 else 1
    shape = jax.ShapeDtypeStruct
    pay = shape((z.piece, z.width), BF16)
    all_pay = shape((z.all_piece, z.width), BF16)
    whole = shape((z.rows, z.width), BF16)
    steps = sorted(range(z.peers), key=lambda step: -step.bit_length())
    second = 10**6

    def swap(value, step):
        pairs = [(i, i ^ step) for i in range(z.splits)]
        return lax.ppermute(value, "hidden", pairs)

    def exchanged(pieces):
        if z.pieces == 1:
            return [lax.all_to_all(pieces[0], "expert", split_axis=0, concat_axis=0, tiled=True)]
        result = list(pieces)
        for step in steps[:-1]:
            pairs = [(i, i ^ step) for i in range(z.peers)]
            result[step] = lax.ppermute(pieces[step], "expert", pairs)
        return result

    def relayed(pieces, tick):
        if z.pieces == 1:
            return [lax.ppermute(exchanged(pieces)[0], "section", [(tick, tick + 1)])]
        result = list(pieces)
        for step in steps:
            pairs = [(tick * z.peers + i, (tick + 1) * z.peers + (i ^ step)) for i in range(z.peers)]
            result[step] = lax.ppermute(pieces[step], ("section", "expert"), pairs)
        return result

    def load_down(group, after):
        *tall, handed = call(
            load_down_kernel, (z, group), 1, (0, 2 * second * 3),
            [pltpu.VMEM((z.units, z.width), BF16)] * z.members + [shape(routes.shape, routes.dtype)],
            [VMEM, VMEM, HBM], [pltpu.SemaphoreType.DMA((z.members,))],
            after, routes, down_proj,
        )
        return tall, handed

    def middle(received, group, tick):
        own, sent = call(
            up_kernel, (z, group), 6, (0, 3 * second * 3),
            [shape(z.partial, F32), shape(z.partial, BF16)],
            [VMEM] * (z.members + z.pieces),
            [
                pltpu.VMEM((z.members, 2 * z.each, 2 * z.width), BF16),
                pltpu.VMEM((2,) + z.partial, F32),
            ],
            *wide[group * z.members:(group + 1) * z.members], *received,
        )
        pair = call(
            pair_kernel, (z,), 2, (0, second), [shape(z.partial, BF16)], [VMEM] * 2, [],
            own, swap(sent, 1),
        )[0]
        pairs = [pair] + [swap(pair, step) for step in range(2, z.splits, 2)]
        if tick == 0:
            tall[group], handed = load_down(group, pair)
            if group == 0:
                pairs_back = [(i + 1, i) for i in range(sections - 1)]
                following.append(lax.ppermute(handed, "section", pairs_back))
        waits = tall[group][:1] + following[:group] if tick == 0 else []
        units = call(
            act_kernel, (z, len(pairs)), 2, (0, second),
            [shape((z.group_each, z.half), BF16)], [VMEM] * (len(pairs) + len(waits)), [],
            *pairs, *waits,
        )[0]
        return units, swap(units, 1)

    def after(halves, tall):
        return call(
            down_kernel, (z,), 4, (0, 3 * second * 2), [pay] * z.pieces, [VMEM] * (z.members + 2), [],
            *tall, *halves,
        )

    routes = routes[0].transpose(0, 2, 1)
    gates = gate_weights[0].transpose(0, 2, 1)
    rows = tokens.reshape(z.rows, z.width)
    kept = rows
    *sent, weight = call(
        pack_kernel, (z,), 3, (0, second),
        [all_pay] * z.pieces + [shape((z.all_pay, z.rows), BF16)],
        [HBM] * 3,
        [
            pltpu.VMEM(routes.shape, routes.dtype),
            pltpu.VMEM(gates.shape, gates.dtype),
            pltpu.VMEM(rows.shape, rows.dtype),
            pltpu.SemaphoreType.DMA((3,)),
        ],
        *(pltpu.with_memory_space_constraint(value, pltpu.HBM) for value in (routes, gates, rows)),
    )
    received = exchanged(sent)
    gate_up = pltpu.with_memory_space_constraint(gate_up, pltpu.HBM)
    down_proj = pltpu.with_memory_space_constraint(down_proj, pltpu.HBM)
    wide = call(
        load_kernel, (z, parts), 1, (0, 10 * second * 3),
        [pltpu.VMEM((2 * z.width, z.units), BF16)] * z.local, [VMEM, HBM],
        [pltpu.SemaphoreType.DMA((z.local * parts,))],
        weight, gate_up,
    )
    tall, following = {}, []
    for tick in range(sections):
        halves = [middle(received, group, tick) for group in range(z.groups)]
        returned = []
        for group in range(z.groups):
            returned += exchanged(after(halves[group], tall[group]))
        last = tick == sections - 1
        kept, *sent = call(
            combine_kernel, (z, tick, last), 4, (0, second),
            [whole] if last else [whole] + [all_pay] * z.pieces,
            [VMEM] * (3 + len(returned) + (not last)), [],
            weight, rows, kept, *returned, *([] if last else following),
        )
        if not last:
            received = relayed(sent, tick)
            rows = lax.ppermute(kept, "section", [(tick, tick + 1)])
    return kept.reshape(1, z.micro, z.tok, z.width)


def solution(mesh):
    placed = (
        P(None, "expert", "hidden"),
        P("section", "hidden", None, "expert"),
        P("section", "expert", "hidden"),
        P("section", None, "expert", None),
        P("section", None, "expert", None),
    )
    return jax.shard_map(
        on_device,
        mesh=mesh,
        in_specs=placed,
        out_specs=P("section", None, "expert", "hidden"),
        check_vma=False,
    )
```

```python
import functools

import jax
import jax.numpy as jnp
from jax import lax
from jax.experimental import pallas as pl
from jax.experimental.pallas import tpu as pltpu
from jax.sharding import PartitionSpec as P

D = 7168
FFE = 1024
CAP = 3
EPS = 1e-06
EXTRA = 16
VMEM = pl.BlockSpec(memory_space=pltpu.VMEM)
HBM = pl.BlockSpec(memory_space=pltpu.HBM)
BF16 = jnp.bfloat16
F32 = jnp.float32
I32 = jnp.int32
ACROSS = (((1,), (1,)), ((), ()))
DOWN = (((0,), (0,)), ((), ()))


def padded(count, unit):
    return -(-count // unit) * unit


def dot(a, b, dims=(((1,), (0,)), ((), ()))):
    return lax.dot_general(a, b, dims, preferred_element_type=F32)


def one_hot(mask):
    return jnp.where(mask, F32(1.0), F32(0.0))


def divided(value, divisor):
    if divisor == 1:
        return value, jnp.zeros_like(value)
    quotient = lax.shift_right_logical(value * (2**20 // divisor + 1), 20)
    return quotient, value - quotient * divisor


class Sizes:
    def __init__(self, tokens, gate_up, peers, splits):
        self.peers, self.splits = peers, splits
        self.micro, self.tok, self.width = tokens.shape
        self.rows = self.micro * self.tok
        self.units_dev = gate_up.shape[3]
        self.units = min(FFE, self.units_dev)
        self.half = self.units // 2
        self.local = self.units_dev // self.units
        self.groups = 2 if self.local % 2 == 0 else 1
        self.members = self.local // self.groups
        self.slots = self.micro * CAP
        self.pay = padded(self.members * self.slots, 8)
        self.pieces = peers if peers <= 8 else 1
        self.group_pay = peers * self.pay
        self.piece = self.group_pay // self.pieces
        self.all_pay = self.groups * self.group_pay
        self.all_piece = self.groups * self.piece
        self.each = padded(peers * self.slots, 8)
        self.group_each = self.members * self.each
        self.partial = (self.group_each + EXTRA, 2 * self.half)

    def order(self):
        shape = (self.group_each, self.group_pay)
        row = lax.broadcasted_iota(I32, (self.group_each, 1), 0)
        expert, rest = divided(row, self.each)
        step, slot = divided(rest, self.slots)
        target = jnp.where(step < self.peers, step * self.pay + expert * self.slots + slot, -1)
        return one_hot(lax.broadcasted_iota(I32, shape, 1) == target).astype(BF16)


def line_up(z, ref):
    total = None
    for batch in range(z.micro):
        shape = (z.tok, z.rows)
        place = lax.broadcasted_iota(I32, shape, 1) == lax.broadcasted_iota(I32, shape, 0) + batch * z.tok
        value = dot(ref[batch].astype(F32).astype(BF16), one_hot(place).astype(BF16))
        total = value if total is None else total + value
    return total


def slot_hits(z, routes_ref):
    row = lax.broadcasted_iota(I32, (z.all_pay, 1), 0)
    step, rest = divided(row, z.groups * z.pay)
    group, place = divided(rest, z.pay)
    member, inside = divided(place, z.slots)
    batch, rank = divided(inside, CAP)
    rank = jnp.where(member < z.members, rank, -1)
    owner = step ^ lax.axis_index("expert") if z.pieces > 1 else step
    if z.units_dev >= FFE:
        expert = owner * z.local + group * z.members + member
    else:
        expert = lax.shift_right_logical(owner, (FFE // z.units_dev).bit_length() - 1)
    routes = line_up(z, routes_ref)
    token = lax.broadcasted_iota(I32, (z.all_pay, z.rows), 1)
    start = batch * z.tok
    same = (token >= start) & (token < start + z.tok)
    expert = expert.astype(F32)
    first = (routes[0:1, :] == expert) & same
    second = (routes[1:2, :] == expert) & same
    chosen = one_hot(first | second)
    shape = (z.rows, z.rows)
    before = lax.broadcasted_iota(I32, shape, 0) < lax.broadcasted_iota(I32, shape, 1)
    count = dot(chosen.astype(BF16), one_hot(before).astype(BF16))
    hits = jnp.where(count == rank.astype(F32), chosen, F32(0.0))
    return hits, first, second


def send_rows(z, hits, rows, outs):
    value = dot(hits.astype(BF16), rows)
    for index, out in enumerate(outs):
        out[...] = value[index * z.all_piece:(index + 1) * z.all_piece].astype(BF16)


def group_rows(z, group, pieces):
    result = []
    for piece in pieces:
        value = piece[...].astype(F32)
        for step in range(z.peers // z.pieces):
            low = (step * z.groups + group) * z.pay
            result.append(value[low:low + z.pay])
    return jnp.concatenate(result, axis=0)


def pack_kernel(z, *refs):
    sources, outs = refs[:3], refs[3:-4]
    routes_ref, gates_ref, rows_ref, sems = refs[-4:]
    copies = [
        pltpu.make_async_copy(source, target, sems.at[index])
        for index, (source, target) in enumerate(zip(sources, refs[-4:-1]))
    ]
    for copy in copies:
        copy.start()
    for copy in copies:
        copy.wait()
    hits, first, second = slot_hits(z, routes_ref)
    gates = line_up(z, gates_ref)
    weight = jnp.where(first, gates[0:1, :], F32(0.0)) + jnp.where(second, gates[1:2, :], F32(0.0))
    outs[-1][...] = (hits * weight).astype(BF16)
    send_rows(z, hits, rows_ref[...], outs[:-1])


def load_kernel(z, parts, gate_up, *refs):
    outs, sems = refs[:-1], refs[-1]
    flat = gate_up.reshape(2 * z.width, z.units_dev)
    depth = 2 * z.width // parts
    copies = []
    for expert in range(z.local):
        for part in range(parts):
            copies.append(
                pltpu.make_async_copy(
                    flat.at[pl.ds(part * depth, depth), pl.ds(expert * z.units, z.units)],
                    outs[expert].at[pl.ds(part * depth, depth)],
                    sems.at[expert * parts + part],
                )
            )
    for copy in copies:
        copy.start()
    for copy in copies:
        copy.wait()


def load_down_kernel(z, group, down_proj, *refs):
    outs, sems = refs[:z.members], refs[-1]
    copies = []
    for index in range(z.members):
        low = (group * z.members + index) * z.units
        copies.append(
            pltpu.make_async_copy(down_proj.at[0, pl.ds(low, z.units), :], outs[index], sems.at[index])
        )
    for copy in copies:
        copy.start()
    for copy in copies:
        copy.wait()


def split_sums(sums, lanes):
    high = sums.astype(BF16).astype(F32)
    row = lax.broadcasted_iota(I32, sums.shape, 0)
    both = jnp.where(row == 0, high, jnp.where(row == 1, sums - high, F32(0.0)))
    if both.shape[1] < lanes:
        both = jnp.concatenate([both, jnp.zeros((EXTRA, lanes - both.shape[1]), F32)], axis=1)
    return both


def up_kernel(z, group, *refs):
    weights, refs = refs[:z.members], refs[z.members:]
    received, refs = refs[:z.pieces], refs[z.pieces:]
    own, sent, spread, staged = refs
    rows = dot(z.order(), group_rows(z, group, received).astype(BF16))
    squares = rows * rows
    high = squares.astype(BF16)
    low = (squares - high.astype(F32)).astype(BF16)
    ones = jnp.ones((EXTRA, z.width), BF16)
    sums = dot(ones, high, ACROSS) + dot(ones, low, ACROSS)
    rows = rows.astype(BF16)
    block = 128
    shape = (block, 2 * block)
    target = lax.broadcasted_iota(I32, shape, 1) - 2 * lax.broadcasted_iota(I32, shape, 0)
    placing = [one_hot(target == side).astype(BF16) for side in range(2)]
    for piece in range(z.width // block):
        columns = slice(piece * block, (piece + 1) * block)
        gate, up = dot(rows[:, columns], placing[0]), dot(rows[:, columns], placing[1])
        for expert in range(z.members):
            here = slice(expert * z.each, (expert + 1) * z.each)
            both = jnp.concatenate([gate[here], up[here]], axis=0).astype(BF16)
            spread[expert, :, 2 * piece * block:2 * (piece + 1) * block] = both
    totals = [dot(spread[expert], weights[expert][...]) for expert in range(z.members)]
    extra = split_sums(sums, 2 * z.half)
    for side in range(2):
        columns = slice(side * z.half, (side + 1) * z.half)
        gate = jnp.concatenate([total[:z.each, columns] for total in totals], axis=0)
        up = jnp.concatenate([total[z.each:, columns] for total in totals], axis=0)
        staged[side, :z.group_each, :] = jnp.concatenate([gate, up], axis=1)
        staged[side, z.group_each:, :] = extra
    core = lax.axis_index("hidden") & 1
    own[...] = staged[core]
    sent[...] = staged[1 - core].astype(BF16)


def joined(z, refs):
    total = refs[0][...].astype(F32)
    for ref in refs[1:]:
        total = total + ref[...].astype(F32)
    products, extra = total[:z.group_each], total[z.group_each:]
    row = lax.broadcasted_iota(I32, extra.shape, 0)
    sums = jnp.sum(jnp.where(row < 2, extra, F32(0.0)), axis=0, keepdims=True)
    return products, sums


def pair_kernel(z, own, other, out):
    products, sums = joined(z, (own, other))
    out[:z.group_each, :] = products.astype(BF16)
    sums = jnp.broadcast_to(sums, (EXTRA, 2 * z.half))
    out[z.group_each:, :] = split_sums(sums, 2 * z.half).astype(BF16)


def act_kernel(z, *refs):
    out = refs[-1]
    products, sums = joined(z, refs[:-1])
    shape = (z.group_each, z.group_each)
    diagonal = lax.broadcasted_iota(I32, shape, 0) == lax.broadcasted_iota(I32, shape, 1)
    sums = jnp.sum(jnp.where(diagonal, sums[:, :z.group_each], F32(0.0)), axis=1, keepdims=True)
    scale = lax.rsqrt(sums / D + EPS)
    gate = scale * products[:, :z.half]
    up = scale * products[:, z.half:]
    out[...] = (gate / (F32(1.0) + jnp.exp(-gate)) * up).astype(BF16)


def down_kernel(z, *refs):
    weights, refs = refs[:z.members], refs[z.members:]
    halves, outs = refs[:2], refs[2:]
    if len(outs) > z.pieces:
        outs[-1][...] = outs[0][...]
        outs = outs[1:-1]
    core = lax.axis_index("hidden") & 1
    results = []
    for expert in range(z.members):
        total = None
        for step in range(2):
            units = halves[step][...].astype(F32)[expert * z.each:(expert + 1) * z.each].astype(BF16)
            low = pl.multiple_of((core ^ step) * z.half, z.half)
            value = dot(units, weights[expert][pl.ds(low, z.half), :])
            total = value if total is None else total + value
        results.append(total)
    value = dot(z.order(), jnp.concatenate(results, axis=0).astype(BF16), DOWN)
    for index, out in enumerate(outs):
        out[...] = value[index * z.piece:(index + 1) * z.piece].astype(BF16)


def combine_kernel(z, tick, last, weight_ref, rows_ref, kept_ref, *refs):
    count = z.groups * z.pieces
    returned, refs = refs[:count], refs[count:]
    stacked = []
    for piece in range(z.pieces):
        values = [returned[group * z.pieces + piece][...].astype(F32) for group in range(z.groups)]
        for step in range(z.peers // z.pieces):
            stacked += [value[step * z.pay:(step + 1) * z.pay] for value in values]
    stacked = jnp.concatenate(stacked, axis=0).astype(BF16)
    mixed = dot(weight_ref[...], stacked, DOWN)
    value = (rows_ref[...].astype(F32) + mixed).astype(BF16)
    if last:
        refs[0][...] = jnp.where(lax.axis_index("section") == tick, value, kept_ref[...])
        return
    routes_ref, out, outs = refs[0], refs[1], refs[2:]
    out[...] = jnp.where(lax.axis_index("section") == tick, value, kept_ref[...])
    hits, _, _ = slot_hits(z, routes_ref)
    send_rows(z, hits, value, outs)


def after_waits(waits, kernel, *refs):
    return kernel(*refs[waits:])


def call(kernel, sizes, megabytes, outs, in_specs, scratch, *args, waits=()):
    results = pl.pallas_call(
        functools.partial(after_waits, len(waits), functools.partial(kernel, *sizes)),
        out_shape=outs,
        in_specs=[VMEM] * len(waits) + in_specs,
        out_specs=[VMEM] * len(outs),
        scratch_shapes=scratch,
        compiler_params=pltpu.CompilerParams(vmem_limit_bytes=megabytes * 2**20),
    )(*waits, *args)
    return list(results)


def on_device(tokens, gate_up, down_proj, routes, gate_weights):
    sections = lax.axis_size("section")
    z = Sizes(tokens, gate_up, lax.axis_size("expert"), lax.axis_size("hidden"))
    parts = 2 if z.width % 256 == 0 else 1
    shape = jax.ShapeDtypeStruct
    pay = shape((z.piece, z.width), BF16)
    all_pay = shape((z.all_piece, z.width), BF16)
    whole = shape((z.rows, z.width), BF16)
    steps = sorted(range(z.peers), key=lambda step: -step.bit_length())

    def swap(value, step):
        pairs = [(i, i ^ step) for i in range(z.splits)]
        return lax.ppermute(value, "hidden", pairs)

    def exchanged(pieces):
        if z.pieces == 1:
            return [lax.all_to_all(pieces[0], "expert", split_axis=0, concat_axis=0, tiled=True)]
        result = list(pieces)
        for step in steps[:-1]:
            pairs = [(i, i ^ step) for i in range(z.peers)]
            result[step] = lax.ppermute(pieces[step], "expert", pairs)
        return result

    def relayed(pieces, tick):
        if z.pieces == 1:
            return [lax.ppermute(exchanged(pieces)[0], "section", [(tick, tick + 1)])]
        result = list(pieces)
        for step in steps:
            pairs = [(tick * z.peers + i, (tick + 1) * z.peers + (i ^ step)) for i in range(z.peers)]
            result[step] = lax.ppermute(pieces[step], ("section", "expert"), pairs)
        return result

    def load_down(group, after):
        return call(
            load_down_kernel, (z, group), 1,
            [pltpu.VMEM((z.units, z.width), BF16)] * z.members,
            [HBM], [pltpu.SemaphoreType.DMA((z.members,))], down_proj, waits=[after],
        )

    def products(received, group):
        own, sent = call(
            up_kernel, (z, group), 6,
            [shape(z.partial, F32), shape(z.partial, BF16)],
            [VMEM] * (z.members + z.pieces),
            [
                pltpu.VMEM((z.members, 2 * z.each, 2 * z.width), BF16),
                pltpu.VMEM((2,) + z.partial, F32),
            ],
            *wide[group * z.members:(group + 1) * z.members], *received,
            waits=tall[0][:1] if group == 0 else [],
        )
        return own, swap(sent, 1)

    def pair_sums(own, other, waits):
        pair = call(
            pair_kernel, (z,), 2, [shape(z.partial, BF16)], [VMEM] * 2, [], own, other, waits=waits
        )[0]
        return [pair] + [swap(pair, step) for step in range(2, z.splits, 2)]

    def activated(pairs, waits):
        units = call(
            act_kernel, (z,), 2,
            [shape((z.group_each, z.half), BF16)], [VMEM] * len(pairs), [], *pairs, waits=waits,
        )[0]
        return units, swap(units, 1)

    def down(halves, group, hand_on):
        return call(
            down_kernel, (z,), 4,
            [pay] * z.pieces + [shape(value.shape, value.dtype) for value in hand_on],
            [VMEM] * (z.members + 2 + len(hand_on)), [],
            *tall[group], *halves, *hand_on,
        )

    routes = routes[0].transpose(0, 2, 1)
    gates = gate_weights[0].transpose(0, 2, 1)
    rows = tokens.reshape(z.rows, z.width)
    kept = rows
    *sent, weight = call(
        pack_kernel, (z,), 3,
        [all_pay] * z.pieces + [shape((z.all_pay, z.rows), BF16)],
        [HBM] * 3,
        [
            pltpu.VMEM(routes.shape, routes.dtype),
            pltpu.VMEM(gates.shape, gates.dtype),
            pltpu.VMEM(rows.shape, rows.dtype),
            pltpu.SemaphoreType.DMA((3,)),
        ],
        *(pltpu.with_memory_space_constraint(value, pltpu.HBM) for value in (routes, gates, rows)),
    )
    received = exchanged(sent)
    gate_up = pltpu.with_memory_space_constraint(gate_up, pltpu.HBM)
    down_proj = pltpu.with_memory_space_constraint(down_proj, pltpu.HBM)
    wide = call(
        load_kernel, (z, parts), 1,
        [pltpu.VMEM((2 * z.width, z.units), BF16)] * z.local,
        [HBM], [pltpu.SemaphoreType.DMA((z.local * parts,))], gate_up, waits=[weight],
    )
    tall = [load_down(0, wide[-1])]
    groups = range(z.groups)
    for tick in range(sections):
        last = tick == sections - 1
        partials = [products(received, group) for group in groups]
        sums = []
        for group in groups:
            if tick == 0 and group > 0:
                tall.append(load_down(group, sums[-1][0]))
            waits = tall[group][:1] if tick == 0 and group > 0 else []
            sums.append(pair_sums(*partials[group], waits))
        returned, waits = [], []
        for group in groups:
            halves = activated(sums[group], waits)
            hand_on = [routes] if tick == 0 and group == z.groups - 1 else []
            outgoing = down(halves, group, hand_on)
            waits = outgoing[:1]
            if hand_on:
                pairs = [(i + 1, i) for i in range(sections - 1)]
                following = lax.ppermute(outgoing.pop(), "section", pairs)
            returned += exchanged(outgoing)
        kept, *sent = call(
            combine_kernel, (z, tick, last), 4,
            [whole] if last else [whole] + [all_pay] * z.pieces,
            [VMEM] * (3 + len(returned) + (not last)), [],
            weight, rows, kept, *returned, *([] if last else [following]),
        )
        if not last:
            received = relayed(sent, tick)
            rows = lax.ppermute(kept, "section", [(tick, tick + 1)])
    return kept.reshape(1, z.micro, z.tok, z.width)


def solution(mesh):
    placed = (
        P(None, "expert", "hidden"),
        P("section", "hidden", None, "expert"),
        P("section", "expert", "hidden"),
        P("section", None, "expert", None),
        P("section", None, "expert", None),
    )
    return jax.shard_map(
        on_device,
        mesh=mesh,
        in_specs=placed,
        out_specs=P("section", None, "expert", "hidden"),
        check_vma=False,
    )
```

```python
import functools

import jax
import jax.numpy as jnp
from jax import lax
from jax.experimental import pallas as pl
from jax.experimental.pallas import tpu as pltpu
from jax.sharding import PartitionSpec as P

D = 7168
FFE = 1024
CAP = 3
EPS = 1e-06
EXTRA = 16
VMEM = pl.BlockSpec(memory_space=pltpu.VMEM)
HBM = pl.BlockSpec(memory_space=pltpu.HBM)
BF16 = jnp.bfloat16
F32 = jnp.float32
I32 = jnp.int32
ACROSS = (((1,), (1,)), ((), ()))
DOWN = (((0,), (0,)), ((), ()))


def padded(count, unit):
    return -(-count // unit) * unit


def dot(a, b, dims=(((1,), (0,)), ((), ()))):
    return lax.dot_general(a, b, dims, preferred_element_type=F32)


def one_hot(mask):
    return jnp.where(mask, F32(1.0), F32(0.0))


def divided(value, divisor):
    if divisor == 1:
        return value, jnp.zeros_like(value)
    quotient = lax.shift_right_logical(value * (2**20 // divisor + 1), 20)
    return quotient, value - quotient * divisor


class Sizes:
    def __init__(self, tokens, gate_up, peers, splits):
        self.peers, self.splits = peers, splits
        self.micro, self.tok, self.width = tokens.shape
        self.rows = self.micro * self.tok
        self.units_dev = gate_up.shape[3]
        self.units = min(FFE, self.units_dev)
        self.half = self.units // 2
        self.local = self.units_dev // self.units
        self.groups = 2 if self.local % 2 == 0 else 1
        self.members = self.local // self.groups
        self.slots = self.micro * CAP
        self.pay = padded(self.members * self.slots, 8)
        self.pieces = peers if peers <= 8 else 1
        self.near = self.pieces // 2
        self.group_pay = peers * self.pay
        self.piece = self.group_pay // self.pieces
        self.all_pay = self.groups * self.group_pay
        self.all_piece = self.groups * self.piece
        self.each = padded(peers * self.slots, 8)
        self.group_each = self.members * self.each
        self.partial = (self.group_each + EXTRA, 2 * self.half)

    def order(self):
        shape = (self.group_each, self.group_pay)
        row = lax.broadcasted_iota(I32, (self.group_each, 1), 0)
        expert, rest = divided(row, self.each)
        step, slot = divided(rest, self.slots)
        target = jnp.where(step < self.peers, step * self.pay + expert * self.slots + slot, -1)
        return one_hot(lax.broadcasted_iota(I32, shape, 1) == target).astype(BF16)


def line_up(z, ref):
    total = None
    for batch in range(z.micro):
        shape = (z.tok, z.rows)
        place = lax.broadcasted_iota(I32, shape, 1) == lax.broadcasted_iota(I32, shape, 0) + batch * z.tok
        value = dot(ref[batch].astype(F32).astype(BF16), one_hot(place).astype(BF16))
        total = value if total is None else total + value
    return total


def slot_hits(z, routes_ref):
    row = lax.broadcasted_iota(I32, (z.all_pay, 1), 0)
    step, rest = divided(row, z.groups * z.pay)
    group, place = divided(rest, z.pay)
    member, inside = divided(place, z.slots)
    batch, rank = divided(inside, CAP)
    rank = jnp.where(member < z.members, rank, -1)
    owner = step ^ lax.axis_index("expert") if z.pieces > 1 else step
    if z.units_dev >= FFE:
        expert = owner * z.local + group * z.members + member
    else:
        expert = lax.shift_right_logical(owner, (FFE // z.units_dev).bit_length() - 1)
    routes = line_up(z, routes_ref)
    token = lax.broadcasted_iota(I32, (z.all_pay, z.rows), 1)
    start = batch * z.tok
    same = (token >= start) & (token < start + z.tok)
    expert = expert.astype(F32)
    first = (routes[0:1, :] == expert) & same
    second = (routes[1:2, :] == expert) & same
    chosen = one_hot(first | second)
    shape = (z.rows, z.rows)
    before = lax.broadcasted_iota(I32, shape, 0) < lax.broadcasted_iota(I32, shape, 1)
    count = dot(chosen.astype(BF16), one_hot(before).astype(BF16))
    hits = jnp.where(count == rank.astype(F32), chosen, F32(0.0))
    return hits, first, second


def send_rows(z, hits, rows, outs, first):
    low = first * z.all_piece
    value = dot(hits[low:low + len(outs) * z.all_piece].astype(BF16), rows)
    for index, out in enumerate(outs):
        out[...] = value[index * z.all_piece:(index + 1) * z.all_piece].astype(BF16)


def near_kernel(z, routes_ref, rows_ref, *outs):
    hits, _, _ = slot_hits(z, routes_ref)
    send_rows(z, hits, rows_ref[...], outs, 0)


def group_rows(z, group, pieces):
    result = []
    for piece in pieces:
        value = piece[...].astype(F32)
        for step in range(z.peers // z.pieces):
            low = (step * z.groups + group) * z.pay
            result.append(value[low:low + z.pay])
    return jnp.concatenate(result, axis=0)


def pack_kernel(z, *refs):
    sources, outs = refs[:3], refs[3:-4]
    routes_ref, gates_ref, rows_ref, sems = refs[-4:]
    copies = [
        pltpu.make_async_copy(source, target, sems.at[index])
        for index, (source, target) in enumerate(zip(sources, refs[-4:-1]))
    ]
    for copy in copies:
        copy.start()
    for copy in copies:
        copy.wait()
    hits, first, second = slot_hits(z, routes_ref)
    gates = line_up(z, gates_ref)
    weight = jnp.where(first, gates[0:1, :], F32(0.0)) + jnp.where(second, gates[1:2, :], F32(0.0))
    outs[-1][...] = (hits * weight).astype(BF16)
    send_rows(z, hits, rows_ref[...], outs[:-1], 0)


def load_kernel(z, parts, gate_up, *refs):
    outs, sems = refs[:-1], refs[-1]
    flat = gate_up.reshape(2 * z.width, z.units_dev)
    depth = 2 * z.width // parts
    copies = []
    for expert in range(z.local):
        for part in range(parts):
            copies.append(
                pltpu.make_async_copy(
                    flat.at[pl.ds(part * depth, depth), pl.ds(expert * z.units, z.units)],
                    outs[expert].at[pl.ds(part * depth, depth)],
                    sems.at[expert * parts + part],
                )
            )
    for copy in copies:
        copy.start()
    for copy in copies:
        copy.wait()


def load_down_kernel(z, group, down_proj, *refs):
    outs, sems = refs[:z.members], refs[-1]
    copies = []
    for index in range(z.members):
        low = (group * z.members + index) * z.units
        copies.append(
            pltpu.make_async_copy(down_proj.at[0, pl.ds(low, z.units), :], outs[index], sems.at[index])
        )
    for copy in copies:
        copy.start()
    for copy in copies:
        copy.wait()


def split_sums(sums, lanes):
    high = sums.astype(BF16).astype(F32)
    row = lax.broadcasted_iota(I32, sums.shape, 0)
    both = jnp.where(row == 0, high, jnp.where(row == 1, sums - high, F32(0.0)))
    if both.shape[1] < lanes:
        both = jnp.concatenate([both, jnp.zeros((EXTRA, lanes - both.shape[1]), F32)], axis=1)
    return both


def up_kernel(z, group, *refs):
    weights, refs = refs[:z.members], refs[z.members:]
    received, refs = refs[:z.pieces], refs[z.pieces:]
    own, sent, spread, staged = refs
    rows = dot(z.order(), group_rows(z, group, received).astype(BF16))
    squares = rows * rows
    high = squares.astype(BF16)
    low = (squares - high.astype(F32)).astype(BF16)
    ones = jnp.ones((EXTRA, z.width), BF16)
    sums = dot(ones, high, ACROSS) + dot(ones, low, ACROSS)
    rows = rows.astype(BF16)
    block = 128
    shape = (block, 2 * block)
    target = lax.broadcasted_iota(I32, shape, 1) - 2 * lax.broadcasted_iota(I32, shape, 0)
    placing = [one_hot(target == side).astype(BF16) for side in range(2)]
    for piece in range(z.width // block):
        columns = slice(piece * block, (piece + 1) * block)
        gate, up = dot(rows[:, columns], placing[0]), dot(rows[:, columns], placing[1])
        for expert in range(z.members):
            here = slice(expert * z.each, (expert + 1) * z.each)
            both = jnp.concatenate([gate[here], up[here]], axis=0).astype(BF16)
            spread[expert, :, 2 * piece * block:2 * (piece + 1) * block] = both
    totals = [dot(spread[expert], weights[expert][...]) for expert in range(z.members)]
    extra = split_sums(sums, 2 * z.half)
    for side in range(2):
        columns = slice(side * z.half, (side + 1) * z.half)
        gate = jnp.concatenate([total[:z.each, columns] for total in totals], axis=0)
        up = jnp.concatenate([total[z.each:, columns] for total in totals], axis=0)
        staged[side, :z.group_each, :] = jnp.concatenate([gate, up], axis=1)
        staged[side, z.group_each:, :] = extra
    core = lax.axis_index("hidden") & 1
    own[...] = staged[core]
    sent[...] = staged[1 - core].astype(BF16)


def joined(z, refs):
    total = refs[0][...].astype(F32)
    for ref in refs[1:]:
        total = total + ref[...].astype(F32)
    products, extra = total[:z.group_each], total[z.group_each:]
    row = lax.broadcasted_iota(I32, extra.shape, 0)
    sums = jnp.sum(jnp.where(row < 2, extra, F32(0.0)), axis=0, keepdims=True)
    return products, sums


def pair_kernel(z, own, other, out):
    products, sums = joined(z, (own, other))
    out[:z.group_each, :] = products.astype(BF16)
    sums = jnp.broadcast_to(sums, (EXTRA, 2 * z.half))
    out[z.group_each:, :] = split_sums(sums, 2 * z.half).astype(BF16)


def act_kernel(z, *refs):
    out = refs[-1]
    products, sums = joined(z, refs[:-1])
    shape = (z.group_each, z.group_each)
    diagonal = lax.broadcasted_iota(I32, shape, 0) == lax.broadcasted_iota(I32, shape, 1)
    sums = jnp.sum(jnp.where(diagonal, sums[:, :z.group_each], F32(0.0)), axis=1, keepdims=True)
    scale = lax.rsqrt(sums / D + EPS)
    gate = scale * products[:, :z.half]
    up = scale * products[:, z.half:]
    out[...] = (gate / (F32(1.0) + jnp.exp(-gate)) * up).astype(BF16)


def down_kernel(z, *refs):
    weights, refs = refs[:z.members], refs[z.members:]
    halves, outs = refs[:2], refs[2:]
    if len(outs) > z.pieces:
        outs[-1][...] = outs[0][...]
        outs = outs[1:-1]
    core = lax.axis_index("hidden") & 1
    results = []
    for expert in range(z.members):
        total = None
        for step in range(2):
            units = halves[step][...].astype(F32)[expert * z.each:(expert + 1) * z.each].astype(BF16)
            low = pl.multiple_of((core ^ step) * z.half, z.half)
            value = dot(units, weights[expert][pl.ds(low, z.half), :])
            total = value if total is None else total + value
        results.append(total)
    value = dot(z.order(), jnp.concatenate(results, axis=0).astype(BF16), DOWN)
    for index, out in enumerate(outs):
        out[...] = value[index * z.piece:(index + 1) * z.piece].astype(BF16)


def combine_kernel(z, tick, last, weight_ref, rows_ref, kept_ref, *refs):
    count = z.groups * z.pieces
    returned, refs = refs[:count], refs[count:]
    stacked = []
    for piece in range(z.pieces):
        values = [returned[group * z.pieces + piece][...].astype(F32) for group in range(z.groups)]
        for step in range(z.peers // z.pieces):
            stacked += [value[step * z.pay:(step + 1) * z.pay] for value in values]
    stacked = jnp.concatenate(stacked, axis=0).astype(BF16)
    mixed = dot(weight_ref[...], stacked, DOWN)
    value = (rows_ref[...].astype(F32) + mixed).astype(BF16)
    if last:
        refs[0][...] = jnp.where(lax.axis_index("section") == tick, value, kept_ref[...])
        return
    routes_ref, out, outs = refs[0], refs[1], refs[2:]
    out[...] = jnp.where(lax.axis_index("section") == tick, value, kept_ref[...])
    hits, _, _ = slot_hits(z, routes_ref)
    send_rows(z, hits, value, outs, z.near)


def after_waits(waits, kernel, *refs):
    return kernel(*refs[waits:])


def call(kernel, sizes, megabytes, outs, in_specs, scratch, *args, waits=()):
    results = pl.pallas_call(
        functools.partial(after_waits, len(waits), functools.partial(kernel, *sizes)),
        out_shape=outs,
        in_specs=[VMEM] * len(waits) + in_specs,
        out_specs=[VMEM] * len(outs),
        scratch_shapes=scratch,
        compiler_params=pltpu.CompilerParams(vmem_limit_bytes=megabytes * 2**20),
    )(*waits, *args)
    return list(results)


def on_device(tokens, gate_up, down_proj, routes, gate_weights):
    sections = lax.axis_size("section")
    z = Sizes(tokens, gate_up, lax.axis_size("expert"), lax.axis_size("hidden"))
    parts = 2 if z.width % 256 == 0 else 1
    shape = jax.ShapeDtypeStruct
    pay = shape((z.piece, z.width), BF16)
    all_pay = shape((z.all_piece, z.width), BF16)
    whole = shape((z.rows, z.width), BF16)
    steps = sorted(range(z.peers), key=lambda step: -step.bit_length())

    def swap(value, step):
        pairs = [(i, i ^ step) for i in range(z.splits)]
        return lax.ppermute(value, "hidden", pairs)

    def exchanged(pieces):
        if z.pieces == 1:
            return [lax.all_to_all(pieces[0], "expert", split_axis=0, concat_axis=0, tiled=True)]
        result = list(pieces)
        for step in steps[:-1]:
            pairs = [(i, i ^ step) for i in range(z.peers)]
            result[step] = lax.ppermute(pieces[step], "expert", pairs)
        return result

    def relayed(pieces, kept, tick):
        hop = [(tick, tick + 1)]
        rows = lax.ppermute(kept, "section", hop)
        if z.pieces == 1:
            return rows, [lax.ppermute(exchanged(pieces)[0], "section", hop)]
        far = {}
        for step in steps:
            if step >= z.near:
                pairs = [(tick * z.peers + i, (tick + 1) * z.peers + (i ^ step)) for i in range(z.peers)]
                far[step] = lax.ppermute(pieces[step - z.near], ("section", "expert"), pairs)
        result = call(near_kernel, (z,), 4, [all_pay] * z.near, [VMEM] * 2, [], routes, rows)
        for step in range(1, z.near):
            pairs = [(i, i ^ step) for i in range(z.peers)]
            result[step] = lax.ppermute(result[step], "expert", pairs)
        return rows, result + [far[step] for step in range(z.near, z.peers)]

    def load_down(group, after):
        return call(
            load_down_kernel, (z, group), 1,
            [pltpu.VMEM((z.units, z.width), BF16)] * z.members,
            [HBM], [pltpu.SemaphoreType.DMA((z.members,))], down_proj, waits=[after],
        )

    def products(received, group, waits):
        own, sent = call(
            up_kernel, (z, group), 6,
            [shape(z.partial, F32), shape(z.partial, BF16)],
            [VMEM] * (z.members + z.pieces),
            [
                pltpu.VMEM((z.members, 2 * z.each, 2 * z.width), BF16),
                pltpu.VMEM((2,) + z.partial, F32),
            ],
            *wide[group * z.members:(group + 1) * z.members], *received,
            waits=waits if group else tall[0][:1],
        )
        return own, swap(sent, 1)

    def pair_sums(own, other, waits):
        pair = call(
            pair_kernel, (z,), 2, [shape(z.partial, BF16)], [VMEM] * 2, [], own, other, waits=waits
        )[0]
        return [pair] + [swap(pair, step) for step in range(2, z.splits, 2)]

    def activated(pairs, waits):
        units = call(
            act_kernel, (z,), 2,
            [shape((z.group_each, z.half), BF16)], [VMEM] * len(pairs), [], *pairs, waits=waits,
        )[0]
        return units, swap(units, 1)

    def down(halves, group, hand_on):
        return call(
            down_kernel, (z,), 4,
            [pay] * z.pieces + [shape(value.shape, value.dtype) for value in hand_on],
            [VMEM] * (z.members + 2 + len(hand_on)), [],
            *tall[group], *halves, *hand_on,
        )

    routes = routes[0].transpose(0, 2, 1)
    gates = gate_weights[0].transpose(0, 2, 1)
    rows = tokens.reshape(z.rows, z.width)
    kept = rows
    *sent, weight = call(
        pack_kernel, (z,), 3,
        [all_pay] * z.pieces + [shape((z.all_pay, z.rows), BF16)],
        [HBM] * 3,
        [
            pltpu.VMEM(routes.shape, routes.dtype),
            pltpu.VMEM(gates.shape, gates.dtype),
            pltpu.VMEM(rows.shape, rows.dtype),
            pltpu.SemaphoreType.DMA((3,)),
        ],
        *(pltpu.with_memory_space_constraint(value, pltpu.HBM) for value in (routes, gates, rows)),
    )
    received = exchanged(sent)
    gate_up = pltpu.with_memory_space_constraint(gate_up, pltpu.HBM)
    down_proj = pltpu.with_memory_space_constraint(down_proj, pltpu.HBM)
    wide = call(
        load_kernel, (z, parts), 1,
        [pltpu.VMEM((2 * z.width, z.units), BF16)] * z.local,
        [HBM], [pltpu.SemaphoreType.DMA((z.local * parts,))], gate_up, waits=[weight],
    )
    tall = [load_down(0, wide[-1])]
    groups = range(z.groups)
    for tick in range(sections):
        last = tick == sections - 1
        sums, returned = [], []
        early, waits = [], []
        for group in groups:
            own, other = products(received, group, [sums[-1][0]] if group else [])
            sums.append(pair_sums(own, other, waits))
            if tick == 0 and group + 1 < z.groups:
                tall.append(load_down(group + 1, sums[-1][0]))
                early = tall[-1][:1]
            if group == 0:
                halves = activated(sums[0], early)
                waits = list(halves[:1])
        for group in groups:
            if group:
                halves = activated(sums[group], outgoing[:1])
            hand_on = [routes] if tick == 0 and group == z.groups - 1 else []
            outgoing = down(halves, group, hand_on)
            if hand_on:
                pairs = [(i + 1, i) for i in range(sections - 1)]
                following = lax.ppermute(outgoing.pop(), "section", pairs)
            returned += exchanged(outgoing)
        kept, *sent = call(
            combine_kernel, (z, tick, last), 4,
            [whole] if last else [whole] + [all_pay] * (z.pieces - z.near),
            [VMEM] * (3 + len(returned) + (not last)), [],
            weight, rows, kept, *returned, *([] if last else [following]),
        )
        if not last:
            rows, received = relayed(sent, kept, tick)
    return kept.reshape(1, z.micro, z.tok, z.width)


def solution(mesh):
    placed = (
        P(None, "expert", "hidden"),
        P("section", "hidden", None, "expert"),
        P("section", "expert", "hidden"),
        P("section", None, "expert", None),
        P("section", None, "expert", None),
    )
    return jax.shard_map(
        on_device,
        mesh=mesh,
        in_specs=placed,
        out_specs=P("section", None, "expert", "hidden"),
        check_vma=False,
    )
```

```python
import functools

import jax
import jax.numpy as jnp
from jax import lax
from jax.experimental import pallas as pl
from jax.experimental.pallas import tpu as pltpu
from jax.sharding import PartitionSpec as P

D = 7168
FFE = 1024
CAP = 3
EPS = 1e-06
EXTRA = 16
VMEM = pl.BlockSpec(memory_space=pltpu.VMEM)
HBM = pl.BlockSpec(memory_space=pltpu.HBM)
BF16 = jnp.bfloat16
F32 = jnp.float32
I32 = jnp.int32
ACROSS = (((1,), (1,)), ((), ()))
DOWN = (((0,), (0,)), ((), ()))


def padded(count, unit):
    return -(-count // unit) * unit


def dot(a, b, dims=(((1,), (0,)), ((), ()))):
    return lax.dot_general(a, b, dims, preferred_element_type=F32)


def one_hot(mask):
    return jnp.where(mask, F32(1.0), F32(0.0))


def divided(value, divisor):
    if divisor == 1:
        return value, jnp.zeros_like(value)
    quotient = lax.shift_right_logical(value * (2**20 // divisor + 1), 20)
    return quotient, value - quotient * divisor


class Sizes:
    def __init__(self, tokens, gate_up, peers, splits):
        self.peers, self.splits = peers, splits
        self.micro, self.tok, self.width = tokens.shape
        self.rows = self.micro * self.tok
        self.units_dev = gate_up.shape[3]
        self.units = min(FFE, self.units_dev)
        self.half = self.units // 2
        self.local = self.units_dev // self.units
        self.groups = 2 if self.local % 2 == 0 else 1
        self.members = self.local // self.groups
        self.slots = self.micro * CAP
        self.pay = padded(self.members * self.slots, 8)
        self.pieces = peers if peers <= 8 else 1
        self.pairs = self.groups - 1 if self.pieces == 4 else 0
        self.near = self.pieces // 2
        self.group_pay = peers * self.pay
        self.piece = self.group_pay // self.pieces
        self.all_pay = self.groups * self.group_pay
        self.all_piece = self.groups * self.piece
        self.each = padded(peers * self.slots, 8)
        self.group_each = self.members * self.each
        self.partial = (self.group_each + EXTRA, 2 * self.half)

    def order(self):
        shape = (self.group_each, self.group_pay)
        row = lax.broadcasted_iota(I32, (self.group_each, 1), 0)
        expert, rest = divided(row, self.each)
        step, slot = divided(rest, self.slots)
        target = jnp.where(step < self.peers, step * self.pay + expert * self.slots + slot, -1)
        return one_hot(lax.broadcasted_iota(I32, shape, 1) == target).astype(BF16)


def line_up(z, ref):
    total = None
    for batch in range(z.micro):
        shape = (z.tok, z.rows)
        place = lax.broadcasted_iota(I32, shape, 1) == lax.broadcasted_iota(I32, shape, 0) + batch * z.tok
        value = dot(ref[batch].astype(F32).astype(BF16), one_hot(place).astype(BF16))
        total = value if total is None else total + value
    return total


def slot_hits(z, routes_ref):
    row = lax.broadcasted_iota(I32, (z.all_pay, 1), 0)
    step, rest = divided(row, z.groups * z.pay)
    group, place = divided(rest, z.pay)
    member, inside = divided(place, z.slots)
    batch, rank = divided(inside, CAP)
    rank = jnp.where(member < z.members, rank, -1)
    owner = step ^ lax.axis_index("expert") if z.pieces > 1 else step
    if z.units_dev >= FFE:
        expert = owner * z.local + group * z.members + member
    else:
        expert = lax.shift_right_logical(owner, (FFE // z.units_dev).bit_length() - 1)
    routes = line_up(z, routes_ref)
    token = lax.broadcasted_iota(I32, (z.all_pay, z.rows), 1)
    start = batch * z.tok
    same = (token >= start) & (token < start + z.tok)
    expert = expert.astype(F32)
    first = (routes[0:1, :] == expert) & same
    second = (routes[1:2, :] == expert) & same
    chosen = one_hot(first | second)
    shape = (z.rows, z.rows)
    before = lax.broadcasted_iota(I32, shape, 0) < lax.broadcasted_iota(I32, shape, 1)
    count = dot(chosen.astype(BF16), one_hot(before).astype(BF16))
    hits = jnp.where(count == rank.astype(F32), chosen, F32(0.0))
    return hits, first, second


def send_rows(z, hits, rows, outs, first):
    low = first * z.all_piece
    value = dot(hits[low:low + len(outs) * z.all_piece].astype(BF16), rows)
    for index, out in enumerate(outs):
        out[...] = value[index * z.all_piece:(index + 1) * z.all_piece].astype(BF16)


def near_kernel(z, routes_ref, rows_ref, *outs):
    hits, _, _ = slot_hits(z, routes_ref)
    send_rows(z, hits, rows_ref[...], outs, 0)


def group_rows(z, group, pieces):
    result = []
    for piece in pieces:
        value = piece[...].astype(F32)
        for step in range(z.peers // z.pieces):
            low = (step * z.groups + group) * z.pay
            result.append(value[low:low + z.pay])
    return jnp.concatenate(result, axis=0)


def pack_kernel(z, *refs):
    sources, outs = refs[:3], refs[3:-4]
    routes_ref, gates_ref, rows_ref, sems = refs[-4:]
    copies = [
        pltpu.make_async_copy(source, target, sems.at[index])
        for index, (source, target) in enumerate(zip(sources, refs[-4:-1]))
    ]
    for copy in copies:
        copy.start()
    for copy in copies:
        copy.wait()
    hits, first, second = slot_hits(z, routes_ref)
    gates = line_up(z, gates_ref)
    weight = jnp.where(first, gates[0:1, :], F32(0.0)) + jnp.where(second, gates[1:2, :], F32(0.0))
    outs[-1][...] = (hits * weight).astype(BF16)
    send_rows(z, hits, rows_ref[...], outs[:-1], 0)


def load_kernel(z, parts, gate_up, *refs):
    outs, sems = refs[:-1], refs[-1]
    flat = gate_up.reshape(2 * z.width, z.units_dev)
    depth = 2 * z.width // parts
    copies = []
    for expert in range(z.local):
        for part in range(parts):
            copies.append(
                pltpu.make_async_copy(
                    flat.at[pl.ds(part * depth, depth), pl.ds(expert * z.units, z.units)],
                    outs[expert].at[pl.ds(part * depth, depth)],
                    sems.at[expert * parts + part],
                )
            )
    for copy in copies:
        copy.start()
    for copy in copies:
        copy.wait()


def load_down_kernel(z, group, down_proj, *refs):
    outs, sems = refs[:z.members], refs[-1]
    copies = []
    for index in range(z.members):
        low = (group * z.members + index) * z.units
        copies.append(
            pltpu.make_async_copy(down_proj.at[0, pl.ds(low, z.units), :], outs[index], sems.at[index])
        )
    for copy in copies:
        copy.start()
    for copy in copies:
        copy.wait()


def split_sums(sums, lanes):
    high = sums.astype(BF16).astype(F32)
    row = lax.broadcasted_iota(I32, sums.shape, 0)
    both = jnp.where(row == 0, high, jnp.where(row == 1, sums - high, F32(0.0)))
    if both.shape[1] < lanes:
        both = jnp.concatenate([both, jnp.zeros((EXTRA, lanes - both.shape[1]), F32)], axis=1)
    return both


def up_kernel(z, group, *refs):
    weights, refs = refs[:z.members], refs[z.members:]
    received, refs = refs[:z.pieces], refs[z.pieces:]
    own, sent, spread, staged = refs
    rows = dot(z.order(), group_rows(z, group, received).astype(BF16))
    squares = rows * rows
    high = squares.astype(BF16)
    low = (squares - high.astype(F32)).astype(BF16)
    ones = jnp.ones((EXTRA, z.width), BF16)
    sums = dot(ones, high, ACROSS) + dot(ones, low, ACROSS)
    rows = rows.astype(BF16)
    block = 128
    shape = (block, 2 * block)
    target = lax.broadcasted_iota(I32, shape, 1) - 2 * lax.broadcasted_iota(I32, shape, 0)
    placing = [one_hot(target == side).astype(BF16) for side in range(2)]
    for piece in range(z.width // block):
        columns = slice(piece * block, (piece + 1) * block)
        gate, up = dot(rows[:, columns], placing[0]), dot(rows[:, columns], placing[1])
        for expert in range(z.members):
            here = slice(expert * z.each, (expert + 1) * z.each)
            both = jnp.concatenate([gate[here], up[here]], axis=0).astype(BF16)
            spread[expert, :, 2 * piece * block:2 * (piece + 1) * block] = both
    totals = [dot(spread[expert], weights[expert][...]) for expert in range(z.members)]
    extra = split_sums(sums, 2 * z.half)
    for side in range(2):
        columns = slice(side * z.half, (side + 1) * z.half)
        gate = jnp.concatenate([total[:z.each, columns] for total in totals], axis=0)
        up = jnp.concatenate([total[z.each:, columns] for total in totals], axis=0)
        staged[side, :z.group_each, :] = jnp.concatenate([gate, up], axis=1)
        staged[side, z.group_each:, :] = extra
    core = lax.axis_index("hidden") & 1
    own[...] = staged[core]
    sent[...] = staged[1 - core].astype(BF16)


def joined(z, refs):
    total = refs[0][...].astype(F32)
    for ref in refs[1:]:
        total = total + ref[...].astype(F32)
    products, extra = total[:z.group_each], total[z.group_each:]
    row = lax.broadcasted_iota(I32, extra.shape, 0)
    sums = jnp.sum(jnp.where(row < 2, extra, F32(0.0)), axis=0, keepdims=True)
    return products, sums


def pair_kernel(z, own, other, out):
    products, sums = joined(z, (own, other))
    out[:z.group_each, :] = products.astype(BF16)
    sums = jnp.broadcast_to(sums, (EXTRA, 2 * z.half))
    out[z.group_each:, :] = split_sums(sums, 2 * z.half).astype(BF16)


def act_kernel(z, count, *refs):
    outs = refs[-count:]
    products, sums = joined(z, refs[:-count])
    shape = (z.group_each, z.group_each)
    diagonal = lax.broadcasted_iota(I32, shape, 0) == lax.broadcasted_iota(I32, shape, 1)
    sums = jnp.sum(jnp.where(diagonal, sums[:, :z.group_each], F32(0.0)), axis=1, keepdims=True)
    scale = lax.rsqrt(sums / D + EPS)
    gate = scale * products[:, :z.half]
    up = scale * products[:, z.half:]
    value = (gate / (F32(1.0) + jnp.exp(-gate)) * up).astype(BF16)
    rows = z.group_each // count
    for index, out in enumerate(outs):
        out[...] = value[index * rows:(index + 1) * rows]


def half_products(z, weights, units_refs, side):
    low = pl.multiple_of(side * z.half, z.half)
    units = jnp.concatenate([ref[...].astype(F32) for ref in units_refs], axis=0)
    results = []
    for expert in range(z.members):
        rows = units[expert * z.each:(expert + 1) * z.each].astype(BF16)
        results.append(dot(rows, weights[expert][pl.ds(low, z.half), :]))
    return jnp.concatenate(results, axis=0)


def own_down_kernel(z, *refs):
    weights, units_ref, out = refs[:z.members], refs[z.members:-1], refs[-1]
    out[...] = half_products(z, weights, units_ref, lax.axis_index("hidden") & 1)


def down_kernel(z, hands_on, *refs):
    weights, refs = refs[:z.members], refs[z.members:]
    units_ref, own_ref, outs = refs[:1], refs[1], refs[2:]
    if hands_on:
        outs[-1][...] = outs[0][...]
        outs = outs[1:-1]
    total = own_ref[...] + half_products(z, weights, units_ref, 1 - (lax.axis_index("hidden") & 1))
    value = dot(z.order(), total.astype(BF16), DOWN)
    low = 0
    for out in outs:
        out[...] = value[low:low + out.shape[0]].astype(BF16)
        low += out.shape[0]


def near_back_kernel(z, *refs):
    *blocks, out = refs
    values = [ref[...].astype(F32)[-z.piece:] for ref in blocks]
    out[...] = jnp.concatenate(values, axis=0).astype(BF16)


def combine_kernel(z, tick, last, weight_ref, rows_ref, kept_ref, *refs):
    if z.pairs:
        near = refs[0][...].astype(F32)
        near = [near[low:low + z.piece] for low in range(0, near.shape[0], z.piece)]
        returned, refs = [], refs[1:]
        for group in range(z.groups):
            if group < z.pairs:
                values, refs = [ref[...].astype(F32)[:z.piece] for ref in refs[:2]], refs[2:]
                returned += [values[0], near[group], values[1], near[z.groups + group]]
            else:
                values, refs = [ref[...].astype(F32) for ref in refs[:3]], refs[3:]
                returned += [values[0], near[group], values[1], values[2]]
    else:
        count = z.groups * z.pieces
        returned, refs = [ref[...].astype(F32) for ref in refs[:count]], refs[count:]
    stacked = []
    for piece in range(z.pieces):
        values = [returned[group * z.pieces + piece] for group in range(z.groups)]
        for step in range(z.peers // z.pieces):
            stacked += [value[step * z.pay:(step + 1) * z.pay] for value in values]
    stacked = jnp.concatenate(stacked, axis=0).astype(BF16)
    mixed = dot(weight_ref[...], stacked, DOWN)
    value = (rows_ref[...].astype(F32) + mixed).astype(BF16)
    if last:
        refs[0][...] = jnp.where(lax.axis_index("section") == tick, value, kept_ref[...])
        return
    routes_ref, out, outs = refs[0], refs[1], refs[2:]
    out[...] = jnp.where(lax.axis_index("section") == tick, value, kept_ref[...])
    hits, _, _ = slot_hits(z, routes_ref)
    send_rows(z, hits, value, outs, z.near)


def after_waits(waits, kernel, *refs):
    return kernel(*refs[waits:])


def call(kernel, sizes, megabytes, outs, in_specs, scratch, *args, waits=()):
    results = pl.pallas_call(
        functools.partial(after_waits, len(waits), functools.partial(kernel, *sizes)),
        out_shape=outs,
        in_specs=[VMEM] * len(waits) + in_specs,
        out_specs=[VMEM] * len(outs),
        scratch_shapes=scratch,
        compiler_params=pltpu.CompilerParams(vmem_limit_bytes=megabytes * 2**20),
    )(*waits, *args)
    return list(results)


def on_device(tokens, gate_up, down_proj, routes, gate_weights):
    sections = lax.axis_size("section")
    z = Sizes(tokens, gate_up, lax.axis_size("expert"), lax.axis_size("hidden"))
    parts = 2 if z.width % 256 == 0 else 1
    shape = jax.ShapeDtypeStruct
    pay = shape((z.piece, z.width), BF16)
    all_pay = shape((z.all_piece, z.width), BF16)
    merged = [pay, pay, shape((2 * z.piece, z.width), BF16)]
    whole = shape((z.rows, z.width), BF16)
    steps = sorted(range(z.peers), key=lambda step: -step.bit_length())

    def swap(value, step):
        pairs = [(i, i ^ step) for i in range(z.splits)]
        return lax.ppermute(value, "hidden", pairs)

    def exchanged(pieces):
        if z.pieces == 1:
            return [lax.all_to_all(pieces[0], "expert", split_axis=0, concat_axis=0, tiled=True)]
        result = list(pieces)
        for step in steps[:-1]:
            pairs = [(i, i ^ step) for i in range(z.peers)]
            result[step] = lax.ppermute(pieces[step], "expert", pairs)
        return result

    def across(value, step):
        return lax.ppermute(value, "expert", [(i, i ^ step) for i in range(z.peers)])

    def sent_back(pieces, group):
        if not z.pairs:
            return exchanged(pieces)
        own, near, *far = pieces
        return [own, near] + [across(value, 2 + step) for step, value in enumerate(far)]

    def near_back(returned):
        if not z.pairs:
            return sum(returned, [])
        blocks = [pieces[1] for pieces in returned] + [pieces[2] for pieces in returned[:z.pairs]]
        rows = shape((len(blocks) * z.piece, z.width), BF16)
        joint = call(near_back_kernel, (z,), 4, [rows], [VMEM] * len(blocks), [], *blocks)[0]
        return [across(joint, 1)] + sum([pieces[:1] + pieces[2:] for pieces in returned], [])

    def relayed(pieces, kept, tick):
        hop = [(tick, tick + 1)]
        rows = lax.ppermute(kept, "section", hop)
        if z.pieces == 1:
            return rows, [lax.ppermute(exchanged(pieces)[0], "section", hop)]
        far = {}
        for step in steps:
            if step >= z.near:
                pairs = [(tick * z.peers + i, (tick + 1) * z.peers + (i ^ step)) for i in range(z.peers)]
                far[step] = lax.ppermute(pieces[step - z.near], ("section", "expert"), pairs)
        result = call(near_kernel, (z,), 4, [all_pay] * z.near, [VMEM] * 2, [], routes, rows)
        for step in range(1, z.near):
            pairs = [(i, i ^ step) for i in range(z.peers)]
            result[step] = lax.ppermute(result[step], "expert", pairs)
        return rows, result + [far[step] for step in range(z.near, z.peers)]

    def load_down(group, after):
        return call(
            load_down_kernel, (z, group), 1,
            [pltpu.VMEM((z.units, z.width), BF16)] * z.members,
            [HBM], [pltpu.SemaphoreType.DMA((z.members,))], down_proj, waits=[after],
        )

    def products(received, group, waits):
        own, sent = call(
            up_kernel, (z, group), 6,
            [shape(z.partial, F32), shape(z.partial, BF16)],
            [VMEM] * (z.members + z.pieces),
            [
                pltpu.VMEM((z.members, 2 * z.each, 2 * z.width), BF16),
                pltpu.VMEM((2,) + z.partial, F32),
            ],
            *wide[group * z.members:(group + 1) * z.members], *received,
            waits=waits if group else tall[0][:1],
        )
        return own, swap(sent, 1)

    def pair_sums(own, other, waits):
        pair = call(
            pair_kernel, (z,), 2, [shape(z.partial, BF16)], [VMEM] * 2, [], own, other, waits=waits
        )[0]
        return [pair] + [swap(pair, step) for step in range(2, z.splits, 2)]

    def activated(pairs, waits):
        count = 1
        units = call(
            act_kernel, (z, count), 2,
            [shape((z.group_each // count, z.half), BF16)] * count, [VMEM] * len(pairs), [], *pairs, waits=waits,
        )
        return units, [swap(part, 1) for part in units]

    def down(halves, group, hand_on):
        own = call(
            own_down_kernel, (z,), 4, [shape((z.group_each, z.width), F32)],
            [VMEM] * (z.members + len(halves[0])), [], *tall[group], *halves[0],
        )[0]
        return call(
            down_kernel, (z, len(hand_on)), 4,
            (merged if group < z.pairs else [pay] * z.pieces)
            + [shape(value.shape, value.dtype) for value in hand_on],
            [VMEM] * (z.members + 1 + len(halves[1]) + len(hand_on)), [],
            *tall[group], *halves[1], own, *hand_on,
        )

    routes = routes[0].transpose(0, 2, 1)
    gates = gate_weights[0].transpose(0, 2, 1)
    rows = tokens.reshape(z.rows, z.width)
    kept = rows
    *sent, weight = call(
        pack_kernel, (z,), 3,
        [all_pay] * z.pieces + [shape((z.all_pay, z.rows), BF16)],
        [HBM] * 3,
        [
            pltpu.VMEM(routes.shape, routes.dtype),
            pltpu.VMEM(gates.shape, gates.dtype),
            pltpu.VMEM(rows.shape, rows.dtype),
            pltpu.SemaphoreType.DMA((3,)),
        ],
        *(pltpu.with_memory_space_constraint(value, pltpu.HBM) for value in (routes, gates, rows)),
    )
    received = exchanged(sent)
    gate_up = pltpu.with_memory_space_constraint(gate_up, pltpu.HBM)
    down_proj = pltpu.with_memory_space_constraint(down_proj, pltpu.HBM)
    wide = call(
        load_kernel, (z, parts), 1,
        [pltpu.VMEM((2 * z.width, z.units), BF16)] * z.local,
        [HBM], [pltpu.SemaphoreType.DMA((z.local * parts,))], gate_up, waits=[weight],
    )
    tall = [load_down(0, wide[-1])]
    groups = range(z.groups)
    for tick in range(sections):
        last = tick == sections - 1
        sums, returned = [], []
        early, waits = [], []
        for group in groups:
            own, other = products(received, group, [sums[-1][0]] if group else [])
            sums.append(pair_sums(own, other, waits))
            if tick == 0 and group + 1 < z.groups:
                tall.append(load_down(group + 1, sums[-1][0]))
                early = tall[-1][:1]
            if group == 0:
                halves = activated(sums[0], early)
                waits = list(halves[0][:1])
        for group in groups:
            if group:
                halves = activated(sums[group], outgoing[:1])
            hand_on = [routes] if tick == 0 and group == z.groups - 1 else []
            outgoing = down(halves, group, hand_on)
            if hand_on:
                pairs = [(i + 1, i) for i in range(sections - 1)]
                following = lax.ppermute(outgoing.pop(), "section", pairs)
            returned.append(sent_back(outgoing, group))
        returned = near_back(returned)
        kept, *sent = call(
            combine_kernel, (z, tick, last), 4,
            [whole] if last else [whole] + [all_pay] * (z.pieces - z.near),
            [VMEM] * (3 + len(returned) + (not last)), [],
            weight, rows, kept, *returned, *([] if last else [following]),
        )
        if not last:
            rows, received = relayed(sent, kept, tick)
    return kept.reshape(1, z.micro, z.tok, z.width)


def solution(mesh):
    placed = (
        P(None, "expert", "hidden"),
        P("section", "hidden", None, "expert"),
        P("section", "expert", "hidden"),
        P("section", None, "expert", None),
        P("section", None, "expert", None),
    )
    return jax.shard_map(
        on_device,
        mesh=mesh,
        in_specs=placed,
        out_specs=P("section", None, "expert", "hidden"),
        check_vma=False,
    )
```

```python
import functools

import jax
import jax.numpy as jnp
from jax import lax
from jax.experimental import pallas as pl
from jax.experimental.pallas import tpu as pltpu
from jax.sharding import PartitionSpec as P

D = 7168
FFE = 1024
CAP = 3
EPS = 1e-06
EXTRA = 16
CUTS = 2
VMEM = pl.BlockSpec(memory_space=pltpu.VMEM)
HBM = pl.BlockSpec(memory_space=pltpu.HBM)
BF16 = jnp.bfloat16
F32 = jnp.float32
I32 = jnp.int32
ACROSS = (((1,), (1,)), ((), ()))
DOWN = (((0,), (0,)), ((), ()))


def padded(count, unit):
    return -(-count // unit) * unit


def dot(a, b, dims=(((1,), (0,)), ((), ()))):
    return lax.dot_general(a, b, dims, preferred_element_type=F32)


def one_hot(mask):
    return jnp.where(mask, F32(1.0), F32(0.0))


def divided(value, divisor):
    if divisor == 1:
        return value, jnp.zeros_like(value)
    quotient = lax.shift_right_logical(value * (2**20 // divisor + 1), 20)
    return quotient, value - quotient * divisor


class Sizes:
    def __init__(self, tokens, gate_up, peers, splits):
        self.peers, self.splits = peers, splits
        self.micro, self.tok, self.width = tokens.shape
        self.rows = self.micro * self.tok
        self.units_dev = gate_up.shape[3]
        self.units = min(FFE, self.units_dev)
        self.half = self.units // 2
        self.local = self.units_dev // self.units
        self.groups = 2 if self.local % 2 == 0 else 1
        self.members = self.local // self.groups
        self.slots = self.micro * CAP
        self.pay = padded(self.members * self.slots, 8)
        self.pieces = peers if peers <= 8 else 1
        self.pairs = self.groups - 1 if self.pieces == 4 else 0
        self.near = self.pieces // 2
        self.repacked = [step for step in range(self.pieces) if step != self.near]
        self.group_pay = peers * self.pay
        self.piece = self.group_pay // self.pieces
        self.all_pay = self.groups * self.group_pay
        self.all_piece = self.groups * self.piece
        self.each = padded(peers * self.slots, 8)
        self.group_each = self.members * self.each
        self.partial = (self.group_each + EXTRA, 2 * self.half)

    def order(self):
        shape = (self.group_each, self.group_pay)
        row = lax.broadcasted_iota(I32, (self.group_each, 1), 0)
        expert, rest = divided(row, self.each)
        step, slot = divided(rest, self.slots)
        target = jnp.where(step < self.peers, step * self.pay + expert * self.slots + slot, -1)
        return one_hot(lax.broadcasted_iota(I32, shape, 1) == target).astype(BF16)


def line_up(z, ref):
    total = None
    for batch in range(z.micro):
        shape = (z.tok, z.rows)
        place = lax.broadcasted_iota(I32, shape, 1) == lax.broadcasted_iota(I32, shape, 0) + batch * z.tok
        value = dot(ref[batch].astype(F32).astype(BF16), one_hot(place).astype(BF16))
        total = value if total is None else total + value
    return total


def slot_hits(z, routes_ref):
    row = lax.broadcasted_iota(I32, (z.all_pay, 1), 0)
    step, rest = divided(row, z.groups * z.pay)
    group, place = divided(rest, z.pay)
    member, inside = divided(place, z.slots)
    batch, rank = divided(inside, CAP)
    rank = jnp.where(member < z.members, rank, -1)
    owner = step ^ lax.axis_index("expert") if z.pieces > 1 else step
    if z.units_dev >= FFE:
        expert = owner * z.local + group * z.members + member
    else:
        expert = lax.shift_right_logical(owner, (FFE // z.units_dev).bit_length() - 1)
    routes = line_up(z, routes_ref)
    token = lax.broadcasted_iota(I32, (z.all_pay, z.rows), 1)
    start = batch * z.tok
    same = (token >= start) & (token < start + z.tok)
    expert = expert.astype(F32)
    first = (routes[0:1, :] == expert) & same
    second = (routes[1:2, :] == expert) & same
    chosen = one_hot(first | second)
    shape = (z.rows, z.rows)
    before = lax.broadcasted_iota(I32, shape, 0) < lax.broadcasted_iota(I32, shape, 1)
    count = dot(chosen.astype(BF16), one_hot(before).astype(BF16))
    hits = jnp.where(count == rank.astype(F32), chosen, F32(0.0))
    return hits, first, second


def send_rows(z, hits, rows, outs, steps):
    hits = [hits[step * z.all_piece:(step + 1) * z.all_piece] for step in steps]
    value = dot(jnp.concatenate(hits, axis=0).astype(BF16), rows)
    for index, out in enumerate(outs):
        out[...] = value[index * z.all_piece:(index + 1) * z.all_piece].astype(BF16)


def repack_kernel(z, routes_ref, rows_ref, *outs):
    hits, _, _ = slot_hits(z, routes_ref)
    send_rows(z, hits, rows_ref[...], outs, z.repacked)


def group_rows(z, group, pieces):
    result = []
    for piece in pieces:
        value = piece[...].astype(F32)
        for step in range(z.peers // z.pieces):
            low = (step * z.groups + group) * z.pay
            result.append(value[low:low + z.pay])
    return jnp.concatenate(result, axis=0)


def pack_kernel(z, *refs):
    sources, outs = refs[:3], refs[3:-4]
    routes_ref, gates_ref, rows_ref, sems = refs[-4:]
    copies = [
        pltpu.make_async_copy(source, target, sems.at[index])
        for index, (source, target) in enumerate(zip(sources, refs[-4:-1]))
    ]
    for copy in copies:
        copy.start()
    for copy in copies:
        copy.wait()
    hits, first, second = slot_hits(z, routes_ref)
    gates = line_up(z, gates_ref)
    weight = jnp.where(first, gates[0:1, :], F32(0.0)) + jnp.where(second, gates[1:2, :], F32(0.0))
    outs[-1][...] = (hits * weight).astype(BF16)
    send_rows(z, hits, rows_ref[...], outs[:-1], range(z.pieces))


def load_kernel(z, parts, gate_up, *refs):
    outs, sems = refs[:-1], refs[-1]
    flat = gate_up.reshape(2 * z.width, z.units_dev)
    depth = 2 * z.width // parts
    copies = []
    for expert in range(z.local):
        for part in range(parts):
            copies.append(
                pltpu.make_async_copy(
                    flat.at[pl.ds(part * depth, depth), pl.ds(expert * z.units, z.units)],
                    outs[expert].at[pl.ds(part * depth, depth)],
                    sems.at[expert * parts + part],
                )
            )
    for copy in copies:
        copy.start()
    for copy in copies:
        copy.wait()


def load_down_kernel(z, group, down_proj, *refs):
    outs, sems = refs[:z.members], refs[-1]
    copies = []
    for index in range(z.members):
        low = (group * z.members + index) * z.units
        copies.append(
            pltpu.make_async_copy(down_proj.at[0, pl.ds(low, z.units), :], outs[index], sems.at[index])
        )
    for copy in copies:
        copy.start()
    for copy in copies:
        copy.wait()


def split_sums(sums, lanes):
    high = sums.astype(BF16).astype(F32)
    row = lax.broadcasted_iota(I32, sums.shape, 0)
    both = jnp.where(row == 0, high, jnp.where(row == 1, sums - high, F32(0.0)))
    if both.shape[1] < lanes:
        both = jnp.concatenate([both, jnp.zeros((EXTRA, lanes - both.shape[1]), F32)], axis=1)
    return both


def up_kernel(z, group, *refs):
    weights, refs = refs[:z.members], refs[z.members:]
    received, refs = refs[:z.pieces], refs[z.pieces:]
    own, *sent, spread, staged = refs
    rows = dot(z.order(), group_rows(z, group, received).astype(BF16))
    squares = rows * rows
    high = squares.astype(BF16)
    low = (squares - high.astype(F32)).astype(BF16)
    ones = jnp.ones((EXTRA, z.width), BF16)
    sums = dot(ones, high, ACROSS) + dot(ones, low, ACROSS)
    rows = rows.astype(BF16)
    block = 128
    shape = (block, 2 * block)
    target = lax.broadcasted_iota(I32, shape, 1) - 2 * lax.broadcasted_iota(I32, shape, 0)
    placing = [one_hot(target == side).astype(BF16) for side in range(2)]
    for piece in range(z.width // block):
        columns = slice(piece * block, (piece + 1) * block)
        gate, up = dot(rows[:, columns], placing[0]), dot(rows[:, columns], placing[1])
        for expert in range(z.members):
            here = slice(expert * z.each, (expert + 1) * z.each)
            both = jnp.concatenate([gate[here], up[here]], axis=0).astype(BF16)
            spread[expert, :, 2 * piece * block:2 * (piece + 1) * block] = both
    totals = [dot(spread[expert], weights[expert][...]) for expert in range(z.members)]
    extra = split_sums(sums, 2 * z.half)
    for side in range(2):
        columns = slice(side * z.half, (side + 1) * z.half)
        gate = jnp.concatenate([total[:z.each, columns] for total in totals], axis=0)
        up = jnp.concatenate([total[z.each:, columns] for total in totals], axis=0)
        staged[side, :z.group_each, :] = jnp.concatenate([gate, up], axis=1)
        staged[side, z.group_each:, :] = extra
    core = lax.axis_index("hidden") & 1
    own[...] = staged[core]
    rows = z.partial[0] // CUTS
    value = staged[1 - core]
    for index, out in enumerate(sent):
        out[...] = value[index * rows:(index + 1) * rows].astype(BF16)


def joined(z, refs):
    total = refs[0][...].astype(F32)
    for ref in refs[1:]:
        total = total + ref[...].astype(F32)
    products, extra = total[:z.group_each], total[z.group_each:]
    row = lax.broadcasted_iota(I32, extra.shape, 0)
    sums = jnp.sum(jnp.where(row < 2, extra, F32(0.0)), axis=0, keepdims=True)
    return products, sums


def pair_kernel(z, own, *refs):
    *other, out = refs
    products, sums = joined(z, [own[...], jnp.concatenate([ref[...].astype(F32) for ref in other], axis=0)])
    out[:z.group_each, :] = products.astype(BF16)
    sums = jnp.broadcast_to(sums, (EXTRA, 2 * z.half))
    out[z.group_each:, :] = split_sums(sums, 2 * z.half).astype(BF16)


def act_kernel(z, count, *refs):
    outs = refs[-count:]
    products, sums = joined(z, refs[:-count])
    shape = (z.group_each, z.group_each)
    diagonal = lax.broadcasted_iota(I32, shape, 0) == lax.broadcasted_iota(I32, shape, 1)
    sums = jnp.sum(jnp.where(diagonal, sums[:, :z.group_each], F32(0.0)), axis=1, keepdims=True)
    scale = lax.rsqrt(sums / D + EPS)
    gate = scale * products[:, :z.half]
    up = scale * products[:, z.half:]
    value = (gate / (F32(1.0) + jnp.exp(-gate)) * up).astype(BF16)
    rows = z.group_each // count
    for index, out in enumerate(outs):
        out[...] = value[index * rows:(index + 1) * rows]


def half_products(z, weights, units_refs, side):
    low = pl.multiple_of(side * z.half, z.half)
    units = jnp.concatenate([ref[...].astype(F32) for ref in units_refs], axis=0)
    results = []
    for expert in range(z.members):
        rows = units[expert * z.each:(expert + 1) * z.each].astype(BF16)
        results.append(dot(rows, weights[expert][pl.ds(low, z.half), :]))
    return jnp.concatenate(results, axis=0)


def own_down_kernel(z, *refs):
    weights, units_ref, out = refs[:z.members], refs[z.members:-1], refs[-1]
    out[...] = half_products(z, weights, units_ref, lax.axis_index("hidden") & 1)


def down_kernel(z, hands_on, *refs):
    weights, refs = refs[:z.members], refs[z.members:]
    units_ref, own_ref, outs = refs[:1], refs[1], refs[2:]
    if hands_on:
        outs[-1][...] = outs[0][...]
        outs = outs[1:-1]
    total = own_ref[...] + half_products(z, weights, units_ref, 1 - (lax.axis_index("hidden") & 1))
    value = dot(z.order(), total.astype(BF16), DOWN)
    low = 0
    for out in outs:
        out[...] = value[low:low + out.shape[0]].astype(BF16)
        low += out.shape[0]


def second_kernel(z, pair_ref, out):
    out[...] = pair_ref[...].astype(F32)[z.piece:].astype(BF16)


def combine_kernel(z, tick, last, weight_ref, rows_ref, kept_ref, *refs):
    count = z.groups * z.pieces
    returned, refs = [ref[...].astype(F32)[:z.piece] for ref in refs[:count]], refs[count:]
    stacked = []
    for piece in range(z.pieces):
        values = [returned[group * z.pieces + piece] for group in range(z.groups)]
        for step in range(z.peers // z.pieces):
            stacked += [value[step * z.pay:(step + 1) * z.pay] for value in values]
    stacked = jnp.concatenate(stacked, axis=0).astype(BF16)
    mixed = dot(weight_ref[...], stacked, DOWN)
    value = (rows_ref[...].astype(F32) + mixed).astype(BF16)
    if last:
        refs[0][...] = jnp.where(lax.axis_index("section") == tick, value, kept_ref[...])
        return
    routes_ref, out, outs = refs[0], refs[1], refs[2:]
    out[...] = jnp.where(lax.axis_index("section") == tick, value, kept_ref[...])
    hits, _, _ = slot_hits(z, routes_ref)
    send_rows(z, hits, value, outs, [z.near])


def after_waits(waits, kernel, *refs):
    return kernel(*refs[waits:])


def call(kernel, sizes, megabytes, outs, in_specs, scratch, *args, waits=()):
    results = pl.pallas_call(
        functools.partial(after_waits, len(waits), functools.partial(kernel, *sizes)),
        out_shape=outs,
        in_specs=[VMEM] * len(waits) + in_specs,
        out_specs=[VMEM] * len(outs),
        scratch_shapes=scratch,
        compiler_params=pltpu.CompilerParams(vmem_limit_bytes=megabytes * 2**20),
    )(*waits, *args)
    return list(results)


def on_device(tokens, gate_up, down_proj, routes, gate_weights):
    sections = lax.axis_size("section")
    z = Sizes(tokens, gate_up, lax.axis_size("expert"), lax.axis_size("hidden"))
    parts = 2 if z.width % 256 == 0 else 1
    shape = jax.ShapeDtypeStruct
    pay = shape((z.piece, z.width), BF16)
    all_pay = shape((z.all_piece, z.width), BF16)
    merged = [pay, pay, shape((2 * z.piece, z.width), BF16)]
    whole = shape((z.rows, z.width), BF16)
    steps = sorted(range(z.peers), key=lambda step: -step.bit_length())

    def swap(value, step):
        pairs = [(i, i ^ step) for i in range(z.splits)]
        return lax.ppermute(value, "hidden", pairs)

    def exchanged(pieces):
        if z.pieces == 1:
            return [lax.all_to_all(pieces[0], "expert", split_axis=0, concat_axis=0, tiled=True)]
        result = list(pieces)
        for step in steps[:-1]:
            pairs = [(i, i ^ step) for i in range(z.peers)]
            result[step] = lax.ppermute(pieces[step], "expert", pairs)
        return result

    def across(value, step):
        return lax.ppermute(value, "expert", [(i, i ^ step) for i in range(z.peers)])

    def sent_back(pieces, group):
        if group >= z.pairs:
            return exchanged(pieces)
        own, near, far = pieces
        far = across(far, 2)
        second = call(second_kernel, (z,), 2, [pay], [VMEM], [], far)[0]
        return [own, across(near, 1), far, across(second, 1)]

    def relayed(pieces, kept, tick):
        hop = [(tick, tick + 1)]
        rows = lax.ppermute(kept, "section", hop)
        if z.pieces == 1:
            return rows, [lax.ppermute(exchanged(pieces)[0], "section", hop)]
        pairs = [(tick * z.peers + i, (tick + 1) * z.peers + (i ^ z.near)) for i in range(z.peers)]
        far = lax.ppermute(pieces[0], ("section", "expert"), pairs)
        result = call(repack_kernel, (z,), 4, [all_pay] * (z.pieces - 1), [VMEM] * 2, [], routes, rows)
        result.insert(z.near, far)
        for step in steps[:-1]:
            if step != z.near:
                result[step] = across(result[step], step)
        return rows, result

    def load_down(group, after):
        return call(
            load_down_kernel, (z, group), 1,
            [pltpu.VMEM((z.units, z.width), BF16)] * z.members,
            [HBM], [pltpu.SemaphoreType.DMA((z.members,))], down_proj, waits=[after],
        )

    def products(received, group, waits):
        own, *sent = call(
            up_kernel, (z, group), 6,
            [shape(z.partial, F32)] + [shape((z.partial[0] // CUTS, z.partial[1]), BF16)] * CUTS,
            [VMEM] * (z.members + z.pieces),
            [
                pltpu.VMEM((z.members, 2 * z.each, 2 * z.width), BF16),
                pltpu.VMEM((2,) + z.partial, F32),
            ],
            *wide[group * z.members:(group + 1) * z.members], *received,
            waits=waits if group else tall[0][:1],
        )
        return own, [swap(value, 1) for value in sent]

    def pair_sums(own, other, waits):
        pair = call(
            pair_kernel, (z,), 2, [shape(z.partial, BF16)], [VMEM] * (1 + CUTS), [], own, *other, waits=waits
        )[0]
        return [pair] + [swap(pair, step) for step in range(2, z.splits, 2)]

    def activated(pairs, waits):
        count = 1
        units = call(
            act_kernel, (z, count), 2,
            [shape((z.group_each // count, z.half), BF16)] * count, [VMEM] * len(pairs), [], *pairs, waits=waits,
        )
        return units, [swap(part, 1) for part in units]

    def down(halves, group, hand_on):
        own = call(
            own_down_kernel, (z,), 4, [shape((z.group_each, z.width), F32)],
            [VMEM] * (z.members + len(halves[0])), [], *tall[group], *halves[0],
        )[0]
        return call(
            down_kernel, (z, len(hand_on)), 4,
            (merged if group < z.pairs else [pay] * z.pieces)
            + [shape(value.shape, value.dtype) for value in hand_on],
            [VMEM] * (z.members + 1 + len(halves[1]) + len(hand_on)), [],
            *tall[group], *halves[1], own, *hand_on,
        )

    routes = routes[0].transpose(0, 2, 1)
    gates = gate_weights[0].transpose(0, 2, 1)
    rows = tokens.reshape(z.rows, z.width)
    kept = rows
    *sent, weight = call(
        pack_kernel, (z,), 3,
        [all_pay] * z.pieces + [shape((z.all_pay, z.rows), BF16)],
        [HBM] * 3,
        [
            pltpu.VMEM(routes.shape, routes.dtype),
            pltpu.VMEM(gates.shape, gates.dtype),
            pltpu.VMEM(rows.shape, rows.dtype),
            pltpu.SemaphoreType.DMA((3,)),
        ],
        *(pltpu.with_memory_space_constraint(value, pltpu.HBM) for value in (routes, gates, rows)),
    )
    received = exchanged(sent)
    gate_up = pltpu.with_memory_space_constraint(gate_up, pltpu.HBM)
    down_proj = pltpu.with_memory_space_constraint(down_proj, pltpu.HBM)
    wide = call(
        load_kernel, (z, parts), 1,
        [pltpu.VMEM((2 * z.width, z.units), BF16)] * z.local,
        [HBM], [pltpu.SemaphoreType.DMA((z.local * parts,))], gate_up, waits=[weight],
    )
    tall = [load_down(0, wide[-1])]
    groups = range(z.groups)
    for tick in range(sections):
        last = tick == sections - 1
        sums, returned = [], []
        early, waits = [], []
        for group in groups:
            own, other = products(received, group, [sums[-1][0]] if group else [])
            sums.append(pair_sums(own, other, waits))
            if tick == 0 and group + 1 < z.groups:
                tall.append(load_down(group + 1, sums[-1][0]))
                early = tall[-1][:1]
            if group == 0:
                halves = activated(sums[0], early)
        for group in groups:
            if group:
                halves = activated(sums[group], outgoing[:1])
            hand_on = [routes] if tick == 0 and group == z.groups - 1 else []
            outgoing = down(halves, group, hand_on)
            if hand_on:
                pairs = [(i + 1, i) for i in range(sections - 1)]
                following = lax.ppermute(outgoing.pop(), "section", pairs)
            returned.append(sent_back(outgoing, group))
        returned = sum(returned, [])
        kept, *sent = call(
            combine_kernel, (z, tick, last), 4,
            [whole] if last else [whole, all_pay],
            [VMEM] * (3 + len(returned) + (not last)), [],
            weight, rows, kept, *returned, *([] if last else [following]),
        )
        if not last:
            rows, received = relayed(sent, kept, tick)
    return kept.reshape(1, z.micro, z.tok, z.width)


def solution(mesh):
    placed = (
        P(None, "expert", "hidden"),
        P("section", "hidden", None, "expert"),
        P("section", "expert", "hidden"),
        P("section", None, "expert", None),
        P("section", None, "expert", None),
    )
    return jax.shard_map(
        on_device,
        mesh=mesh,
        in_specs=placed,
        out_specs=P("section", None, "expert", "hidden"),
        check_vma=False,
    )
```

```python
import functools

import jax
import jax.numpy as jnp
from jax import lax
from jax.experimental import pallas as pl
from jax.experimental.pallas import tpu as pltpu
from jax.sharding import PartitionSpec as P

D = 7168
FFE = 1024
CAP = 3
EPS = 1e-06
EXTRA = 16
CUTS = 2
VMEM = pl.BlockSpec(memory_space=pltpu.VMEM)
HBM = pl.BlockSpec(memory_space=pltpu.HBM)
BF16 = jnp.bfloat16
F32 = jnp.float32
I32 = jnp.int32
ACROSS = (((1,), (1,)), ((), ()))
DOWN = (((0,), (0,)), ((), ()))


def padded(count, unit):
    return -(-count // unit) * unit


def dot(a, b, dims=(((1,), (0,)), ((), ()))):
    return lax.dot_general(a, b, dims, preferred_element_type=F32)


def one_hot(mask):
    return jnp.where(mask, F32(1.0), F32(0.0))


def divided(value, divisor):
    if divisor == 1:
        return value, jnp.zeros_like(value)
    quotient = lax.shift_right_logical(value * (2**20 // divisor + 1), 20)
    return quotient, value - quotient * divisor


class Sizes:
    def __init__(self, tokens, gate_up, peers, splits):
        self.peers, self.splits = peers, splits
        self.micro, self.tok, self.width = tokens.shape
        self.rows = self.micro * self.tok
        self.units_dev = gate_up.shape[3]
        self.units = min(FFE, self.units_dev)
        self.half = self.units // 2
        self.local = self.units_dev // self.units
        self.groups = 2 if self.local % 2 == 0 else 1
        self.members = self.local // self.groups
        self.slots = self.micro * CAP
        self.pay = padded(self.members * self.slots, 8)
        self.pieces = peers if peers <= 8 else 1
        self.pairs = self.groups - 1 if self.pieces == 4 else 0
        self.near = self.pieces // 2
        self.listed = sorted(range(self.pieces), key=lambda step: -step.bit_length())
        self.repacked = [step for step in range(self.pieces) if step != self.near]
        self.group_pay = peers * self.pay
        self.piece = self.group_pay // self.pieces
        self.all_pay = self.groups * self.group_pay
        self.all_piece = self.groups * self.piece
        self.each = padded(peers * self.slots, 8)
        self.group_each = self.members * self.each
        self.partial = (self.group_each + EXTRA, 2 * self.half)

    def order(self):
        shape = (self.group_each, self.group_pay)
        row = lax.broadcasted_iota(I32, (self.group_each, 1), 0)
        expert, rest = divided(row, self.each)
        step, slot = divided(rest, self.slots)
        target = jnp.where(step < self.peers, step * self.pay + expert * self.slots + slot, -1)
        return one_hot(lax.broadcasted_iota(I32, shape, 1) == target).astype(BF16)


def line_up(z, ref):
    total = None
    for batch in range(z.micro):
        shape = (z.tok, z.rows)
        place = lax.broadcasted_iota(I32, shape, 1) == lax.broadcasted_iota(I32, shape, 0) + batch * z.tok
        value = dot(ref[batch].astype(F32).astype(BF16), one_hot(place).astype(BF16))
        total = value if total is None else total + value
    return total


def slot_hits(z, routes_ref):
    row = lax.broadcasted_iota(I32, (z.all_pay, 1), 0)
    step, rest = divided(row, z.groups * z.pay)
    group, place = divided(rest, z.pay)
    member, inside = divided(place, z.slots)
    batch, rank = divided(inside, CAP)
    rank = jnp.where(member < z.members, rank, -1)
    owner = step ^ lax.axis_index("expert") if z.pieces > 1 else step
    if z.units_dev >= FFE:
        expert = owner * z.local + group * z.members + member
    else:
        expert = lax.shift_right_logical(owner, (FFE // z.units_dev).bit_length() - 1)
    routes = line_up(z, routes_ref)
    token = lax.broadcasted_iota(I32, (z.all_pay, z.rows), 1)
    start = batch * z.tok
    same = (token >= start) & (token < start + z.tok)
    expert = expert.astype(F32)
    first = (routes[0:1, :] == expert) & same
    second = (routes[1:2, :] == expert) & same
    chosen = one_hot(first | second)
    shape = (z.rows, z.rows)
    before = lax.broadcasted_iota(I32, shape, 0) < lax.broadcasted_iota(I32, shape, 1)
    count = dot(chosen.astype(BF16), one_hot(before).astype(BF16))
    hits = jnp.where(count == rank.astype(F32), chosen, F32(0.0))
    return hits, first, second


def send_rows(z, hits, rows, outs, steps):
    hits = [hits[step * z.all_piece:(step + 1) * z.all_piece] for step in steps]
    value = dot(jnp.concatenate(hits, axis=0).astype(BF16), rows)
    for index, out in enumerate(outs):
        out[...] = value[index * z.all_piece:(index + 1) * z.all_piece].astype(BF16)


def repack_kernel(z, routes_ref, rows_ref, *outs):
    hits, _, _ = slot_hits(z, routes_ref)
    send_rows(z, hits, rows_ref[...], outs, z.repacked)


def group_rows(z, group, pieces):
    result = []
    for piece in pieces:
        value = piece[...].astype(F32)
        for step in range(z.peers // z.pieces):
            low = (step * z.groups + group) * z.pay
            result.append(value[low:low + z.pay])
    return jnp.concatenate(result, axis=0)


def pack_kernel(z, *refs):
    sources, outs = refs[:3], refs[3:-4]
    routes_ref, gates_ref, rows_ref, sems = refs[-4:]
    copies = [
        pltpu.make_async_copy(source, target, sems.at[index])
        for index, (source, target) in enumerate(zip(sources, refs[-4:-1]))
    ]
    for copy in copies:
        copy.start()
    for copy in copies:
        copy.wait()
    hits, first, second = slot_hits(z, routes_ref)
    gates = line_up(z, gates_ref)
    weight = jnp.where(first, gates[0:1, :], F32(0.0)) + jnp.where(second, gates[1:2, :], F32(0.0))
    outs[-1][...] = (hits * weight).astype(BF16)
    send_rows(z, hits, rows_ref[...], outs[:-1], range(z.pieces))


def load_kernel(z, parts, gate_up, *refs):
    outs, sems = refs[:-1], refs[-1]
    flat = gate_up.reshape(2 * z.width, z.units_dev)
    depth = 2 * z.width // parts
    copies = []
    for expert in range(z.local):
        for part in range(parts):
            rows = pl.ds(part * depth, depth)
            copies.append(
                pltpu.make_async_copy(
                    flat.at[rows, pl.ds(expert * z.units, z.units)],
                    outs[expert].at[rows],
                    sems.at[expert * parts + part],
                )
            )
    for copy in copies:
        copy.start()
    for copy in copies:
        copy.wait()


def load_down_kernel(z, down_proj, *refs):
    outs, sems = refs[:-1], refs[-1]
    copies = [
        pltpu.make_async_copy(
            down_proj.at[0, pl.ds(expert * z.units, z.units), :], outs[expert], sems.at[expert]
        )
        for expert in range(z.local)
    ]
    for copy in copies:
        copy.start()
    for copy in copies:
        copy.wait()


def split_sums(sums, lanes):
    high = sums.astype(BF16).astype(F32)
    row = lax.broadcasted_iota(I32, sums.shape, 0)
    both = jnp.where(row == 0, high, jnp.where(row == 1, sums - high, F32(0.0)))
    if both.shape[1] < lanes:
        both = jnp.concatenate([both, jnp.zeros((EXTRA, lanes - both.shape[1]), F32)], axis=1)
    return both


def up_kernel(z, group, *refs):
    weights, refs = refs[:z.members], refs[z.members:]
    received, refs = refs[:z.pieces], refs[z.pieces:]
    received = [received[z.listed.index(step)] for step in range(z.pieces)]
    own, *sent, spread, staged = refs
    rows = dot(z.order(), group_rows(z, group, received).astype(BF16))
    squares = rows * rows
    high = squares.astype(BF16)
    low = (squares - high.astype(F32)).astype(BF16)
    ones = jnp.ones((EXTRA, z.width), BF16)
    sums = dot(ones, high, ACROSS) + dot(ones, low, ACROSS)
    rows = rows.astype(BF16)
    block = 128
    shape = (block, 2 * block)
    target = lax.broadcasted_iota(I32, shape, 1) - 2 * lax.broadcasted_iota(I32, shape, 0)
    placing = [one_hot(target == side).astype(BF16) for side in range(2)]
    for piece in range(z.width // block):
        columns = slice(piece * block, (piece + 1) * block)
        gate, up = dot(rows[:, columns], placing[0]), dot(rows[:, columns], placing[1])
        for expert in range(z.members):
            here = slice(expert * z.each, (expert + 1) * z.each)
            both = jnp.concatenate([gate[here], up[here]], axis=0).astype(BF16)
            spread[expert, :, 2 * piece * block:2 * (piece + 1) * block] = both
    totals = [dot(spread[expert], weights[expert][...]) for expert in range(z.members)]
    extra = split_sums(sums, 2 * z.half)
    for side in range(2):
        columns = slice(side * z.half, (side + 1) * z.half)
        gate = jnp.concatenate([total[:z.each, columns] for total in totals], axis=0)
        up = jnp.concatenate([total[z.each:, columns] for total in totals], axis=0)
        staged[side, :z.group_each, :] = jnp.concatenate([gate, up], axis=1)
        staged[side, z.group_each:, :] = extra
    core = lax.axis_index("hidden") & 1
    own[...] = staged[core]
    rows = z.partial[0] // CUTS
    value = staged[1 - core]
    for index, out in enumerate(sent):
        out[...] = value[index * rows:(index + 1) * rows].astype(BF16)


def joined(z, refs):
    total = refs[0][...].astype(F32)
    for ref in refs[1:]:
        total = total + ref[...].astype(F32)
    products, extra = total[:z.group_each], total[z.group_each:]
    row = lax.broadcasted_iota(I32, extra.shape, 0)
    sums = jnp.sum(jnp.where(row < 2, extra, F32(0.0)), axis=0, keepdims=True)
    return products, sums


def pair_kernel(z, own, *refs):
    *other, out = refs
    products, sums = joined(z, [own[...], jnp.concatenate([ref[...].astype(F32) for ref in other], axis=0)])
    out[:z.group_each, :] = products.astype(BF16)
    sums = jnp.broadcast_to(sums, (EXTRA, 2 * z.half))
    out[z.group_each:, :] = split_sums(sums, 2 * z.half).astype(BF16)


def act_kernel(z, count, *refs):
    outs = refs[-count:]
    products, sums = joined(z, refs[:-count])
    shape = (z.group_each, z.group_each)
    diagonal = lax.broadcasted_iota(I32, shape, 0) == lax.broadcasted_iota(I32, shape, 1)
    sums = jnp.sum(jnp.where(diagonal, sums[:, :z.group_each], F32(0.0)), axis=1, keepdims=True)
    scale = lax.rsqrt(sums / D + EPS)
    gate = scale * products[:, :z.half]
    up = scale * products[:, z.half:]
    value = (gate / (F32(1.0) + jnp.exp(-gate)) * up).astype(BF16)
    rows = z.group_each // count
    for index, out in enumerate(outs):
        out[...] = value[index * rows:(index + 1) * rows]


def half_products(z, weights, units_refs, side):
    low = pl.multiple_of(side * z.half, z.half)
    units = jnp.concatenate([ref[...].astype(F32) for ref in units_refs], axis=0)
    results = []
    for expert in range(z.members):
        rows = units[expert * z.each:(expert + 1) * z.each].astype(BF16)
        results.append(dot(rows, weights[expert][pl.ds(low, z.half), :]))
    return jnp.concatenate(results, axis=0)


def own_down_kernel(z, *refs):
    weights, units_ref, out = refs[:z.members], refs[z.members:-1], refs[-1]
    out[...] = half_products(z, weights, units_ref, lax.axis_index("hidden") & 1)


def down_kernel(z, hands_on, *refs):
    weights, refs = refs[:z.members], refs[z.members:]
    units_ref, own_ref, outs = refs[:1], refs[1], refs[2:]
    if hands_on:
        outs[-1][...] = outs[0][...]
        outs = outs[1:-1]
    total = own_ref[...] + half_products(z, weights, units_ref, 1 - (lax.axis_index("hidden") & 1))
    value = dot(z.order(), total.astype(BF16), DOWN)
    low = 0
    for out in outs:
        out[...] = value[low:low + out.shape[0]].astype(BF16)
        low += out.shape[0]


def hand_on_kernel(source, target):
    target[...] = source[...]


def second_kernel(z, pair_ref, out):
    out[...] = pair_ref[...].astype(F32)[z.piece:].astype(BF16)


def combine_kernel(z, tick, last, weight_ref, rows_ref, kept_ref, *refs):
    count = z.groups * z.pieces
    returned, refs = [ref[...].astype(F32)[:z.piece] for ref in refs[:count]], refs[count:]
    stacked = []
    for piece in range(z.pieces):
        values = [returned[group * z.pieces + piece] for group in range(z.groups)]
        for step in range(z.peers // z.pieces):
            stacked += [value[step * z.pay:(step + 1) * z.pay] for value in values]
    stacked = jnp.concatenate(stacked, axis=0).astype(BF16)
    mixed = dot(weight_ref[...], stacked, DOWN)
    value = (rows_ref[...].astype(F32) + mixed).astype(BF16)
    if last:
        refs[0][...] = jnp.where(lax.axis_index("section") == tick, value, kept_ref[...])
        return
    routes_ref, out, outs = refs[0], refs[1], refs[2:]
    out[...] = jnp.where(lax.axis_index("section") == tick, value, kept_ref[...])
    hits, _, _ = slot_hits(z, routes_ref)
    send_rows(z, hits, value, outs, [z.near])


def after_waits(waits, kernel, *refs):
    return kernel(*refs[waits:])


def call(kernel, sizes, megabytes, outs, in_specs, scratch, *args, waits=()):
    results = pl.pallas_call(
        functools.partial(after_waits, len(waits), functools.partial(kernel, *sizes)),
        out_shape=outs,
        in_specs=[VMEM] * len(waits) + in_specs,
        out_specs=[VMEM] * len(outs),
        scratch_shapes=scratch,
        compiler_params=pltpu.CompilerParams(vmem_limit_bytes=megabytes * 2**20),
    )(*waits, *args)
    return list(results)


def on_device(tokens, gate_up, down_proj, routes, gate_weights):
    sections = lax.axis_size("section")
    z = Sizes(tokens, gate_up, lax.axis_size("expert"), lax.axis_size("hidden"))
    parts = 2 if z.width % 256 == 0 else 1
    shape = jax.ShapeDtypeStruct
    pay = shape((z.piece, z.width), BF16)
    all_pay = shape((z.all_piece, z.width), BF16)
    merged = [pay, pay, shape((2 * z.piece, z.width), BF16)]
    whole = shape((z.rows, z.width), BF16)
    steps = sorted(range(z.peers), key=lambda step: -step.bit_length())

    def swap(value, step):
        pairs = [(i, i ^ step) for i in range(z.splits)]
        return lax.ppermute(value, "hidden", pairs)

    def exchanged(pieces):
        if z.pieces == 1:
            return [lax.all_to_all(pieces[0], "expert", split_axis=0, concat_axis=0, tiled=True)]
        result = list(pieces)
        for step in steps[:-1]:
            pairs = [(i, i ^ step) for i in range(z.peers)]
            result[step] = lax.ppermute(pieces[step], "expert", pairs)
        return result

    def across(value, step):
        return lax.ppermute(value, "expert", [(i, i ^ step) for i in range(z.peers)])

    def sent_back(pieces, group):
        if group >= z.pairs:
            return exchanged(pieces)
        own, near, far = pieces
        far = across(far, 2)
        second = call(second_kernel, (z,), 2, [pay], [VMEM], [], far)[0]
        return [own, across(near, 1), far, across(second, 1)]

    def within(value, step, section):
        low = section * z.peers
        pairs = [(low + i, low + (i ^ step)) for i in range(z.peers)]
        return lax.ppermute(value, ("section", "expert"), pairs)

    def relayed(pieces, kept, tick):
        hop = [(tick, tick + 1)]
        rows = lax.ppermute(kept, "section", hop)
        if z.pieces == 1:
            return rows, [lax.ppermute(exchanged(pieces)[0], "section", hop)]
        far = within(pieces[0], z.near, tick)
        result = call(repack_kernel, (z,), 4, [all_pay] * (z.pieces - 1), [VMEM] * 2, [], routes, rows)
        far = call(hand_on_kernel, (), 2, [all_pay], [VMEM], [], far, waits=result[:1])[0]
        result.insert(z.near, lax.ppermute(far, "section", hop))
        for step in steps[:-1]:
            if step != z.near:
                result[step] = within(result[step], step, tick + 1)
        return rows, result

    def products(received, group, waits):
        own, *sent = call(
            up_kernel, (z, group), 6,
            [shape(z.partial, F32)] + [shape((z.partial[0] // CUTS, z.partial[1]), BF16)] * CUTS,
            [VMEM] * (z.members + z.pieces),
            [
                pltpu.VMEM((z.members, 2 * z.each, 2 * z.width), BF16),
                pltpu.VMEM((2,) + z.partial, F32),
            ],
            *wide[group * z.members:(group + 1) * z.members], *(received[step] for step in z.listed),
            waits=waits,
        )
        return own, [swap(value, 1) for value in sent]

    def pair_sums(own, other):
        pair = call(
            pair_kernel, (z,), 2, [shape(z.partial, BF16)], [VMEM] * (1 + CUTS), [], own, *other
        )[0]
        return [pair] + [swap(pair, step) for step in range(2, z.splits, 2)]

    def activated(pairs, waits):
        count = 1
        units = call(
            act_kernel, (z, count), 2,
            [shape((z.group_each // count, z.half), BF16)] * count, [VMEM] * len(pairs), [], *pairs, waits=waits,
        )
        return units, [swap(part, 1) for part in units]

    def down(halves, group, hand_on):
        own = call(
            own_down_kernel, (z,), 4, [shape((z.group_each, z.width), F32)],
            [VMEM] * (z.members + len(halves[0])), [], *tall[group], *halves[0],
        )[0]
        return call(
            down_kernel, (z, len(hand_on)), 4,
            (merged if group < z.pairs else [pay] * z.pieces)
            + [shape(value.shape, value.dtype) for value in hand_on],
            [VMEM] * (z.members + 1 + len(halves[1]) + len(hand_on)), [],
            *tall[group], *halves[1], own, *hand_on,
        )

    routes = routes[0].transpose(0, 2, 1)
    gates = gate_weights[0].transpose(0, 2, 1)
    rows = tokens.reshape(z.rows, z.width)
    kept = rows
    *sent, weight = call(
        pack_kernel, (z,), 3,
        [all_pay] * z.pieces + [shape((z.all_pay, z.rows), BF16)],
        [HBM] * 3,
        [
            pltpu.VMEM(routes.shape, routes.dtype),
            pltpu.VMEM(gates.shape, gates.dtype),
            pltpu.VMEM(rows.shape, rows.dtype),
            pltpu.SemaphoreType.DMA((3,)),
        ],
        *(pltpu.with_memory_space_constraint(value, pltpu.HBM) for value in (routes, gates, rows)),
    )
    received = exchanged(sent)
    gate_up = pltpu.with_memory_space_constraint(gate_up, pltpu.HBM)
    down_proj = pltpu.with_memory_space_constraint(down_proj, pltpu.HBM)
    wide = call(
        load_kernel, (z, parts), 1,
        [pltpu.VMEM((2 * z.width, z.units), BF16)] * z.local,
        [HBM], [pltpu.SemaphoreType.DMA((z.local * parts,))], gate_up, waits=[weight],
    )
    tall = call(
        load_down_kernel, (z,), 1,
        [pltpu.VMEM((z.units, z.width), BF16)] * z.local,
        [HBM], [pltpu.SemaphoreType.DMA((z.local,))], down_proj, waits=wide[-1:],
    )
    tall = [tall[group * z.members:(group + 1) * z.members] for group in range(z.groups)]
    groups = range(z.groups)
    for tick in range(sections):
        last = tick == sections - 1
        sums, returned = [], []
        for group in groups:
            own, other = products(received, group, [sums[-1][0]] if group else tall[0][:1])
            sums.append(pair_sums(own, other))
            if group == 0:
                halves = activated(sums[0], [])
        for group in groups:
            if group:
                halves = activated(sums[group], outgoing[:1])
            hand_on = [routes] if tick == 0 and group == z.groups - 1 else []
            outgoing = down(halves, group, hand_on)
            if hand_on:
                pairs = [(i + 1, i) for i in range(sections - 1)]
                following = lax.ppermute(outgoing.pop(), "section", pairs)
            returned.append(sent_back(outgoing, group))
        returned = sum(returned, [])
        kept, *sent = call(
            combine_kernel, (z, tick, last), 4,
            [whole] if last else [whole, all_pay],
            [VMEM] * (3 + len(returned) + (not last)), [],
            weight, rows, kept, *returned, *([] if last else [following]),
        )
        if not last:
            rows, received = relayed(sent, kept, tick)
    return kept.reshape(1, z.micro, z.tok, z.width)


def solution(mesh):
    placed = (
        P(None, "expert", "hidden"),
        P("section", "hidden", None, "expert"),
        P("section", "expert", "hidden"),
        P("section", None, "expert", None),
        P("section", None, "expert", None),
    )
    return jax.shard_map(
        on_device,
        mesh=mesh,
        in_specs=placed,
        out_specs=P("section", None, "expert", "hidden"),
        check_vma=False,
    )
```

```python
import functools

import jax
import jax.numpy as jnp
from jax import lax
from jax.experimental import pallas as pl
from jax.experimental.pallas import tpu as pltpu
from jax.sharding import PartitionSpec as P

D = 7168
FFE = 1024
CAP = 3
EPS = 1e-06
EXTRA = 16
CUTS = 2
VMEM = pl.BlockSpec(memory_space=pltpu.VMEM)
HBM = pl.BlockSpec(memory_space=pltpu.HBM)
BF16 = jnp.bfloat16
F32 = jnp.float32
I32 = jnp.int32
ACROSS = (((1,), (1,)), ((), ()))
DOWN = (((0,), (0,)), ((), ()))


def padded(count, unit):
    return -(-count // unit) * unit


def dot(a, b, dims=(((1,), (0,)), ((), ()))):
    return lax.dot_general(a, b, dims, preferred_element_type=F32)


def one_hot(mask):
    return jnp.where(mask, F32(1.0), F32(0.0))


def divided(value, divisor):
    if divisor == 1:
        return value, jnp.zeros_like(value)
    quotient = lax.shift_right_logical(value * (2**20 // divisor + 1), 20)
    return quotient, value - quotient * divisor


class Sizes:
    def __init__(self, tokens, gate_up, peers, splits):
        self.peers, self.splits = peers, splits
        self.micro, self.tok, self.width = tokens.shape
        self.rows = self.micro * self.tok
        self.units_dev = gate_up.shape[3]
        self.units = min(FFE, self.units_dev)
        self.half = self.units // 2
        self.local = self.units_dev // self.units
        self.groups = 2 if self.local % 2 == 0 else 1
        self.members = self.local // self.groups
        self.slots = self.micro * CAP
        self.pay = padded(self.members * self.slots, 8)
        self.pieces = peers if peers <= 8 else 1
        self.pairs = self.groups - 1 if self.pieces == 4 else 0
        self.near = self.pieces // 2
        self.listed = sorted(range(self.pieces), key=lambda step: -step.bit_length())
        self.repacked = [step for step in range(self.pieces) if step != self.near]
        self.group_pay = peers * self.pay
        self.piece = self.group_pay // self.pieces
        self.all_pay = self.groups * self.group_pay
        self.all_piece = self.groups * self.piece
        self.each = padded(peers * self.slots, 8)
        self.group_each = self.members * self.each
        self.partial = (self.group_each + EXTRA, 2 * self.half)

    def order(self):
        shape = (self.group_each, self.group_pay)
        row = lax.broadcasted_iota(I32, (self.group_each, 1), 0)
        expert, rest = divided(row, self.each)
        step, slot = divided(rest, self.slots)
        target = jnp.where(step < self.peers, step * self.pay + expert * self.slots + slot, -1)
        return one_hot(lax.broadcasted_iota(I32, shape, 1) == target).astype(BF16)


def line_up(z, ref):
    total = None
    for batch in range(z.micro):
        shape = (z.tok, z.rows)
        place = lax.broadcasted_iota(I32, shape, 1) == lax.broadcasted_iota(I32, shape, 0) + batch * z.tok
        value = dot(ref[batch].astype(F32).astype(BF16), one_hot(place).astype(BF16))
        total = value if total is None else total + value
    return total


def slot_hits(z, routes_ref):
    row = lax.broadcasted_iota(I32, (z.all_pay, 1), 0)
    step, rest = divided(row, z.groups * z.pay)
    group, place = divided(rest, z.pay)
    member, inside = divided(place, z.slots)
    batch, rank = divided(inside, CAP)
    rank = jnp.where(member < z.members, rank, -1)
    owner = step ^ lax.axis_index("expert") if z.pieces > 1 else step
    if z.units_dev >= FFE:
        expert = owner * z.local + group * z.members + member
    else:
        expert = lax.shift_right_logical(owner, (FFE // z.units_dev).bit_length() - 1)
    routes = line_up(z, routes_ref)
    token = lax.broadcasted_iota(I32, (z.all_pay, z.rows), 1)
    start = batch * z.tok
    same = (token >= start) & (token < start + z.tok)
    expert = expert.astype(F32)
    first = (routes[0:1, :] == expert) & same
    second = (routes[1:2, :] == expert) & same
    chosen = one_hot(first | second)
    shape = (z.rows, z.rows)
    before = lax.broadcasted_iota(I32, shape, 0) < lax.broadcasted_iota(I32, shape, 1)
    count = dot(chosen.astype(BF16), one_hot(before).astype(BF16))
    hits = jnp.where(count == rank.astype(F32), chosen, F32(0.0))
    return hits, first, second


def send_rows(z, hits, rows, outs, steps):
    hits = [hits[step * z.all_piece:(step + 1) * z.all_piece] for step in steps]
    value = dot(jnp.concatenate(hits, axis=0).astype(BF16), rows)
    for index, out in enumerate(outs):
        out[...] = value[index * z.all_piece:(index + 1) * z.all_piece].astype(BF16)


def repack_kernel(z, routes_ref, rows_ref, *outs):
    hits, _, _ = slot_hits(z, routes_ref)
    send_rows(z, hits, rows_ref[...], outs, z.repacked)


def group_rows(z, group, pieces):
    result = []
    for piece in pieces:
        value = piece[...].astype(F32)
        for step in range(z.peers // z.pieces):
            low = (step * z.groups + group) * z.pay
            result.append(value[low:low + z.pay])
    return jnp.concatenate(result, axis=0)


def pack_kernel(z, *refs):
    sources, outs = refs[:3], refs[3:-4]
    routes_ref, gates_ref, rows_ref, sems = refs[-4:]
    copies = [
        pltpu.make_async_copy(source, target, sems.at[index])
        for index, (source, target) in enumerate(zip(sources, refs[-4:-1]))
    ]
    for copy in copies:
        copy.start()
    for copy in copies:
        copy.wait()
    hits, first, second = slot_hits(z, routes_ref)
    gates = line_up(z, gates_ref)
    weight = jnp.where(first, gates[0:1, :], F32(0.0)) + jnp.where(second, gates[1:2, :], F32(0.0))
    outs[-1][...] = (hits * weight).astype(BF16)
    send_rows(z, hits, rows_ref[...], outs[:-1], range(z.pieces))


def load_kernel(z, parts, gate_up, *refs):
    outs, sems = refs[:-1], refs[-1]
    flat = gate_up.reshape(2 * z.width, z.units_dev)
    depth = 2 * z.width // parts
    copies = []
    for expert in range(z.local):
        for part in range(parts):
            rows = pl.ds(part * depth, depth)
            copies.append(
                pltpu.make_async_copy(
                    flat.at[rows, pl.ds(expert * z.units, z.units)],
                    outs[expert].at[rows],
                    sems.at[expert * parts + part],
                )
            )
    for copy in copies:
        copy.start()
    for copy in copies:
        copy.wait()


def load_down_kernel(z, down_proj, *refs):
    outs, sems = refs[:-1], refs[-1]
    copies = [
        pltpu.make_async_copy(
            down_proj.at[0, pl.ds(expert * z.units, z.units), :], outs[expert], sems.at[expert]
        )
        for expert in range(z.local)
    ]
    for copy in copies:
        copy.start()
    for copy in copies:
        copy.wait()


def split_sums(sums, lanes):
    high = sums.astype(BF16).astype(F32)
    row = lax.broadcasted_iota(I32, sums.shape, 0)
    both = jnp.where(row == 0, high, jnp.where(row == 1, sums - high, F32(0.0)))
    if both.shape[1] < lanes:
        both = jnp.concatenate([both, jnp.zeros((EXTRA, lanes - both.shape[1]), F32)], axis=1)
    return both


def up_kernel(z, group, *refs):
    weights, refs = refs[:z.members], refs[z.members:]
    received, refs = refs[:z.pieces], refs[z.pieces:]
    received = [received[z.listed.index(step)] for step in range(z.pieces)]
    own, *sent, spread, staged = refs
    rows = dot(z.order(), group_rows(z, group, received).astype(BF16))
    squares = rows * rows
    high = squares.astype(BF16)
    low = (squares - high.astype(F32)).astype(BF16)
    ones = jnp.ones((EXTRA, z.width), BF16)
    sums = dot(ones, high, ACROSS) + dot(ones, low, ACROSS)
    rows = rows.astype(BF16)
    block = 128
    shape = (block, 2 * block)
    target = lax.broadcasted_iota(I32, shape, 1) - 2 * lax.broadcasted_iota(I32, shape, 0)
    placing = [one_hot(target == side).astype(BF16) for side in range(2)]
    for piece in range(z.width // block):
        columns = slice(piece * block, (piece + 1) * block)
        gate, up = dot(rows[:, columns], placing[0]), dot(rows[:, columns], placing[1])
        for expert in range(z.members):
            here = slice(expert * z.each, (expert + 1) * z.each)
            both = jnp.concatenate([gate[here], up[here]], axis=0).astype(BF16)
            spread[expert, :, 2 * piece * block:2 * (piece + 1) * block] = both
    totals = [dot(spread[expert], weights[expert][...]) for expert in range(z.members)]
    extra = split_sums(sums, 2 * z.half)
    for side in range(2):
        columns = slice(side * z.half, (side + 1) * z.half)
        gate = jnp.concatenate([total[:z.each, columns] for total in totals], axis=0)
        up = jnp.concatenate([total[z.each:, columns] for total in totals], axis=0)
        staged[side, :z.group_each, :] = jnp.concatenate([gate, up], axis=1)
        staged[side, z.group_each:, :] = extra
    core = lax.axis_index("hidden") & 1
    own[...] = staged[core]
    rows = z.partial[0] // CUTS
    value = staged[1 - core]
    for index, out in enumerate(sent):
        out[...] = value[index * rows:(index + 1) * rows].astype(BF16)


def joined(z, refs):
    total = refs[0][...].astype(F32)
    for ref in refs[1:]:
        total = total + ref[...].astype(F32)
    products, extra = total[:z.group_each], total[z.group_each:]
    row = lax.broadcasted_iota(I32, extra.shape, 0)
    sums = jnp.sum(jnp.where(row < 2, extra, F32(0.0)), axis=0, keepdims=True)
    return products, sums


def pair_kernel(z, own, *refs):
    *other, out = refs
    products, sums = joined(z, [own[...], jnp.concatenate([ref[...].astype(F32) for ref in other], axis=0)])
    out[:z.group_each, :] = products.astype(BF16)
    sums = jnp.broadcast_to(sums, (EXTRA, 2 * z.half))
    out[z.group_each:, :] = split_sums(sums, 2 * z.half).astype(BF16)


def act_kernel(z, count, *refs):
    outs = refs[-count:]
    products, sums = joined(z, refs[:-count])
    shape = (z.group_each, z.group_each)
    diagonal = lax.broadcasted_iota(I32, shape, 0) == lax.broadcasted_iota(I32, shape, 1)
    sums = jnp.sum(jnp.where(diagonal, sums[:, :z.group_each], F32(0.0)), axis=1, keepdims=True)
    scale = lax.rsqrt(sums / D + EPS)
    gate = scale * products[:, :z.half]
    up = scale * products[:, z.half:]
    value = (gate / (F32(1.0) + jnp.exp(-gate)) * up).astype(BF16)
    rows = z.group_each // count
    for index, out in enumerate(outs):
        out[...] = value[index * rows:(index + 1) * rows]


def half_products(z, weights, units_refs, side):
    low = pl.multiple_of(side * z.half, z.half)
    units = jnp.concatenate([ref[...].astype(F32) for ref in units_refs], axis=0)
    results = []
    for expert in range(z.members):
        rows = units[expert * z.each:(expert + 1) * z.each].astype(BF16)
        results.append(dot(rows, weights[expert][pl.ds(low, z.half), :]))
    return jnp.concatenate(results, axis=0)


def own_down_kernel(z, *refs):
    weights, units_ref, out = refs[:z.members], refs[z.members:-1], refs[-1]
    out[...] = half_products(z, weights, units_ref, lax.axis_index("hidden") & 1)


def down_kernel(z, hands_on, *refs):
    weights, refs = refs[:z.members], refs[z.members:]
    units_ref, own_ref, outs = refs[:1], refs[1], refs[2:]
    if hands_on:
        outs[-1][...] = outs[0][...]
        outs = outs[1:-1]
    total = own_ref[...] + half_products(z, weights, units_ref, 1 - (lax.axis_index("hidden") & 1))
    value = dot(z.order(), total.astype(BF16), DOWN)
    low = 0
    for out in outs:
        out[...] = value[low:low + out.shape[0]].astype(BF16)
        low += out.shape[0]


def second_kernel(z, pair_ref, out):
    out[...] = pair_ref[...].astype(F32)[z.piece:].astype(BF16)


def combine_kernel(z, tick, last, weight_ref, rows_ref, kept_ref, *refs):
    count = z.groups * z.pieces
    returned, refs = [ref[...].astype(F32)[:z.piece] for ref in refs[:count]], refs[count:]
    stacked = []
    for piece in range(z.pieces):
        values = [returned[group * z.pieces + piece] for group in range(z.groups)]
        for step in range(z.peers // z.pieces):
            stacked += [value[step * z.pay:(step + 1) * z.pay] for value in values]
    stacked = jnp.concatenate(stacked, axis=0).astype(BF16)
    mixed = dot(weight_ref[...], stacked, DOWN)
    value = (rows_ref[...].astype(F32) + mixed).astype(BF16)
    if last:
        refs[0][...] = jnp.where(lax.axis_index("section") == tick, value, kept_ref[...])
        return
    routes_ref, out, outs = refs[0], refs[1], refs[2:]
    out[...] = jnp.where(lax.axis_index("section") == tick, value, kept_ref[...])
    hits, _, _ = slot_hits(z, routes_ref)
    send_rows(z, hits, value, outs, [z.near])


def after_waits(waits, kernel, *refs):
    return kernel(*refs[waits:])


def call(kernel, sizes, megabytes, outs, in_specs, scratch, *args, waits=()):
    results = pl.pallas_call(
        functools.partial(after_waits, len(waits), functools.partial(kernel, *sizes)),
        out_shape=outs,
        in_specs=[VMEM] * len(waits) + in_specs,
        out_specs=[VMEM] * len(outs),
        scratch_shapes=scratch,
        compiler_params=pltpu.CompilerParams(vmem_limit_bytes=megabytes * 2**20),
    )(*waits, *args)
    return list(results)


def on_device(tokens, gate_up, down_proj, routes, gate_weights):
    sections = lax.axis_size("section")
    z = Sizes(tokens, gate_up, lax.axis_size("expert"), lax.axis_size("hidden"))
    parts = 2 if z.width % 256 == 0 else 1
    shape = jax.ShapeDtypeStruct
    pay = shape((z.piece, z.width), BF16)
    all_pay = shape((z.all_piece, z.width), BF16)
    merged = [pay, pay, shape((2 * z.piece, z.width), BF16)]
    whole = shape((z.rows, z.width), BF16)
    steps = sorted(range(z.peers), key=lambda step: -step.bit_length())

    def swap(value, step):
        pairs = [(i, i ^ step) for i in range(z.splits)]
        return lax.ppermute(value, "hidden", pairs)

    def exchanged(pieces):
        if z.pieces == 1:
            return [lax.all_to_all(pieces[0], "expert", split_axis=0, concat_axis=0, tiled=True)]
        result = list(pieces)
        for step in steps[:-1]:
            pairs = [(i, i ^ step) for i in range(z.peers)]
            result[step] = lax.ppermute(pieces[step], "expert", pairs)
        return result

    def across(value, step):
        return lax.ppermute(value, "expert", [(i, i ^ step) for i in range(z.peers)])

    def sent_back(pieces, group):
        if group >= z.pairs:
            return exchanged(pieces)
        own, near, far = pieces
        far = across(far, 2)
        second = call(second_kernel, (z,), 2, [pay], [VMEM], [], far)[0]
        return [own, across(near, 1), far, across(second, 1)]

    def within(value, step, section):
        low = section * z.peers
        pairs = [(low + i, low + (i ^ step)) for i in range(z.peers)]
        return lax.ppermute(value, ("section", "expert"), pairs)

    def relayed(pieces, kept, tick):
        hop = [(tick, tick + 1)]
        rows = lax.ppermute(kept, "section", hop)
        if z.pieces == 1:
            return rows, [lax.ppermute(exchanged(pieces)[0], "section", hop)]
        pairs = [(tick * z.peers + i, (tick + 1) * z.peers + (i ^ z.near)) for i in range(z.peers)]
        far = lax.ppermute(pieces[0], ("section", "expert"), pairs)
        result = call(repack_kernel, (z,), 4, [all_pay] * (z.pieces - 1), [VMEM] * 2, [], routes, rows)
        result.insert(z.near, far)
        for step in steps[:-1]:
            if step != z.near:
                result[step] = within(result[step], step, tick + 1)
        return rows, result

    def products(received, group, waits):
        own, *sent = call(
            up_kernel, (z, group), 6,
            [shape(z.partial, F32)] + [shape((z.partial[0] // CUTS, z.partial[1]), BF16)] * CUTS,
            [VMEM] * (z.members + z.pieces),
            [
                pltpu.VMEM((z.members, 2 * z.each, 2 * z.width), BF16),
                pltpu.VMEM((2,) + z.partial, F32),
            ],
            *wide[group * z.members:(group + 1) * z.members], *(received[step] for step in z.listed),
            waits=waits,
        )
        return own, [swap(value, 1) for value in sent]

    def pair_sums(own, other):
        pair = call(
            pair_kernel, (z,), 2, [shape(z.partial, BF16)], [VMEM] * (1 + CUTS), [], own, *other
        )[0]
        return [pair] + [swap(pair, step) for step in range(2, z.splits, 2)]

    def activated(pairs, waits):
        count = 1
        units = call(
            act_kernel, (z, count), 2,
            [shape((z.group_each // count, z.half), BF16)] * count, [VMEM] * len(pairs), [], *pairs, waits=waits,
        )
        return units, [swap(part, 1) for part in units]

    def down(halves, group, hand_on):
        own = call(
            own_down_kernel, (z,), 4, [shape((z.group_each, z.width), F32)],
            [VMEM] * (z.members + len(halves[0])), [], *tall[group], *halves[0],
        )[0]
        return call(
            down_kernel, (z, len(hand_on)), 4,
            (merged if group < z.pairs else [pay] * z.pieces)
            + [shape(value.shape, value.dtype) for value in hand_on],
            [VMEM] * (z.members + 1 + len(halves[1]) + len(hand_on)), [],
            *tall[group], *halves[1], own, *hand_on,
        )

    routes = routes[0].transpose(0, 2, 1)
    gates = gate_weights[0].transpose(0, 2, 1)
    rows = tokens.reshape(z.rows, z.width)
    kept = rows
    *sent, weight = call(
        pack_kernel, (z,), 3,
        [all_pay] * z.pieces + [shape((z.all_pay, z.rows), BF16)],
        [HBM] * 3,
        [
            pltpu.VMEM(routes.shape, routes.dtype),
            pltpu.VMEM(gates.shape, gates.dtype),
            pltpu.VMEM(rows.shape, rows.dtype),
            pltpu.SemaphoreType.DMA((3,)),
        ],
        *(pltpu.with_memory_space_constraint(value, pltpu.HBM) for value in (routes, gates, rows)),
    )
    received = exchanged(sent)
    gate_up = pltpu.with_memory_space_constraint(gate_up, pltpu.HBM)
    down_proj = pltpu.with_memory_space_constraint(down_proj, pltpu.HBM)
    wide = call(
        load_kernel, (z, parts), 1,
        [pltpu.VMEM((2 * z.width, z.units), BF16)] * z.local,
        [HBM], [pltpu.SemaphoreType.DMA((z.local * parts,))], gate_up, waits=[weight],
    )
    tall = call(
        load_down_kernel, (z,), 1,
        [pltpu.VMEM((z.units, z.width), BF16)] * z.local,
        [HBM], [pltpu.SemaphoreType.DMA((z.local,))], down_proj, waits=wide[-1:],
    )
    tall = [tall[group * z.members:(group + 1) * z.members] for group in range(z.groups)]
    groups = range(z.groups)
    for tick in range(sections):
        last = tick == sections - 1
        sums, returned = [], []
        for group in groups:
            own, other = products(received, group, [sums[-1][0]] if group else tall[0][:1])
            sums.append(pair_sums(own, other))
            if group == 0:
                halves = activated(sums[0], [])
        for group in groups:
            if group:
                halves = activated(sums[group], outgoing[:1])
            hand_on = [routes] if tick == 0 and group == z.groups - 1 else []
            outgoing = down(halves, group, hand_on)
            if hand_on:
                pairs = [(i + 1, i) for i in range(sections - 1)]
                following = lax.ppermute(outgoing.pop(), "section", pairs)
            returned.append(sent_back(outgoing, group))
        returned = sum(returned, [])
        kept, *sent = call(
            combine_kernel, (z, tick, last), 4,
            [whole] if last else [whole, all_pay],
            [VMEM] * (3 + len(returned) + (not last)), [],
            weight, rows, kept, *returned, *([] if last else [following]),
        )
        if not last:
            rows, received = relayed(sent, kept, tick)
    return kept.reshape(1, z.micro, z.tok, z.width)


def solution(mesh):
    placed = (
        P(None, "expert", "hidden"),
        P("section", "hidden", None, "expert"),
        P("section", "expert", "hidden"),
        P("section", None, "expert", None),
        P("section", None, "expert", None),
    )
    return jax.shard_map(
        on_device,
        mesh=mesh,
        in_specs=placed,
        out_specs=P("section", None, "expert", "hidden"),
        check_vma=False,
    )
```

```python
import functools

import jax
import jax.numpy as jnp
from jax import lax
from jax.experimental import pallas as pl
from jax.experimental.pallas import tpu as pltpu
from jax.sharding import PartitionSpec as P

D = 7168
FFE = 1024
CAP = 3
EPS = 1e-06
EXTRA = 16
CUTS = 2
VMEM = pl.BlockSpec(memory_space=pltpu.VMEM)
HBM = pl.BlockSpec(memory_space=pltpu.HBM)
BF16 = jnp.bfloat16
F32 = jnp.float32
I32 = jnp.int32
ACROSS = (((1,), (1,)), ((), ()))
DOWN = (((0,), (0,)), ((), ()))


def padded(count, unit):
    return -(-count // unit) * unit


def dot(a, b, dims=(((1,), (0,)), ((), ()))):
    return lax.dot_general(a, b, dims, preferred_element_type=F32)


def one_hot(mask):
    return jnp.where(mask, F32(1.0), F32(0.0))


def divided(value, divisor):
    if divisor == 1:
        return value, jnp.zeros_like(value)
    quotient = lax.shift_right_logical(value * (2**20 // divisor + 1), 20)
    return quotient, value - quotient * divisor


class Sizes:
    def __init__(self, tokens, gate_up, peers, splits):
        self.peers, self.splits = peers, splits
        self.micro, self.tok, self.width = tokens.shape
        self.rows = self.micro * self.tok
        self.units_dev = gate_up.shape[3]
        self.units = min(FFE, self.units_dev)
        self.half = self.units // 2
        self.local = self.units_dev // self.units
        self.groups = 2 if self.local % 2 == 0 else 1
        self.members = self.local // self.groups
        self.slots = self.micro * CAP
        self.pay = padded(self.members * self.slots, 8)
        self.pieces = peers if peers <= 8 else 1
        self.pairs = self.groups - 1 if self.pieces == 4 else 0
        self.near = self.pieces // 2
        self.listed = sorted(range(self.pieces), key=lambda step: -step.bit_length())
        self.group_pay = peers * self.pay
        self.piece = self.group_pay // self.pieces
        self.all_pay = self.groups * self.group_pay
        self.all_piece = self.groups * self.piece
        self.each = padded(peers * self.slots, 8)
        self.group_each = self.members * self.each
        self.partial = (self.group_each + EXTRA, 2 * self.half)

    def order(self):
        shape = (self.group_each, self.group_pay)
        row = lax.broadcasted_iota(I32, (self.group_each, 1), 0)
        expert, rest = divided(row, self.each)
        step, slot = divided(rest, self.slots)
        target = jnp.where(step < self.peers, step * self.pay + expert * self.slots + slot, -1)
        return one_hot(lax.broadcasted_iota(I32, shape, 1) == target).astype(BF16)


def line_up(z, ref):
    total = None
    for batch in range(z.micro):
        shape = (z.tok, z.rows)
        place = lax.broadcasted_iota(I32, shape, 1) == lax.broadcasted_iota(I32, shape, 0) + batch * z.tok
        value = dot(ref[batch].astype(F32).astype(BF16), one_hot(place).astype(BF16))
        total = value if total is None else total + value
    return total


def slot_hits(z, routes_ref):
    row = lax.broadcasted_iota(I32, (z.all_pay, 1), 0)
    step, rest = divided(row, z.groups * z.pay)
    group, place = divided(rest, z.pay)
    member, inside = divided(place, z.slots)
    batch, rank = divided(inside, CAP)
    rank = jnp.where(member < z.members, rank, -1)
    owner = step ^ lax.axis_index("expert") if z.pieces > 1 else step
    if z.units_dev >= FFE:
        expert = owner * z.local + group * z.members + member
    else:
        expert = lax.shift_right_logical(owner, (FFE // z.units_dev).bit_length() - 1)
    routes = line_up(z, routes_ref)
    token = lax.broadcasted_iota(I32, (z.all_pay, z.rows), 1)
    start = batch * z.tok
    same = (token >= start) & (token < start + z.tok)
    expert = expert.astype(F32)
    first = (routes[0:1, :] == expert) & same
    second = (routes[1:2, :] == expert) & same
    chosen = one_hot(first | second)
    shape = (z.rows, z.rows)
    before = lax.broadcasted_iota(I32, shape, 0) < lax.broadcasted_iota(I32, shape, 1)
    count = dot(chosen.astype(BF16), one_hot(before).astype(BF16))
    hits = jnp.where(count == rank.astype(F32), chosen, F32(0.0))
    return hits, first, second


def send_rows(z, hits, rows, outs, steps):
    hits = [hits[step * z.all_piece:(step + 1) * z.all_piece] for step in steps]
    value = dot(jnp.concatenate(hits, axis=0).astype(BF16), rows)
    for index, out in enumerate(outs):
        out[...] = value[index * z.all_piece:(index + 1) * z.all_piece].astype(BF16)


def near_kernel(z, routes_ref, rows_ref, *outs):
    hits, _, _ = slot_hits(z, routes_ref)
    send_rows(z, hits, rows_ref[...], outs, range(z.near))


def group_rows(z, group, pieces):
    result = []
    for piece in pieces:
        value = piece[...].astype(F32)
        for step in range(z.peers // z.pieces):
            low = (step * z.groups + group) * z.pay
            result.append(value[low:low + z.pay])
    return jnp.concatenate(result, axis=0)


def pack_kernel(z, *refs):
    sources, outs = refs[:3], refs[3:-4]
    routes_ref, gates_ref, rows_ref, sems = refs[-4:]
    copies = [
        pltpu.make_async_copy(source, target, sems.at[index])
        for index, (source, target) in enumerate(zip(sources, refs[-4:-1]))
    ]
    for copy in copies:
        copy.start()
    for copy in copies:
        copy.wait()
    hits, first, second = slot_hits(z, routes_ref)
    gates = line_up(z, gates_ref)
    weight = jnp.where(first, gates[0:1, :], F32(0.0)) + jnp.where(second, gates[1:2, :], F32(0.0))
    outs[-1][...] = (hits * weight).astype(BF16)
    send_rows(z, hits, rows_ref[...], outs[:-1], range(z.pieces))


def load_kernel(z, parts, gate_up, *refs):
    outs, sems = refs[:-1], refs[-1]
    flat = gate_up.reshape(2 * z.width, z.units_dev)
    depth = 2 * z.width // parts
    copies = []
    for expert in range(z.local):
        for part in range(parts):
            rows = pl.ds(part * depth, depth)
            copies.append(
                pltpu.make_async_copy(
                    flat.at[rows, pl.ds(expert * z.units, z.units)],
                    outs[expert].at[rows],
                    sems.at[expert * parts + part],
                )
            )
    for copy in copies:
        copy.start()
    for copy in copies:
        copy.wait()


def load_down_kernel(z, down_proj, *refs):
    outs, sems = refs[:-1], refs[-1]
    copies = [
        pltpu.make_async_copy(
            down_proj.at[0, pl.ds(expert * z.units, z.units), :], outs[expert], sems.at[expert]
        )
        for expert in range(z.local)
    ]
    for copy in copies:
        copy.start()
    for copy in copies:
        copy.wait()


def split_sums(sums, lanes):
    high = sums.astype(BF16).astype(F32)
    row = lax.broadcasted_iota(I32, sums.shape, 0)
    both = jnp.where(row == 0, high, jnp.where(row == 1, sums - high, F32(0.0)))
    if both.shape[1] < lanes:
        both = jnp.concatenate([both, jnp.zeros((EXTRA, lanes - both.shape[1]), F32)], axis=1)
    return both


def up_kernel(z, group, *refs):
    weights, refs = refs[:z.members], refs[z.members:]
    received, refs = refs[:z.pieces], refs[z.pieces:]
    received = [received[z.listed.index(step)] for step in range(z.pieces)]
    own, *sent, spread, staged = refs
    rows = dot(z.order(), group_rows(z, group, received).astype(BF16))
    squares = rows * rows
    high = squares.astype(BF16)
    low = (squares - high.astype(F32)).astype(BF16)
    ones = jnp.ones((EXTRA, z.width), BF16)
    sums = dot(ones, high, ACROSS) + dot(ones, low, ACROSS)
    rows = rows.astype(BF16)
    block = 128
    shape = (block, 2 * block)
    target = lax.broadcasted_iota(I32, shape, 1) - 2 * lax.broadcasted_iota(I32, shape, 0)
    placing = [one_hot(target == side).astype(BF16) for side in range(2)]
    for piece in range(z.width // block):
        columns = slice(piece * block, (piece + 1) * block)
        gate, up = dot(rows[:, columns], placing[0]), dot(rows[:, columns], placing[1])
        for expert in range(z.members):
            here = slice(expert * z.each, (expert + 1) * z.each)
            both = jnp.concatenate([gate[here], up[here]], axis=0).astype(BF16)
            spread[expert, :, 2 * piece * block:2 * (piece + 1) * block] = both
    totals = [dot(spread[expert], weights[expert][...]) for expert in range(z.members)]
    extra = split_sums(sums, 2 * z.half)
    for side in range(2):
        columns = slice(side * z.half, (side + 1) * z.half)
        gate = jnp.concatenate([total[:z.each, columns] for total in totals], axis=0)
        up = jnp.concatenate([total[z.each:, columns] for total in totals], axis=0)
        staged[side, :z.group_each, :] = jnp.concatenate([gate, up], axis=1)
        staged[side, z.group_each:, :] = extra
    core = lax.axis_index("hidden") & 1
    own[...] = staged[core]
    rows = z.partial[0] // CUTS
    value = staged[1 - core]
    for index, out in enumerate(sent):
        out[...] = value[index * rows:(index + 1) * rows].astype(BF16)


def joined(z, refs):
    total = refs[0][...].astype(F32)
    for ref in refs[1:]:
        total = total + ref[...].astype(F32)
    products, extra = total[:z.group_each], total[z.group_each:]
    row = lax.broadcasted_iota(I32, extra.shape, 0)
    sums = jnp.sum(jnp.where(row < 2, extra, F32(0.0)), axis=0, keepdims=True)
    return products, sums


def pair_kernel(z, own, *refs):
    *other, out = refs
    products, sums = joined(z, [own[...], jnp.concatenate([ref[...].astype(F32) for ref in other], axis=0)])
    out[:z.group_each, :] = products.astype(BF16)
    sums = jnp.broadcast_to(sums, (EXTRA, 2 * z.half))
    out[z.group_each:, :] = split_sums(sums, 2 * z.half).astype(BF16)


def act_kernel(z, count, *refs):
    outs = refs[-count:]
    products, sums = joined(z, refs[:-count])
    shape = (z.group_each, z.group_each)
    diagonal = lax.broadcasted_iota(I32, shape, 0) == lax.broadcasted_iota(I32, shape, 1)
    sums = jnp.sum(jnp.where(diagonal, sums[:, :z.group_each], F32(0.0)), axis=1, keepdims=True)
    scale = lax.rsqrt(sums / D + EPS)
    gate = scale * products[:, :z.half]
    up = scale * products[:, z.half:]
    value = (gate / (F32(1.0) + jnp.exp(-gate)) * up).astype(BF16)
    rows = z.group_each // count
    for index, out in enumerate(outs):
        out[...] = value[index * rows:(index + 1) * rows]


def half_products(z, weights, units_refs, side):
    low = pl.multiple_of(side * z.half, z.half)
    units = jnp.concatenate([ref[...].astype(F32) for ref in units_refs], axis=0)
    results = []
    for expert in range(z.members):
        rows = units[expert * z.each:(expert + 1) * z.each].astype(BF16)
        results.append(dot(rows, weights[expert][pl.ds(low, z.half), :]))
    return jnp.concatenate(results, axis=0)


def own_down_kernel(z, *refs):
    weights, units_ref, out = refs[:z.members], refs[z.members:-1], refs[-1]
    out[...] = half_products(z, weights, units_ref, lax.axis_index("hidden") & 1)


def down_kernel(z, hands_on, *refs):
    weights, refs = refs[:z.members], refs[z.members:]
    units_ref, own_ref, outs = refs[:1], refs[1], refs[2:]
    if hands_on:
        outs[-1][...] = outs[0][...]
        outs = outs[1:-1]
    total = own_ref[...] + half_products(z, weights, units_ref, 1 - (lax.axis_index("hidden") & 1))
    value = dot(z.order(), total.astype(BF16), DOWN)
    low = 0
    for out in outs:
        out[...] = value[low:low + out.shape[0]].astype(BF16)
        low += out.shape[0]


def second_kernel(z, pair_ref, out):
    out[...] = pair_ref[...].astype(F32)[z.piece:].astype(BF16)


def combine_kernel(z, tick, last, weight_ref, rows_ref, kept_ref, *refs):
    count = z.groups * z.pieces
    returned, refs = [ref[...].astype(F32)[:z.piece] for ref in refs[:count]], refs[count:]
    stacked = []
    for piece in range(z.pieces):
        values = [returned[group * z.pieces + piece] for group in range(z.groups)]
        for step in range(z.peers // z.pieces):
            stacked += [value[step * z.pay:(step + 1) * z.pay] for value in values]
    stacked = jnp.concatenate(stacked, axis=0).astype(BF16)
    mixed = dot(weight_ref[...], stacked, DOWN)
    value = (rows_ref[...].astype(F32) + mixed).astype(BF16)
    if last:
        refs[0][...] = jnp.where(lax.axis_index("section") == tick, value, kept_ref[...])
        return
    routes_ref, out, outs = refs[0], refs[1], refs[2:]
    out[...] = jnp.where(lax.axis_index("section") == tick, value, kept_ref[...])
    hits, _, _ = slot_hits(z, routes_ref)
    send_rows(z, hits, value, outs, range(z.near, z.pieces))


def after_waits(waits, kernel, *refs):
    return kernel(*refs[waits:])


def call(kernel, sizes, megabytes, outs, in_specs, scratch, *args, waits=()):
    results = pl.pallas_call(
        functools.partial(after_waits, len(waits), functools.partial(kernel, *sizes)),
        out_shape=outs,
        in_specs=[VMEM] * len(waits) + in_specs,
        out_specs=[VMEM] * len(outs),
        scratch_shapes=scratch,
        compiler_params=pltpu.CompilerParams(vmem_limit_bytes=megabytes * 2**20),
    )(*waits, *args)
    return list(results)


def on_device(tokens, gate_up, down_proj, routes, gate_weights):
    sections = lax.axis_size("section")
    z = Sizes(tokens, gate_up, lax.axis_size("expert"), lax.axis_size("hidden"))
    parts = 2 if z.width % 256 == 0 else 1
    shape = jax.ShapeDtypeStruct
    pay = shape((z.piece, z.width), BF16)
    all_pay = shape((z.all_piece, z.width), BF16)
    merged = [pay, pay, shape((2 * z.piece, z.width), BF16)]
    whole = shape((z.rows, z.width), BF16)
    steps = sorted(range(z.peers), key=lambda step: -step.bit_length())

    def swap(value, step):
        pairs = [(i, i ^ step) for i in range(z.splits)]
        return lax.ppermute(value, "hidden", pairs)

    def exchanged(pieces):
        if z.pieces == 1:
            return [lax.all_to_all(pieces[0], "expert", split_axis=0, concat_axis=0, tiled=True)]
        result = list(pieces)
        for step in steps[:-1]:
            pairs = [(i, i ^ step) for i in range(z.peers)]
            result[step] = lax.ppermute(pieces[step], "expert", pairs)
        return result

    def across(value, step):
        return lax.ppermute(value, "expert", [(i, i ^ step) for i in range(z.peers)])

    def sent_back(pieces, group):
        if group >= z.pairs:
            return exchanged(pieces)
        own, near, far = pieces
        far = across(far, 2)
        second = call(second_kernel, (z,), 2, [pay], [VMEM], [], far)[0]
        return [own, across(near, 1), far, across(second, 1)]

    def within(value, step, section):
        low = section * z.peers
        pairs = [(low + i, low + (i ^ step)) for i in range(z.peers)]
        return lax.ppermute(value, ("section", "expert"), pairs)

    def relayed(pieces, kept, tick):
        hop = [(tick, tick + 1)]
        rows = lax.ppermute(kept, "section", hop)
        if z.pieces == 1:
            return rows, [lax.ppermute(exchanged(pieces)[0], "section", hop)]
        far = {}
        for step in steps:
            if step >= z.near:
                pairs = [(tick * z.peers + i, (tick + 1) * z.peers + (i ^ step)) for i in range(z.peers)]
                far[step] = lax.ppermute(pieces[step - z.near], ("section", "expert"), pairs)
        result = call(near_kernel, (z,), 4, [all_pay] * z.near, [VMEM] * 2, [], routes, rows)
        for step in range(1, z.near):
            result[step] = within(result[step], step, tick + 1)
        return rows, result + [far[step] for step in range(z.near, z.pieces)]

    def products(received, group, waits):
        own, *sent = call(
            up_kernel, (z, group), 6,
            [shape(z.partial, F32)] + [shape((z.partial[0] // CUTS, z.partial[1]), BF16)] * CUTS,
            [VMEM] * (z.members + z.pieces),
            [
                pltpu.VMEM((z.members, 2 * z.each, 2 * z.width), BF16),
                pltpu.VMEM((2,) + z.partial, F32),
            ],
            *wide[group * z.members:(group + 1) * z.members], *(received[step] for step in z.listed),
            waits=waits,
        )
        return own, [swap(value, 1) for value in sent]

    def pair_sums(own, other):
        pair = call(
            pair_kernel, (z,), 2, [shape(z.partial, BF16)], [VMEM] * (1 + CUTS), [], own, *other
        )[0]
        return [pair] + [swap(pair, step) for step in range(2, z.splits, 2)]

    def activated(pairs, waits):
        count = 1
        units = call(
            act_kernel, (z, count), 2,
            [shape((z.group_each // count, z.half), BF16)] * count, [VMEM] * len(pairs), [], *pairs, waits=waits,
        )
        return units, [swap(part, 1) for part in units]

    def down(halves, group, hand_on):
        own = call(
            own_down_kernel, (z,), 4, [shape((z.group_each, z.width), F32)],
            [VMEM] * (z.members + len(halves[0])), [], *tall[group], *halves[0],
        )[0]
        return call(
            down_kernel, (z, len(hand_on)), 4,
            (merged if group < z.pairs else [pay] * z.pieces)
            + [shape(value.shape, value.dtype) for value in hand_on],
            [VMEM] * (z.members + 1 + len(halves[1]) + len(hand_on)), [],
            *tall[group], *halves[1], own, *hand_on,
        )

    routes = routes[0].transpose(0, 2, 1)
    gates = gate_weights[0].transpose(0, 2, 1)
    rows = tokens.reshape(z.rows, z.width)
    kept = rows
    *sent, weight = call(
        pack_kernel, (z,), 3,
        [all_pay] * z.pieces + [shape((z.all_pay, z.rows), BF16)],
        [HBM] * 3,
        [
            pltpu.VMEM(routes.shape, routes.dtype),
            pltpu.VMEM(gates.shape, gates.dtype),
            pltpu.VMEM(rows.shape, rows.dtype),
            pltpu.SemaphoreType.DMA((3,)),
        ],
        *(pltpu.with_memory_space_constraint(value, pltpu.HBM) for value in (routes, gates, rows)),
    )
    received = exchanged(sent)
    gate_up = pltpu.with_memory_space_constraint(gate_up, pltpu.HBM)
    down_proj = pltpu.with_memory_space_constraint(down_proj, pltpu.HBM)
    wide = call(
        load_kernel, (z, parts), 1,
        [pltpu.VMEM((2 * z.width, z.units), BF16)] * z.local,
        [HBM], [pltpu.SemaphoreType.DMA((z.local * parts,))], gate_up, waits=[weight],
    )
    tall = call(
        load_down_kernel, (z,), 1,
        [pltpu.VMEM((z.units, z.width), BF16)] * z.local,
        [HBM], [pltpu.SemaphoreType.DMA((z.local,))], down_proj, waits=wide[-1:],
    )
    tall = [tall[group * z.members:(group + 1) * z.members] for group in range(z.groups)]
    groups = range(z.groups)
    for tick in range(sections):
        last = tick == sections - 1
        sums, returned = [], []
        for group in groups:
            own, other = products(received, group, [sums[-1][0]] if group else tall[0][:1])
            sums.append(pair_sums(own, other))
            if group == 0:
                halves = activated(sums[0], [])
        for group in groups:
            if group:
                halves = activated(sums[group], outgoing[:1])
            hand_on = [routes] if tick == 0 and group == z.groups - 1 else []
            outgoing = down(halves, group, hand_on)
            if hand_on:
                pairs = [(i + 1, i) for i in range(sections - 1)]
                following = lax.ppermute(outgoing.pop(), "section", pairs)
            returned.append(sent_back(outgoing, group))
        returned = sum(returned, [])
        kept, *sent = call(
            combine_kernel, (z, tick, last), 4,
            [whole] if last else [whole] + [all_pay] * (z.pieces - z.near),
            [VMEM] * (3 + len(returned) + (not last)), [],
            weight, rows, kept, *returned, *([] if last else [following]),
        )
        if not last:
            rows, received = relayed(sent, kept, tick)
    return kept.reshape(1, z.micro, z.tok, z.width)


def solution(mesh):
    placed = (
        P(None, "expert", "hidden"),
        P("section", "hidden", None, "expert"),
        P("section", "expert", "hidden"),
        P("section", None, "expert", None),
        P("section", None, "expert", None),
    )
    return jax.shard_map(
        on_device,
        mesh=mesh,
        in_specs=placed,
        out_specs=P("section", None, "expert", "hidden"),
        check_vma=False,
    )
```

```python
import functools

import jax
import jax.numpy as jnp
from jax import lax
from jax.experimental import pallas as pl
from jax.experimental.pallas import tpu as pltpu
from jax.sharding import PartitionSpec as P

D = 7168
FFE = 1024
CAP = 3
EPS = 1e-06
EXTRA = 16
CUTS = 2
VMEM = pl.BlockSpec(memory_space=pltpu.VMEM)
HBM = pl.BlockSpec(memory_space=pltpu.HBM)
BF16 = jnp.bfloat16
F32 = jnp.float32
I32 = jnp.int32
ACROSS = (((1,), (1,)), ((), ()))
DOWN = (((0,), (0,)), ((), ()))


def padded(count, unit):
    return -(-count // unit) * unit


def dot(a, b, dims=(((1,), (0,)), ((), ()))):
    return lax.dot_general(a, b, dims, preferred_element_type=F32)


def one_hot(mask):
    return jnp.where(mask, F32(1.0), F32(0.0))


def divided(value, divisor):
    if divisor == 1:
        return value, jnp.zeros_like(value)
    quotient = lax.shift_right_logical(value * (2**20 // divisor + 1), 20)
    return quotient, value - quotient * divisor


class Sizes:
    def __init__(self, tokens, gate_up, peers, splits):
        self.peers, self.splits = peers, splits
        self.micro, self.tok, self.width = tokens.shape
        self.rows = self.micro * self.tok
        self.units_dev = gate_up.shape[3]
        self.units = min(FFE, self.units_dev)
        self.half = self.units // 2
        self.local = self.units_dev // self.units
        self.groups = 2 if self.local % 2 == 0 else 1
        self.members = self.local // self.groups
        self.slots = self.micro * CAP
        self.pay = padded(self.members * self.slots, 8)
        self.pieces = peers if peers <= 8 else 1
        self.pairs = self.groups - 1 if self.pieces == 4 else 0
        self.near = self.pieces // 2
        self.listed = sorted(range(self.pieces), key=lambda step: -step.bit_length())
        self.group_pay = peers * self.pay
        self.piece = self.group_pay // self.pieces
        self.all_pay = self.groups * self.group_pay
        self.all_piece = self.groups * self.piece
        self.each = padded(peers * self.slots, 8)
        self.group_each = self.members * self.each
        self.partial = (self.group_each + EXTRA, 2 * self.half)

    def order(self):
        shape = (self.group_each, self.group_pay)
        row = lax.broadcasted_iota(I32, (self.group_each, 1), 0)
        expert, rest = divided(row, self.each)
        step, slot = divided(rest, self.slots)
        target = jnp.where(step < self.peers, step * self.pay + expert * self.slots + slot, -1)
        return one_hot(lax.broadcasted_iota(I32, shape, 1) == target).astype(BF16)


def line_up(z, ref):
    total = None
    for batch in range(z.micro):
        shape = (z.tok, z.rows)
        place = lax.broadcasted_iota(I32, shape, 1) == lax.broadcasted_iota(I32, shape, 0) + batch * z.tok
        value = dot(ref[batch].astype(F32).astype(BF16), one_hot(place).astype(BF16))
        total = value if total is None else total + value
    return total


def slot_hits(z, routes_ref):
    row = lax.broadcasted_iota(I32, (z.all_pay, 1), 0)
    step, rest = divided(row, z.groups * z.pay)
    group, place = divided(rest, z.pay)
    member, inside = divided(place, z.slots)
    batch, rank = divided(inside, CAP)
    rank = jnp.where(member < z.members, rank, -1)
    owner = step ^ lax.axis_index("expert") if z.pieces > 1 else step
    if z.units_dev >= FFE:
        expert = owner * z.local + group * z.members + member
    else:
        expert = lax.shift_right_logical(owner, (FFE // z.units_dev).bit_length() - 1)
    routes = line_up(z, routes_ref)
    token = lax.broadcasted_iota(I32, (z.all_pay, z.rows), 1)
    start = batch * z.tok
    same = (token >= start) & (token < start + z.tok)
    expert = expert.astype(F32)
    first = (routes[0:1, :] == expert) & same
    second = (routes[1:2, :] == expert) & same
    chosen = one_hot(first | second)
    shape = (z.rows, z.rows)
    before = lax.broadcasted_iota(I32, shape, 0) < lax.broadcasted_iota(I32, shape, 1)
    count = dot(chosen.astype(BF16), one_hot(before).astype(BF16))
    hits = jnp.where(count == rank.astype(F32), chosen, F32(0.0))
    return hits, first, second


def send_rows(z, hits, rows, outs, steps):
    hits = [hits[step * z.all_piece:(step + 1) * z.all_piece] for step in steps]
    value = dot(jnp.concatenate(hits, axis=0).astype(BF16), rows)
    for index, out in enumerate(outs):
        out[...] = value[index * z.all_piece:(index + 1) * z.all_piece].astype(BF16)


def near_kernel(z, routes_ref, rows_ref, *outs):
    hits, _, _ = slot_hits(z, routes_ref)
    send_rows(z, hits, rows_ref[...], outs, range(z.near))


def group_rows(z, group, pieces):
    result = []
    for piece in pieces:
        value = piece[...].astype(F32)
        for step in range(z.peers // z.pieces):
            low = (step * z.groups + group) * z.pay
            result.append(value[low:low + z.pay])
    return jnp.concatenate(result, axis=0)


def pack_kernel(z, *refs):
    sources, outs = refs[:3], refs[3:-4]
    routes_ref, gates_ref, rows_ref, sems = refs[-4:]
    copies = [
        pltpu.make_async_copy(source, target, sems.at[index])
        for index, (source, target) in enumerate(zip(sources, refs[-4:-1]))
    ]
    for copy in copies:
        copy.start()
    copies[0].wait()
    hits, first, second = slot_hits(z, routes_ref)
    copies[1].wait()
    gates = line_up(z, gates_ref)
    weight = jnp.where(first, gates[0:1, :], F32(0.0)) + jnp.where(second, gates[1:2, :], F32(0.0))
    outs[-1][...] = (hits * weight).astype(BF16)
    copies[2].wait()
    send_rows(z, hits, rows_ref[...], outs[:-1], range(z.pieces))


def load_kernel(z, parts, gate_up, *refs):
    outs, sems = refs[:-1], refs[-1]
    flat = gate_up.reshape(2 * z.width, z.units_dev)
    depth = 2 * z.width // parts
    copies = []
    for expert in range(z.local):
        for part in range(parts):
            rows = pl.ds(part * depth, depth)
            copies.append(
                pltpu.make_async_copy(
                    flat.at[rows, pl.ds(expert * z.units, z.units)],
                    outs[expert].at[rows],
                    sems.at[expert * parts + part],
                )
            )
    for copy in copies:
        copy.start()
    for copy in copies:
        copy.wait()


def load_down_kernel(z, down_proj, *refs):
    outs, sems = refs[:-1], refs[-1]
    copies = [
        pltpu.make_async_copy(
            down_proj.at[0, pl.ds(expert * z.units, z.units), :], outs[expert], sems.at[expert]
        )
        for expert in range(z.local)
    ]
    for copy in copies:
        copy.start()
    for copy in copies:
        copy.wait()


def split_sums(sums, lanes):
    high = sums.astype(BF16).astype(F32)
    row = lax.broadcasted_iota(I32, sums.shape, 0)
    both = jnp.where(row == 0, high, jnp.where(row == 1, sums - high, F32(0.0)))
    if both.shape[1] < lanes:
        both = jnp.concatenate([both, jnp.zeros((EXTRA, lanes - both.shape[1]), F32)], axis=1)
    return both


def up_kernel(z, group, *refs):
    weights, refs = refs[:z.members], refs[z.members:]
    received, refs = refs[:z.pieces], refs[z.pieces:]
    received = [received[z.listed.index(step)] for step in range(z.pieces)]
    own, *sent, spread, staged = refs
    rows = dot(z.order(), group_rows(z, group, received).astype(BF16))
    squares = rows * rows
    high = squares.astype(BF16)
    low = (squares - high.astype(F32)).astype(BF16)
    ones = jnp.ones((EXTRA, z.width), BF16)
    sums = dot(ones, high, ACROSS) + dot(ones, low, ACROSS)
    rows = rows.astype(BF16)
    block = 128
    shape = (block, 2 * block)
    target = lax.broadcasted_iota(I32, shape, 1) - 2 * lax.broadcasted_iota(I32, shape, 0)
    placing = [one_hot(target == side).astype(BF16) for side in range(2)]
    for piece in range(z.width // block):
        columns = slice(piece * block, (piece + 1) * block)
        gate, up = dot(rows[:, columns], placing[0]), dot(rows[:, columns], placing[1])
        for expert in range(z.members):
            here = slice(expert * z.each, (expert + 1) * z.each)
            both = jnp.concatenate([gate[here], up[here]], axis=0).astype(BF16)
            spread[expert, :, 2 * piece * block:2 * (piece + 1) * block] = both
    totals = [dot(spread[expert], weights[expert][...]) for expert in range(z.members)]
    extra = split_sums(sums, 2 * z.half)
    for side in range(2):
        columns = slice(side * z.half, (side + 1) * z.half)
        gate = jnp.concatenate([total[:z.each, columns] for total in totals], axis=0)
        up = jnp.concatenate([total[z.each:, columns] for total in totals], axis=0)
        staged[side, :z.group_each, :] = jnp.concatenate([gate, up], axis=1)
        staged[side, z.group_each:, :] = extra
    core = lax.axis_index("hidden") & 1
    own[...] = staged[core]
    rows = z.partial[0] // CUTS
    value = staged[1 - core]
    for index, out in enumerate(sent):
        out[...] = value[index * rows:(index + 1) * rows].astype(BF16)


def joined(z, refs):
    total = refs[0][...].astype(F32)
    for ref in refs[1:]:
        total = total + ref[...].astype(F32)
    products, extra = total[:z.group_each], total[z.group_each:]
    row = lax.broadcasted_iota(I32, extra.shape, 0)
    sums = jnp.sum(jnp.where(row < 2, extra, F32(0.0)), axis=0, keepdims=True)
    return products, sums


def pair_kernel(z, own, *refs):
    *other, out = refs
    products, sums = joined(z, [own[...], jnp.concatenate([ref[...].astype(F32) for ref in other], axis=0)])
    out[:z.group_each, :] = products.astype(BF16)
    sums = jnp.broadcast_to(sums, (EXTRA, 2 * z.half))
    out[z.group_each:, :] = split_sums(sums, 2 * z.half).astype(BF16)


def act_kernel(z, count, *refs):
    outs = refs[-count:]
    products, sums = joined(z, refs[:-count])
    shape = (z.group_each, z.group_each)
    diagonal = lax.broadcasted_iota(I32, shape, 0) == lax.broadcasted_iota(I32, shape, 1)
    sums = jnp.sum(jnp.where(diagonal, sums[:, :z.group_each], F32(0.0)), axis=1, keepdims=True)
    scale = lax.rsqrt(sums / D + EPS)
    gate = scale * products[:, :z.half]
    up = scale * products[:, z.half:]
    value = (gate / (F32(1.0) + jnp.exp(-gate)) * up).astype(BF16)
    rows = z.group_each // count
    for index, out in enumerate(outs):
        out[...] = value[index * rows:(index + 1) * rows]


def half_products(z, weights, units_refs, side):
    low = pl.multiple_of(side * z.half, z.half)
    units = jnp.concatenate([ref[...].astype(F32) for ref in units_refs], axis=0)
    results = []
    for expert in range(z.members):
        rows = units[expert * z.each:(expert + 1) * z.each].astype(BF16)
        results.append(dot(rows, weights[expert][pl.ds(low, z.half), :]))
    return jnp.concatenate(results, axis=0)


def own_down_kernel(z, *refs):
    weights, units_ref, out = refs[:z.members], refs[z.members:-1], refs[-1]
    out[...] = half_products(z, weights, units_ref, lax.axis_index("hidden") & 1)


def down_kernel(z, hands_on, *refs):
    weights, refs = refs[:z.members], refs[z.members:]
    units_ref, own_ref, outs = refs[:1], refs[1], refs[2:]
    if hands_on:
        outs[-1][...] = outs[0][...]
        outs = outs[1:-1]
    total = own_ref[...] + half_products(z, weights, units_ref, 1 - (lax.axis_index("hidden") & 1))
    value = dot(z.order(), total.astype(BF16), DOWN)
    low = 0
    for out in outs:
        out[...] = value[low:low + out.shape[0]].astype(BF16)
        low += out.shape[0]


def hand_on_kernel(source, target):
    target[...] = source[...]


def second_kernel(z, pair_ref, out):
    out[...] = pair_ref[...].astype(F32)[z.piece:].astype(BF16)


def combine_kernel(z, tick, last, weight_ref, rows_ref, kept_ref, *refs):
    count = z.groups * z.pieces
    returned, refs = [ref[...].astype(F32)[:z.piece] for ref in refs[:count]], refs[count:]
    stacked = []
    for piece in range(z.pieces):
        values = [returned[group * z.pieces + piece] for group in range(z.groups)]
        for step in range(z.peers // z.pieces):
            stacked += [value[step * z.pay:(step + 1) * z.pay] for value in values]
    stacked = jnp.concatenate(stacked, axis=0).astype(BF16)
    mixed = dot(weight_ref[...], stacked, DOWN)
    value = (rows_ref[...].astype(F32) + mixed).astype(BF16)
    if last:
        refs[0][...] = jnp.where(lax.axis_index("section") == tick, value, kept_ref[...])
        return
    routes_ref, out, outs = refs[0], refs[1], refs[2:]
    out[...] = jnp.where(lax.axis_index("section") == tick, value, kept_ref[...])
    hits, _, _ = slot_hits(z, routes_ref)
    send_rows(z, hits, value, outs, range(z.near, z.pieces))


def after_waits(waits, kernel, *refs):
    return kernel(*refs[waits:])


def call(kernel, sizes, megabytes, outs, in_specs, scratch, *args, waits=()):
    results = pl.pallas_call(
        functools.partial(after_waits, len(waits), functools.partial(kernel, *sizes)),
        out_shape=outs,
        in_specs=[VMEM] * len(waits) + in_specs,
        out_specs=[VMEM] * len(outs),
        scratch_shapes=scratch,
        compiler_params=pltpu.CompilerParams(vmem_limit_bytes=megabytes * 2**20),
    )(*waits, *args)
    return list(results)


def on_device(tokens, gate_up, down_proj, routes, gate_weights):
    sections = lax.axis_size("section")
    z = Sizes(tokens, gate_up, lax.axis_size("expert"), lax.axis_size("hidden"))
    parts = 2 if z.width % 256 == 0 else 1
    shape = jax.ShapeDtypeStruct
    pay = shape((z.piece, z.width), BF16)
    all_pay = shape((z.all_piece, z.width), BF16)
    merged = [pay, pay, shape((2 * z.piece, z.width), BF16)]
    whole = shape((z.rows, z.width), BF16)
    steps = sorted(range(z.peers), key=lambda step: -step.bit_length())

    def swap(value, step):
        pairs = [(i, i ^ step) for i in range(z.splits)]
        return lax.ppermute(value, "hidden", pairs)

    def exchanged(pieces):
        if z.pieces == 1:
            return [lax.all_to_all(pieces[0], "expert", split_axis=0, concat_axis=0, tiled=True)]
        result = list(pieces)
        for step in steps[:-1]:
            pairs = [(i, i ^ step) for i in range(z.peers)]
            result[step] = lax.ppermute(pieces[step], "expert", pairs)
        return result

    def across(value, step):
        return lax.ppermute(value, "expert", [(i, i ^ step) for i in range(z.peers)])

    def sent_back(pieces, group):
        if group >= z.pairs:
            return exchanged(pieces)
        own, near, far = pieces
        far = across(far, 2)
        second = call(second_kernel, (z,), 2, [pay], [VMEM], [], far)[0]
        return [own, across(near, 1), far, across(second, 1)]

    def within(value, step, section):
        low = section * z.peers
        pairs = [(low + i, low + (i ^ step)) for i in range(z.peers)]
        return lax.ppermute(value, ("section", "expert"), pairs)

    def relayed(pieces, kept, tick):
        hop = [(tick, tick + 1)]
        rows = lax.ppermute(kept, "section", hop)
        if z.pieces == 1:
            return rows, [lax.ppermute(exchanged(pieces)[0], "section", hop)]
        far = {}
        for step in steps:
            if step == z.near:
                pairs = [(tick * z.peers + i, (tick + 1) * z.peers + (i ^ step)) for i in range(z.peers)]
                far[step] = lax.ppermute(pieces[0], ("section", "expert"), pairs)
            elif step > z.near:
                far[step] = within(pieces[step - z.near], step, tick)
        result = call(near_kernel, (z,), 4, [all_pay] * z.near, [VMEM] * 2, [], routes, rows)
        for step in range(z.near + 1, z.pieces):
            block = call(hand_on_kernel, (), 2, [all_pay], [VMEM], [], far[step], waits=result[:1])[0]
            far[step] = lax.ppermute(block, "section", hop)
        for step in range(1, z.near):
            result[step] = within(result[step], step, tick + 1)
        return rows, result + [far[step] for step in range(z.near, z.pieces)]

    def products(received, group, waits):
        own, *sent = call(
            up_kernel, (z, group), 6,
            [shape(z.partial, F32)] + [shape((z.partial[0] // CUTS, z.partial[1]), BF16)] * CUTS,
            [VMEM] * (z.members + z.pieces),
            [
                pltpu.VMEM((z.members, 2 * z.each, 2 * z.width), BF16),
                pltpu.VMEM((2,) + z.partial, F32),
            ],
            *wide[group * z.members:(group + 1) * z.members], *(received[step] for step in z.listed),
            waits=waits,
        )
        return own, [swap(value, 1) for value in sent]

    def pair_sums(own, other):
        pair = call(
            pair_kernel, (z,), 2, [shape(z.partial, BF16)], [VMEM] * (1 + CUTS), [], own, *other
        )[0]
        return [pair] + [swap(pair, step) for step in range(2, z.splits, 2)]

    def activated(pairs, waits):
        count = 1
        units = call(
            act_kernel, (z, count), 2,
            [shape((z.group_each // count, z.half), BF16)] * count, [VMEM] * len(pairs), [], *pairs, waits=waits,
        )
        return units, [swap(part, 1) for part in units]

    def down(halves, group, hand_on):
        own = call(
            own_down_kernel, (z,), 4, [shape((z.group_each, z.width), F32)],
            [VMEM] * (z.members + len(halves[0])), [], *tall[group], *halves[0],
        )[0]
        return call(
            down_kernel, (z, len(hand_on)), 4,
            (merged if group < z.pairs else [pay] * z.pieces)
            + [shape(value.shape, value.dtype) for value in hand_on],
            [VMEM] * (z.members + 1 + len(halves[1]) + len(hand_on)), [],
            *tall[group], *halves[1], own, *hand_on,
        )

    routes = routes[0].transpose(0, 2, 1)
    gates = gate_weights[0].transpose(0, 2, 1)
    rows = tokens.reshape(z.rows, z.width)
    kept = rows
    *sent, weight = call(
        pack_kernel, (z,), 3,
        [all_pay] * z.pieces + [shape((z.all_pay, z.rows), BF16)],
        [HBM] * 3,
        [
            pltpu.VMEM(routes.shape, routes.dtype),
            pltpu.VMEM(gates.shape, gates.dtype),
            pltpu.VMEM(rows.shape, rows.dtype),
            pltpu.SemaphoreType.DMA((3,)),
        ],
        *(pltpu.with_memory_space_constraint(value, pltpu.HBM) for value in (routes, gates, rows)),
    )
    received = exchanged(sent)
    gate_up = pltpu.with_memory_space_constraint(gate_up, pltpu.HBM)
    down_proj = pltpu.with_memory_space_constraint(down_proj, pltpu.HBM)
    wide = call(
        load_kernel, (z, parts), 1,
        [pltpu.VMEM((2 * z.width, z.units), BF16)] * z.local,
        [HBM], [pltpu.SemaphoreType.DMA((z.local * parts,))], gate_up, waits=[weight],
    )
    tall = call(
        load_down_kernel, (z,), 1,
        [pltpu.VMEM((z.units, z.width), BF16)] * z.local,
        [HBM], [pltpu.SemaphoreType.DMA((z.local,))], down_proj, waits=wide[-1:],
    )
    tall = [tall[group * z.members:(group + 1) * z.members] for group in range(z.groups)]
    groups = range(z.groups)
    for tick in range(sections):
        last = tick == sections - 1
        sums, returned = [], []
        for group in groups:
            own, other = products(received, group, [sums[-1][0]] if group else tall[0][:1])
            sums.append(pair_sums(own, other))
            if group == 0:
                halves = activated(sums[0], [])
        for group in groups:
            if group:
                halves = activated(sums[group], outgoing[:1])
            hand_on = [routes] if tick == 0 and group == z.groups - 1 else []
            outgoing = down(halves, group, hand_on)
            if hand_on:
                pairs = [(i + 1, i) for i in range(sections - 1)]
                following = lax.ppermute(outgoing.pop(), "section", pairs)
            returned.append(sent_back(outgoing, group))
        returned = sum(returned, [])
        kept, *sent = call(
            combine_kernel, (z, tick, last), 4,
            [whole] if last else [whole] + [all_pay] * (z.pieces - z.near),
            [VMEM] * (3 + len(returned) + (not last)), [],
            weight, rows, kept, *returned, *([] if last else [following]),
        )
        if not last:
            rows, received = relayed(sent, kept, tick)
    return kept.reshape(1, z.micro, z.tok, z.width)


def solution(mesh):
    placed = (
        P(None, "expert", "hidden"),
        P("section", "hidden", None, "expert"),
        P("section", "expert", "hidden"),
        P("section", None, "expert", None),
        P("section", None, "expert", None),
    )
    return jax.shard_map(
        on_device,
        mesh=mesh,
        in_specs=placed,
        out_specs=P("section", None, "expert", "hidden"),
        check_vma=False,
    )
```

```python
import functools

import jax
import jax.numpy as jnp
from jax import lax
from jax.experimental import pallas as pl
from jax.experimental.pallas import tpu as pltpu
from jax.sharding import PartitionSpec as P

D = 7168
FFE = 1024
CAP = 3
EPS = 1e-06
EXTRA = 16
CUTS = 2
VMEM = pl.BlockSpec(memory_space=pltpu.VMEM)
HBM = pl.BlockSpec(memory_space=pltpu.HBM)
BF16 = jnp.bfloat16
F32 = jnp.float32
I32 = jnp.int32
ACROSS = (((1,), (1,)), ((), ()))
DOWN = (((0,), (0,)), ((), ()))


def padded(count, unit):
    return -(-count // unit) * unit


def dot(a, b, dims=(((1,), (0,)), ((), ()))):
    return lax.dot_general(a, b, dims, preferred_element_type=F32)


def one_hot(mask):
    return jnp.where(mask, F32(1.0), F32(0.0))


def divided(value, divisor):
    if divisor == 1:
        return value, jnp.zeros_like(value)
    quotient = lax.shift_right_logical(value * (2**20 // divisor + 1), 20)
    return quotient, value - quotient * divisor


class Sizes:
    def __init__(self, tokens, gate_up, peers, splits):
        self.peers, self.splits = peers, splits
        self.micro, self.tok, self.width = tokens.shape
        self.rows = self.micro * self.tok
        self.units_dev = gate_up.shape[3]
        self.units = min(FFE, self.units_dev)
        self.half = self.units // 2
        self.local = self.units_dev // self.units
        self.groups = 2 if self.local % 2 == 0 else 1
        self.members = self.local // self.groups
        self.slots = self.micro * CAP
        self.pay = padded(self.members * self.slots, 8)
        self.pieces = peers if peers <= 8 else 1
        self.pairs = self.groups - 1 if self.pieces == 4 else 0
        self.near = self.pieces // 2
        self.listed = sorted(range(self.pieces), key=lambda step: -step.bit_length())
        self.group_pay = peers * self.pay
        self.piece = self.group_pay // self.pieces
        self.all_pay = self.groups * self.group_pay
        self.all_piece = self.groups * self.piece
        self.each = padded(peers * self.slots, 8)
        self.group_each = self.members * self.each
        self.partial = (self.group_each + EXTRA, 2 * self.half)

    def order(self):
        shape = (self.group_each, self.group_pay)
        row = lax.broadcasted_iota(I32, (self.group_each, 1), 0)
        expert, rest = divided(row, self.each)
        step, slot = divided(rest, self.slots)
        target = jnp.where(step < self.peers, step * self.pay + expert * self.slots + slot, -1)
        return one_hot(lax.broadcasted_iota(I32, shape, 1) == target).astype(BF16)


def line_up(z, ref):
    total = None
    for batch in range(z.micro):
        shape = (z.tok, z.rows)
        place = lax.broadcasted_iota(I32, shape, 1) == lax.broadcasted_iota(I32, shape, 0) + batch * z.tok
        value = dot(ref[batch].astype(F32).astype(BF16), one_hot(place).astype(BF16))
        total = value if total is None else total + value
    return total


def slot_hits(z, routes_ref):
    row = lax.broadcasted_iota(I32, (z.all_pay, 1), 0)
    step, rest = divided(row, z.groups * z.pay)
    group, place = divided(rest, z.pay)
    member, inside = divided(place, z.slots)
    batch, rank = divided(inside, CAP)
    rank = jnp.where(member < z.members, rank, -1)
    owner = step ^ lax.axis_index("expert") if z.pieces > 1 else step
    if z.units_dev >= FFE:
        expert = owner * z.local + group * z.members + member
    else:
        expert = lax.shift_right_logical(owner, (FFE // z.units_dev).bit_length() - 1)
    routes = line_up(z, routes_ref)
    token = lax.broadcasted_iota(I32, (z.all_pay, z.rows), 1)
    start = batch * z.tok
    same = (token >= start) & (token < start + z.tok)
    expert = expert.astype(F32)
    first = (routes[0:1, :] == expert) & same
    second = (routes[1:2, :] == expert) & same
    chosen = one_hot(first | second)
    shape = (z.rows, z.rows)
    before = lax.broadcasted_iota(I32, shape, 0) < lax.broadcasted_iota(I32, shape, 1)
    count = dot(chosen.astype(BF16), one_hot(before).astype(BF16))
    hits = jnp.where(count == rank.astype(F32), chosen, F32(0.0))
    return hits, first, second


def send_rows(z, hits, rows, outs, steps):
    hits = [hits[step * z.all_piece:(step + 1) * z.all_piece] for step in steps]
    value = dot(jnp.concatenate(hits, axis=0).astype(BF16), rows)
    for index, out in enumerate(outs):
        out[...] = value[index * z.all_piece:(index + 1) * z.all_piece].astype(BF16)


def near_kernel(z, routes_ref, rows_ref, *outs):
    hits, _, _ = slot_hits(z, routes_ref)
    send_rows(z, hits, rows_ref[...], outs, range(z.near))


def group_rows(z, group, pieces):
    result = []
    for piece in pieces:
        value = piece[...].astype(F32)
        for step in range(z.peers // z.pieces):
            low = (step * z.groups + group) * z.pay
            result.append(value[low:low + z.pay])
    return jnp.concatenate(result, axis=0)


def pack_kernel(z, *refs):
    sources, outs = refs[:3], refs[3:-4]
    routes_ref, gates_ref, rows_ref, sems = refs[-4:]
    copies = [
        pltpu.make_async_copy(source, target, sems.at[index])
        for index, (source, target) in enumerate(zip(sources, refs[-4:-1]))
    ]
    for copy in copies:
        copy.start()
    copies[0].wait()
    hits, first, second = slot_hits(z, routes_ref)
    copies[1].wait()
    gates = line_up(z, gates_ref)
    weight = jnp.where(first, gates[0:1, :], F32(0.0)) + jnp.where(second, gates[1:2, :], F32(0.0))
    outs[-1][...] = (hits * weight).astype(BF16)
    copies[2].wait()
    send_rows(z, hits, rows_ref[...], outs[:-1], range(z.pieces))


def load_kernel(z, parts, gate_up, *refs):
    outs, sems = refs[:-1], refs[-1]
    flat = gate_up.reshape(2 * z.width, z.units_dev)
    depth = 2 * z.width // parts
    copies = []
    for expert in range(z.local):
        for part in range(parts):
            rows = pl.ds(part * depth, depth)
            copies.append(
                pltpu.make_async_copy(
                    flat.at[rows, pl.ds(expert * z.units, z.units)],
                    outs[expert].at[rows],
                    sems.at[expert * parts + part],
                )
            )
    for copy in copies:
        copy.start()
    for copy in copies:
        copy.wait()


def load_down_kernel(z, group, down_proj, *refs):
    outs, sems = refs[:-1], refs[-1]
    copies = []
    for index in range(z.members):
        rows = pl.ds((group * z.members + index) * z.units, z.units)
        copies.append(pltpu.make_async_copy(down_proj.at[0, rows, :], outs[index], sems.at[index]))
    for copy in copies:
        copy.start()
    for copy in copies:
        copy.wait()


def split_sums(sums, lanes):
    high = sums.astype(BF16).astype(F32)
    row = lax.broadcasted_iota(I32, sums.shape, 0)
    both = jnp.where(row == 0, high, jnp.where(row == 1, sums - high, F32(0.0)))
    if both.shape[1] < lanes:
        both = jnp.concatenate([both, jnp.zeros((EXTRA, lanes - both.shape[1]), F32)], axis=1)
    return both


def up_kernel(z, group, *refs):
    weights, refs = refs[:z.members], refs[z.members:]
    received, refs = refs[:z.pieces], refs[z.pieces:]
    received = [received[z.listed.index(step)] for step in range(z.pieces)]
    own, *sent, spread, staged = refs
    rows = dot(z.order(), group_rows(z, group, received).astype(BF16))
    squares = rows * rows
    high = squares.astype(BF16)
    low = (squares - high.astype(F32)).astype(BF16)
    ones = jnp.ones((EXTRA, z.width), BF16)
    sums = dot(ones, high, ACROSS) + dot(ones, low, ACROSS)
    rows = rows.astype(BF16)
    block = 128
    shape = (block, 2 * block)
    target = lax.broadcasted_iota(I32, shape, 1) - 2 * lax.broadcasted_iota(I32, shape, 0)
    placing = [one_hot(target == side).astype(BF16) for side in range(2)]
    for piece in range(z.width // block):
        columns = slice(piece * block, (piece + 1) * block)
        gate, up = dot(rows[:, columns], placing[0]), dot(rows[:, columns], placing[1])
        for expert in range(z.members):
            here = slice(expert * z.each, (expert + 1) * z.each)
            both = jnp.concatenate([gate[here], up[here]], axis=0).astype(BF16)
            spread[expert, :, 2 * piece * block:2 * (piece + 1) * block] = both
    totals = [dot(spread[expert], weights[expert][...]) for expert in range(z.members)]
    extra = split_sums(sums, 2 * z.half)
    for side in range(2):
        columns = slice(side * z.half, (side + 1) * z.half)
        gate = jnp.concatenate([total[:z.each, columns] for total in totals], axis=0)
        up = jnp.concatenate([total[z.each:, columns] for total in totals], axis=0)
        staged[side, :z.group_each, :] = jnp.concatenate([gate, up], axis=1)
        staged[side, z.group_each:, :] = extra
    core = lax.axis_index("hidden") & 1
    own[...] = staged[core]
    rows = z.partial[0] // CUTS
    value = staged[1 - core]
    for index, out in enumerate(sent):
        out[...] = value[index * rows:(index + 1) * rows].astype(BF16)


def joined(z, refs):
    total = refs[0][...].astype(F32)
    for ref in refs[1:]:
        total = total + ref[...].astype(F32)
    products, extra = total[:z.group_each], total[z.group_each:]
    row = lax.broadcasted_iota(I32, extra.shape, 0)
    sums = jnp.sum(jnp.where(row < 2, extra, F32(0.0)), axis=0, keepdims=True)
    return products, sums


def pair_kernel(z, own, *refs):
    *other, out = refs
    products, sums = joined(z, [own[...], jnp.concatenate([ref[...].astype(F32) for ref in other], axis=0)])
    sums = split_sums(jnp.broadcast_to(sums, (EXTRA, 2 * z.half)), 2 * z.half)
    out[...] = jnp.concatenate([products, sums], axis=0).astype(BF16)


def act_kernel(z, count, *refs):
    outs = refs[-count:]
    products, sums = joined(z, refs[:-count])
    shape = (z.group_each, z.group_each)
    diagonal = lax.broadcasted_iota(I32, shape, 0) == lax.broadcasted_iota(I32, shape, 1)
    sums = jnp.sum(jnp.where(diagonal, sums[:, :z.group_each], F32(0.0)), axis=1, keepdims=True)
    scale = lax.rsqrt(sums / D + EPS)
    gate = scale * products[:, :z.half]
    up = scale * products[:, z.half:]
    value = (gate / (F32(1.0) + jnp.exp(-gate)) * up).astype(BF16)
    rows = z.group_each // count
    for index, out in enumerate(outs):
        out[...] = value[index * rows:(index + 1) * rows]


def half_products(z, weights, units_refs, side):
    low = pl.multiple_of(side * z.half, z.half)
    units = jnp.concatenate([ref[...].astype(F32) for ref in units_refs], axis=0)
    results = []
    for expert in range(z.members):
        rows = units[expert * z.each:(expert + 1) * z.each].astype(BF16)
        results.append(dot(rows, weights[expert][pl.ds(low, z.half), :]))
    return jnp.concatenate(results, axis=0)


def own_down_kernel(z, *refs):
    weights, units_ref, out = refs[:z.members], refs[z.members:-1], refs[-1]
    out[...] = half_products(z, weights, units_ref, lax.axis_index("hidden") & 1)


def down_kernel(z, hands_on, *refs):
    weights, refs = refs[:z.members], refs[z.members:]
    units_ref, own_ref, outs = refs[:1], refs[1], refs[2:]
    if hands_on:
        outs[-1][...] = outs[0][...]
        outs = outs[1:-1]
    total = own_ref[...] + half_products(z, weights, units_ref, 1 - (lax.axis_index("hidden") & 1))
    value = dot(z.order(), total.astype(BF16), DOWN)
    low = 0
    for out in outs:
        out[...] = value[low:low + out.shape[0]].astype(BF16)
        low += out.shape[0]


def second_kernel(z, pair_ref, out):
    out[...] = pair_ref[...].astype(F32)[z.piece:].astype(BF16)


def combine_kernel(z, tick, last, weight_ref, rows_ref, kept_ref, *refs):
    count = z.groups * z.pieces
    returned, refs = [ref[...].astype(F32)[:z.piece] for ref in refs[:count]], refs[count:]
    stacked = []
    for piece in range(z.pieces):
        values = [returned[group * z.pieces + piece] for group in range(z.groups)]
        for step in range(z.peers // z.pieces):
            stacked += [value[step * z.pay:(step + 1) * z.pay] for value in values]
    stacked = jnp.concatenate(stacked, axis=0).astype(BF16)
    mixed = dot(weight_ref[...], stacked, DOWN)
    value = (rows_ref[...].astype(F32) + mixed).astype(BF16)
    if last:
        refs[0][...] = jnp.where(lax.axis_index("section") == tick, value, kept_ref[...])
        return
    routes_ref, out, outs = refs[0], refs[1], refs[2:]
    out[...] = jnp.where(lax.axis_index("section") == tick, value, kept_ref[...])
    hits, _, _ = slot_hits(z, routes_ref)
    send_rows(z, hits, value, outs, range(z.near, z.pieces))


def after_waits(waits, kernel, *refs):
    return kernel(*refs[waits:])


def call(kernel, sizes, megabytes, outs, in_specs, scratch, *args, waits=()):
    results = pl.pallas_call(
        functools.partial(after_waits, len(waits), functools.partial(kernel, *sizes)),
        out_shape=outs,
        in_specs=[VMEM] * len(waits) + in_specs,
        out_specs=[VMEM] * len(outs),
        scratch_shapes=scratch,
        compiler_params=pltpu.CompilerParams(vmem_limit_bytes=megabytes * 2**20),
    )(*waits, *args)
    return list(results)


def on_device(tokens, gate_up, down_proj, routes, gate_weights):
    sections = lax.axis_size("section")
    z = Sizes(tokens, gate_up, lax.axis_size("expert"), lax.axis_size("hidden"))
    parts = 2 if z.width % 256 == 0 else 1
    shape = jax.ShapeDtypeStruct
    pay = shape((z.piece, z.width), BF16)
    all_pay = shape((z.all_piece, z.width), BF16)
    merged = [pay, pay, shape((2 * z.piece, z.width), BF16)]
    whole = shape((z.rows, z.width), BF16)
    steps = sorted(range(z.peers), key=lambda step: -step.bit_length())

    def swap(value, step):
        pairs = [(i, i ^ step) for i in range(z.splits)]
        return lax.ppermute(value, "hidden", pairs)

    def exchanged(pieces):
        if z.pieces == 1:
            return [lax.all_to_all(pieces[0], "expert", split_axis=0, concat_axis=0, tiled=True)]
        result = list(pieces)
        for step in steps[:-1]:
            pairs = [(i, i ^ step) for i in range(z.peers)]
            result[step] = lax.ppermute(pieces[step], "expert", pairs)
        return result

    def across(value, step):
        return lax.ppermute(value, "expert", [(i, i ^ step) for i in range(z.peers)])

    def sent_back(pieces, group):
        if group >= z.pairs:
            return exchanged(pieces)
        own, near, far = pieces
        far = across(far, 2)
        second = call(second_kernel, (z,), 2, [pay], [VMEM], [], far)[0]
        return [own, across(near, 1), far, across(second, 1)]

    def within(value, step, section):
        low = section * z.peers
        pairs = [(low + i, low + (i ^ step)) for i in range(z.peers)]
        return lax.ppermute(value, ("section", "expert"), pairs)

    def relayed(pieces, kept, tick):
        hop = [(tick, tick + 1)]
        rows = lax.ppermute(kept, "section", hop)
        if z.pieces == 1:
            return rows, [lax.ppermute(exchanged(pieces)[0], "section", hop)]
        far = {}
        for step in steps:
            if step >= z.near:
                pairs = [(tick * z.peers + i, (tick + 1) * z.peers + (i ^ step)) for i in range(z.peers)]
                far[step] = lax.ppermute(pieces[step - z.near], ("section", "expert"), pairs)
        result = call(near_kernel, (z,), 4, [all_pay] * z.near, [VMEM] * 2, [], routes, rows)
        for step in range(1, z.near):
            result[step] = within(result[step], step, tick + 1)
        return rows, result + [far[step] for step in range(z.near, z.pieces)]

    def products(received, group, waits):
        own, *sent = call(
            up_kernel, (z, group), 6,
            [shape(z.partial, F32)] + [shape((z.partial[0] // CUTS, z.partial[1]), BF16)] * CUTS,
            [VMEM] * (z.members + z.pieces),
            [
                pltpu.VMEM((z.members, 2 * z.each, 2 * z.width), BF16),
                pltpu.VMEM((2,) + z.partial, F32),
            ],
            *wide[group * z.members:(group + 1) * z.members], *(received[step] for step in z.listed),
            waits=waits,
        )
        return own, [swap(value, 1) for value in sent]

    def pair_sums(own, other):
        pair = call(
            pair_kernel, (z,), 2, [shape(z.partial, BF16)], [VMEM] * (1 + CUTS), [], own, *other
        )[0]
        return [pair] + [swap(pair, step) for step in range(2, z.splits, 2)]

    def activated(pairs, waits):
        count = 1
        units = call(
            act_kernel, (z, count), 2,
            [shape((z.group_each // count, z.half), BF16)] * count, [VMEM] * len(pairs), [], *pairs, waits=waits,
        )
        return units, [swap(part, 1) for part in units]

    def down(halves, group, hand_on):
        own = call(
            own_down_kernel, (z,), 4, [shape((z.group_each, z.width), F32)],
            [VMEM] * (z.members + len(halves[0])), [], *tall[group], *halves[0],
        )[0]
        return call(
            down_kernel, (z, len(hand_on)), 4,
            (merged if group < z.pairs else [pay] * z.pieces)
            + [shape(value.shape, value.dtype) for value in hand_on],
            [VMEM] * (z.members + 1 + len(halves[1]) + len(hand_on)), [],
            *tall[group], *halves[1], own, *hand_on,
        )

    routes = routes[0].transpose(0, 2, 1)
    gates = gate_weights[0].transpose(0, 2, 1)
    rows = tokens.reshape(z.rows, z.width)
    kept = rows
    *sent, weight = call(
        pack_kernel, (z,), 3,
        [all_pay] * z.pieces + [shape((z.all_pay, z.rows), BF16)],
        [HBM] * 3,
        [
            pltpu.VMEM(routes.shape, routes.dtype),
            pltpu.VMEM(gates.shape, gates.dtype),
            pltpu.VMEM(rows.shape, rows.dtype),
            pltpu.SemaphoreType.DMA((3,)),
        ],
        *(pltpu.with_memory_space_constraint(value, pltpu.HBM) for value in (routes, gates, rows)),
    )
    received = exchanged(sent)
    gate_up = pltpu.with_memory_space_constraint(gate_up, pltpu.HBM)
    down_proj = pltpu.with_memory_space_constraint(down_proj, pltpu.HBM)
    wide = call(
        load_kernel, (z, parts), 1,
        [pltpu.VMEM((2 * z.width, z.units), BF16)] * z.local,
        [HBM], [pltpu.SemaphoreType.DMA((z.local * parts,))], gate_up, waits=[weight],
    )

    def load_down(group, after):
        return call(
            load_down_kernel, (z, group), 1,
            [pltpu.VMEM((z.units, z.width), BF16)] * z.members,
            [HBM], [pltpu.SemaphoreType.DMA((z.members,))], down_proj, waits=[after],
        )

    tall = [load_down(0, wide[-1])]
    groups = range(z.groups)
    for tick in range(sections):
        last = tick == sections - 1
        sums, returned = [], []
        for group in groups:
            own, other = products(received, group, [sums[-1][0]] if group else tall[0][:1])
            sums.append(pair_sums(own, other))
            if group == 0:
                halves = activated(sums[0], [])
        for group in groups:
            if group and tick == 0:
                tall.append(load_down(group, outgoing[0]))
            if group:
                halves = activated(sums[group], tall[group][:1] if tick == 0 else outgoing[:1])
            hand_on = [routes] if tick == 0 and group == z.groups - 1 else []
            outgoing = down(halves, group, hand_on)
            if hand_on:
                pairs = [(i + 1, i) for i in range(sections - 1)]
                following = lax.ppermute(outgoing.pop(), "section", pairs)
            returned.append(sent_back(outgoing, group))
        returned = sum(returned, [])
        kept, *sent = call(
            combine_kernel, (z, tick, last), 4,
            [whole] if last else [whole] + [all_pay] * (z.pieces - z.near),
            [VMEM] * (3 + len(returned) + (not last)), [],
            weight, rows, kept, *returned, *([] if last else [following]),
        )
        if not last:
            rows, received = relayed(sent, kept, tick)
    return kept.reshape(1, z.micro, z.tok, z.width)


def solution(mesh):
    placed = (
        P(None, "expert", "hidden"),
        P("section", "hidden", None, "expert"),
        P("section", "expert", "hidden"),
        P("section", None, "expert", None),
        P("section", None, "expert", None),
    )
    return jax.shard_map(
        on_device,
        mesh=mesh,
        in_specs=placed,
        out_specs=P("section", None, "expert", "hidden"),
        check_vma=False,
    )
```

```python
import functools

import jax
import jax.numpy as jnp
from jax import lax
from jax.experimental import pallas as pl
from jax.experimental.pallas import tpu as pltpu
from jax.sharding import PartitionSpec as P

D = 7168
FFE = 1024
CAP = 3
EPS = 1e-06
EXTRA = 16
CUTS = 2
VMEM = pl.BlockSpec(memory_space=pltpu.VMEM)
HBM = pl.BlockSpec(memory_space=pltpu.HBM)
BF16 = jnp.bfloat16
F32 = jnp.float32
I32 = jnp.int32
ACROSS = (((1,), (1,)), ((), ()))
DOWN = (((0,), (0,)), ((), ()))


def padded(count, unit):
    return -(-count // unit) * unit


def dot(a, b, dims=(((1,), (0,)), ((), ()))):
    return lax.dot_general(a, b, dims, preferred_element_type=F32)


def one_hot(mask):
    return jnp.where(mask, F32(1.0), F32(0.0))


def divided(value, divisor):
    if divisor == 1:
        return value, jnp.zeros_like(value)
    quotient = lax.shift_right_logical(value * (2**20 // divisor + 1), 20)
    return quotient, value - quotient * divisor


class Sizes:
    def __init__(self, tokens, gate_up, peers, splits):
        self.peers, self.splits = peers, splits
        self.micro, self.tok, self.width = tokens.shape
        self.rows = self.micro * self.tok
        self.units_dev = gate_up.shape[3]
        self.units = min(FFE, self.units_dev)
        self.half = self.units // 2
        self.local = self.units_dev // self.units
        self.groups = 2 if self.local % 2 == 0 else 1
        self.members = self.local // self.groups
        self.slots = self.micro * CAP
        self.pay = padded(self.members * self.slots, 8)
        self.pieces = peers if peers <= 8 else 1
        self.pairs = self.groups - 1 if self.pieces == 4 else 0
        self.near = self.pieces // 2
        self.listed = sorted(range(self.pieces), key=lambda step: -step.bit_length())
        self.group_pay = peers * self.pay
        self.piece = self.group_pay // self.pieces
        self.all_pay = self.groups * self.group_pay
        self.all_piece = self.groups * self.piece
        self.each = padded(peers * self.slots, 8)
        self.group_each = self.members * self.each
        self.partial = (self.group_each + EXTRA, 2 * self.half)

    def order(self):
        shape = (self.group_each, self.group_pay)
        row = lax.broadcasted_iota(I32, (self.group_each, 1), 0)
        expert, rest = divided(row, self.each)
        step, slot = divided(rest, self.slots)
        target = jnp.where(step < self.peers, step * self.pay + expert * self.slots + slot, -1)
        return one_hot(lax.broadcasted_iota(I32, shape, 1) == target).astype(BF16)


def line_up(z, ref):
    total = None
    for batch in range(z.micro):
        shape = (z.tok, z.rows)
        place = lax.broadcasted_iota(I32, shape, 1) == lax.broadcasted_iota(I32, shape, 0) + batch * z.tok
        value = dot(ref[batch].astype(F32).astype(BF16), one_hot(place).astype(BF16))
        total = value if total is None else total + value
    return total


def slot_hits(z, routes_ref):
    row = lax.broadcasted_iota(I32, (z.all_pay, 1), 0)
    step, rest = divided(row, z.groups * z.pay)
    group, place = divided(rest, z.pay)
    member, inside = divided(place, z.slots)
    batch, rank = divided(inside, CAP)
    rank = jnp.where(member < z.members, rank, -1)
    owner = step ^ lax.axis_index("expert") if z.pieces > 1 else step
    if z.units_dev >= FFE:
        expert = owner * z.local + group * z.members + member
    else:
        expert = lax.shift_right_logical(owner, (FFE // z.units_dev).bit_length() - 1)
    routes = line_up(z, routes_ref)
    token = lax.broadcasted_iota(I32, (z.all_pay, z.rows), 1)
    start = batch * z.tok
    same = (token >= start) & (token < start + z.tok)
    expert = expert.astype(F32)
    first = (routes[0:1, :] == expert) & same
    second = (routes[1:2, :] == expert) & same
    chosen = one_hot(first | second)
    shape = (z.rows, z.rows)
    before = lax.broadcasted_iota(I32, shape, 0) < lax.broadcasted_iota(I32, shape, 1)
    count = dot(chosen.astype(BF16), one_hot(before).astype(BF16))
    hits = jnp.where(count == rank.astype(F32), chosen, F32(0.0))
    return hits, first, second


def send_rows(z, hits, rows, outs, steps):
    hits = [hits[step * z.all_piece:(step + 1) * z.all_piece] for step in steps]
    value = dot(jnp.concatenate(hits, axis=0).astype(BF16), rows)
    for index, out in enumerate(outs):
        out[...] = value[index * z.all_piece:(index + 1) * z.all_piece].astype(BF16)


def near_kernel(z, routes_ref, rows_ref, *outs):
    hits, _, _ = slot_hits(z, routes_ref)
    send_rows(z, hits, rows_ref[...], outs, range(z.near))


def group_rows(z, group, pieces):
    result = []
    for piece in pieces:
        value = piece[...].astype(F32)
        for step in range(z.peers // z.pieces):
            low = (step * z.groups + group) * z.pay
            result.append(value[low:low + z.pay])
    return jnp.concatenate(result, axis=0)


def pack_kernel(z, *refs):
    sources, outs = refs[:3], refs[3:-4]
    routes_ref, gates_ref, rows_ref, sems = refs[-4:]
    copies = [
        pltpu.make_async_copy(source, target, sems.at[index])
        for index, (source, target) in enumerate(zip(sources, refs[-4:-1]))
    ]
    for copy in copies:
        copy.start()
    copies[0].wait()
    hits, first, second = slot_hits(z, routes_ref)
    copies[1].wait()
    gates = line_up(z, gates_ref)
    weight = jnp.where(first, gates[0:1, :], F32(0.0)) + jnp.where(second, gates[1:2, :], F32(0.0))
    outs[-1][...] = (hits * weight).astype(BF16)
    copies[2].wait()
    send_rows(z, hits, rows_ref[...], outs[:-1], range(z.pieces))


def load_kernel(z, parts, gate_up, *refs):
    outs, sems = refs[:-1], refs[-1]
    flat = gate_up.reshape(2 * z.width, z.units_dev)
    depth = 2 * z.width // parts
    copies = []
    for expert in range(z.local):
        for part in range(parts):
            rows = pl.ds(part * depth, depth)
            copies.append(
                pltpu.make_async_copy(
                    flat.at[rows, pl.ds(expert * z.units, z.units)],
                    outs[expert].at[rows],
                    sems.at[expert * parts + part],
                )
            )
    for copy in copies:
        copy.start()
    for copy in copies:
        copy.wait()


def load_down_kernel(z, group, down_proj, *refs):
    outs, sems = refs[:-1], refs[-1]
    copies = []
    for index in range(z.members):
        rows = pl.ds((group * z.members + index) * z.units, z.units)
        copies.append(pltpu.make_async_copy(down_proj.at[0, rows, :], outs[index], sems.at[index]))
    for copy in copies:
        copy.start()
    for copy in copies:
        copy.wait()


def split_sums(sums, lanes):
    high = sums.astype(BF16).astype(F32)
    row = lax.broadcasted_iota(I32, sums.shape, 0)
    both = jnp.where(row == 0, high, jnp.where(row == 1, sums - high, F32(0.0)))
    if both.shape[1] < lanes:
        both = jnp.concatenate([both, jnp.zeros((EXTRA, lanes - both.shape[1]), F32)], axis=1)
    return both


def up_kernel(z, group, *refs):
    weights, refs = refs[:z.members], refs[z.members:]
    received, refs = refs[:z.pieces], refs[z.pieces:]
    received = [received[z.listed.index(step)] for step in range(z.pieces)]
    own, *sent, spread, staged = refs
    rows = dot(z.order(), group_rows(z, group, received).astype(BF16))
    squares = rows * rows
    high = squares.astype(BF16)
    low = (squares - high.astype(F32)).astype(BF16)
    ones = jnp.ones((EXTRA, z.width), BF16)
    sums = dot(ones, high, ACROSS) + dot(ones, low, ACROSS)
    rows = rows.astype(BF16)
    block = 128
    shape = (block, 2 * block)
    target = lax.broadcasted_iota(I32, shape, 1) - 2 * lax.broadcasted_iota(I32, shape, 0)
    placing = [one_hot(target == side).astype(BF16) for side in range(2)]
    for piece in range(z.width // block):
        columns = slice(piece * block, (piece + 1) * block)
        gate, up = dot(rows[:, columns], placing[0]), dot(rows[:, columns], placing[1])
        for expert in range(z.members):
            here = slice(expert * z.each, (expert + 1) * z.each)
            both = jnp.concatenate([gate[here], up[here]], axis=0).astype(BF16)
            spread[expert, :, 2 * piece * block:2 * (piece + 1) * block] = both
    totals = [dot(spread[expert], weights[expert][...]) for expert in range(z.members)]
    extra = split_sums(sums, 2 * z.half)
    for side in range(2):
        columns = slice(side * z.half, (side + 1) * z.half)
        gate = jnp.concatenate([total[:z.each, columns] for total in totals], axis=0)
        up = jnp.concatenate([total[z.each:, columns] for total in totals], axis=0)
        staged[side, :z.group_each, :] = jnp.concatenate([gate, up], axis=1)
        staged[side, z.group_each:, :] = extra
    core = lax.axis_index("hidden") & 1
    own[...] = staged[core]
    rows = z.partial[0] // CUTS
    value = staged[1 - core]
    for index, out in enumerate(sent):
        out[...] = value[index * rows:(index + 1) * rows].astype(BF16)


def joined(z, refs):
    total = refs[0][...].astype(F32)
    for ref in refs[1:]:
        total = total + ref[...].astype(F32)
    products, extra = total[:z.group_each], total[z.group_each:]
    row = lax.broadcasted_iota(I32, extra.shape, 0)
    sums = jnp.sum(jnp.where(row < 2, extra, F32(0.0)), axis=0, keepdims=True)
    return products, sums


def pair_kernel(z, own, *refs):
    *other, out = refs
    products, sums = joined(z, [own[...], jnp.concatenate([ref[...].astype(F32) for ref in other], axis=0)])
    sums = split_sums(jnp.broadcast_to(sums, (EXTRA, 2 * z.half)), 2 * z.half)
    out[...] = jnp.concatenate([products, sums], axis=0).astype(BF16)


def act_kernel(z, count, *refs):
    outs = refs[-count:]
    products, sums = joined(z, refs[:-count])
    shape = (z.group_each, z.group_each)
    diagonal = lax.broadcasted_iota(I32, shape, 0) == lax.broadcasted_iota(I32, shape, 1)
    sums = jnp.sum(jnp.where(diagonal, sums[:, :z.group_each], F32(0.0)), axis=1, keepdims=True)
    scale = lax.rsqrt(sums / D + EPS)
    gate = scale * products[:, :z.half]
    up = scale * products[:, z.half:]
    value = (gate / (F32(1.0) + jnp.exp(-gate)) * up).astype(BF16)
    rows = z.group_each // count
    for index, out in enumerate(outs):
        out[...] = value[index * rows:(index + 1) * rows]


def half_products(z, weights, units_refs, side):
    low = pl.multiple_of(side * z.half, z.half)
    units = jnp.concatenate([ref[...].astype(F32) for ref in units_refs], axis=0)
    results = []
    for expert in range(z.members):
        rows = units[expert * z.each:(expert + 1) * z.each].astype(BF16)
        results.append(dot(rows, weights[expert][pl.ds(low, z.half), :]))
    return jnp.concatenate(results, axis=0)


def own_down_kernel(z, *refs):
    weights, units_ref, out = refs[:z.members], refs[z.members:-1], refs[-1]
    out[...] = half_products(z, weights, units_ref, lax.axis_index("hidden") & 1)


def down_kernel(z, nears, *refs):
    weights, refs = refs[:z.members], refs[z.members:]
    units_ref, own_ref, refs = refs[:1], refs[1], refs[2:]
    near, outs = [ref[...].astype(F32) for ref in refs[:nears]], refs[nears:]
    total = own_ref[...] + half_products(z, weights, units_ref, 1 - (lax.axis_index("hidden") & 1))
    value = dot(z.order(), total.astype(BF16), DOWN)
    value = jnp.concatenate([value[:z.piece], *near, value[z.piece:]], axis=0) if near else value
    low = 0
    for out in outs:
        out[...] = value[low:low + out.shape[0]].astype(BF16)
        low += out.shape[0]


def second_kernel(z, pair_ref, out):
    out[...] = pair_ref[...].astype(F32)[z.piece:].astype(BF16)


def combine_kernel(z, tick, last, weight_ref, rows_ref, kept_ref, *refs):
    returned = []
    if z.pairs:
        count = z.groups * z.pieces
        values, refs = [ref[...].astype(F32) for ref in refs[:count]], refs[count:]
        near = values[-z.groups:]
        for group in range(z.groups):
            own, *far = values[3 * group:3 * group + 3]
            returned += [own, near[group], far[0][:z.piece], far[1]]
    else:
        count = z.groups * z.pieces
        returned, refs = [ref[...].astype(F32) for ref in refs[:count]], refs[count:]
    stacked = []
    for piece in range(z.pieces):
        values = [returned[group * z.pieces + piece] for group in range(z.groups)]
        for step in range(z.peers // z.pieces):
            stacked += [value[step * z.pay:(step + 1) * z.pay] for value in values]
    stacked = jnp.concatenate(stacked, axis=0).astype(BF16)
    mixed = dot(weight_ref[...], stacked, DOWN)
    value = (rows_ref[...].astype(F32) + mixed).astype(BF16)
    if last:
        refs[0][...] = jnp.where(lax.axis_index("section") == tick, value, kept_ref[...])
        return
    routes_ref, out, outs = refs[0], refs[1], refs[2:]
    out[...] = jnp.where(lax.axis_index("section") == tick, value, kept_ref[...])
    hits, _, _ = slot_hits(z, routes_ref)
    send_rows(z, hits, value, outs, range(z.near, z.pieces))


def after_waits(waits, kernel, *refs):
    return kernel(*refs[waits:])


def call(kernel, sizes, megabytes, outs, in_specs, scratch, *args, waits=()):
    results = pl.pallas_call(
        functools.partial(after_waits, len(waits), functools.partial(kernel, *sizes)),
        out_shape=outs,
        in_specs=[VMEM] * len(waits) + in_specs,
        out_specs=[VMEM] * len(outs),
        scratch_shapes=scratch,
        compiler_params=pltpu.CompilerParams(vmem_limit_bytes=megabytes * 2**20),
    )(*waits, *args)
    return list(results)


def on_device(tokens, gate_up, down_proj, routes, gate_weights):
    sections = lax.axis_size("section")
    z = Sizes(tokens, gate_up, lax.axis_size("expert"), lax.axis_size("hidden"))
    parts = 2 if z.width % 256 == 0 else 1
    shape = jax.ShapeDtypeStruct
    pay = shape((z.piece, z.width), BF16)
    all_pay = shape((z.all_piece, z.width), BF16)
    joined_near = [pay] * (z.groups + 3)
    merged = [pay, pay, shape((2 * z.piece, z.width), BF16)]
    whole = shape((z.rows, z.width), BF16)
    steps = sorted(range(z.peers), key=lambda step: -step.bit_length())

    def swap(value, step):
        pairs = [(i, i ^ step) for i in range(z.splits)]
        return lax.ppermute(value, "hidden", pairs)

    def exchanged(pieces):
        if z.pieces == 1:
            return [lax.all_to_all(pieces[0], "expert", split_axis=0, concat_axis=0, tiled=True)]
        result = list(pieces)
        for step in steps[:-1]:
            pairs = [(i, i ^ step) for i in range(z.peers)]
            result[step] = lax.ppermute(pieces[step], "expert", pairs)
        return result

    def across(value, step):
        return lax.ppermute(value, "expert", [(i, i ^ step) for i in range(z.peers)])

    def sent_back(pieces, group):
        if not z.pairs:
            return exchanged(pieces)
        if group < z.pairs:
            return [pieces[0], across(pieces[2], 2)]
        own, *near, two, three = pieces
        two, three = across(two, 2), across(three, 3)
        return [own, two, three, *(across(value, 1) for value in near)]

    def sent_on(pair, waits):
        return across(call(second_kernel, (z,), 2, [pay], [VMEM], [], pair, waits=waits)[0], 1)

    def within(value, step, section):
        low = section * z.peers
        pairs = [(low + i, low + (i ^ step)) for i in range(z.peers)]
        return lax.ppermute(value, ("section", "expert"), pairs)

    def relayed(pieces, kept, tick):
        hop = [(tick, tick + 1)]
        rows = lax.ppermute(kept, "section", hop)
        if z.pieces == 1:
            return rows, [lax.ppermute(exchanged(pieces)[0], "section", hop)]
        far = {}
        for step in steps:
            if step >= z.near:
                pairs = [(tick * z.peers + i, (tick + 1) * z.peers + (i ^ step)) for i in range(z.peers)]
                far[step] = lax.ppermute(pieces[step - z.near], ("section", "expert"), pairs)
        result = call(near_kernel, (z,), 4, [all_pay] * z.near, [VMEM] * 2, [], routes, rows)
        for step in range(1, z.near):
            result[step] = within(result[step], step, tick + 1)
        return rows, result + [far[step] for step in range(z.near, z.pieces)]

    def products(received, group, waits):
        own, *sent = call(
            up_kernel, (z, group), 6,
            [shape(z.partial, F32)] + [shape((z.partial[0] // CUTS, z.partial[1]), BF16)] * CUTS,
            [VMEM] * (z.members + z.pieces),
            [
                pltpu.VMEM((z.members, 2 * z.each, 2 * z.width), BF16),
                pltpu.VMEM((2,) + z.partial, F32),
            ],
            *wide[group * z.members:(group + 1) * z.members], *(received[step] for step in z.listed),
            waits=waits,
        )
        return own, [swap(value, 1) for value in sent]

    def pair_sums(own, other):
        pair = call(
            pair_kernel, (z,), 2, [shape(z.partial, BF16)], [VMEM] * (1 + CUTS), [], own, *other
        )[0]
        return [pair] + [swap(pair, step) for step in range(2, z.splits, 2)]

    def activated(pairs, waits):
        count = 1
        units = call(
            act_kernel, (z, count), 2,
            [shape((z.group_each // count, z.half), BF16)] * count, [VMEM] * len(pairs), [], *pairs, waits=waits,
        )
        return units, [swap(part, 1) for part in units]

    def down(halves, group, nears):
        own = call(
            own_down_kernel, (z,), 4, [shape((z.group_each, z.width), F32)],
            [VMEM] * (z.members + len(halves[0])), [], *tall[group], *halves[0],
        )[0]
        return call(
            down_kernel, (z, len(nears)), 4,
            merged if group < z.pairs else joined_near if nears else [pay] * z.pieces,
            [VMEM] * (z.members + 1 + len(halves[1]) + len(nears)), [],
            *tall[group], *halves[1], own, *nears,
        )

    routes = routes[0].transpose(0, 2, 1)
    gates = gate_weights[0].transpose(0, 2, 1)
    rows = tokens.reshape(z.rows, z.width)
    kept = rows
    *sent, weight = call(
        pack_kernel, (z,), 3,
        [all_pay] * z.pieces + [shape((z.all_pay, z.rows), BF16)],
        [HBM] * 3,
        [
            pltpu.VMEM(routes.shape, routes.dtype),
            pltpu.VMEM(gates.shape, gates.dtype),
            pltpu.VMEM(rows.shape, rows.dtype),
            pltpu.SemaphoreType.DMA((3,)),
        ],
        *(pltpu.with_memory_space_constraint(value, pltpu.HBM) for value in (routes, gates, rows)),
    )
    received = exchanged(sent)
    gate_up = pltpu.with_memory_space_constraint(gate_up, pltpu.HBM)
    down_proj = pltpu.with_memory_space_constraint(down_proj, pltpu.HBM)
    wide = call(
        load_kernel, (z, parts), 1,
        [pltpu.VMEM((2 * z.width, z.units), BF16)] * z.local,
        [HBM], [pltpu.SemaphoreType.DMA((z.local * parts,))], gate_up, waits=[weight],
    )

    def load_down(group, after):
        return call(
            load_down_kernel, (z, group), 1,
            [pltpu.VMEM((z.units, z.width), BF16)] * z.members,
            [HBM], [pltpu.SemaphoreType.DMA((z.members,))], down_proj, waits=[after],
        )

    tall = [load_down(0, wide[-1])]
    groups = range(z.groups)
    following = lax.ppermute(routes, "section", [(i + 1, i) for i in range(sections - 1)])
    for tick in range(sections):
        last = tick == sections - 1
        sums, returned, nears = [], [], []
        for group in groups:
            own, other = products(received, group, [sums[-1][0]] if group else tall[0][:1])
            sums.append(pair_sums(own, other))
            if group == 0:
                halves = activated(sums[0], [])
        for group in groups:
            if group and tick == 0:
                tall.append(load_down(group, outgoing[0]))
            if group:
                halves = activated(sums[group], tall[group][:1] + [following] if tick == 0 else outgoing[:1])
            outgoing = down(halves, group, nears if group >= z.pairs else [])
            nears += outgoing[1:2] if group < z.pairs else []
            returned.append(sent_back(outgoing, group))
        for group in range(z.pairs):
            returned[group].append(sent_on(returned[group][1], outgoing[:1]))
        returned = sum(returned, [])
        kept, *sent = call(
            combine_kernel, (z, tick, last), 4,
            [whole] if last else [whole] + [all_pay] * (z.pieces - z.near),
            [VMEM] * (3 + len(returned) + (not last)), [],
            weight, rows, kept, *returned, *([] if last else [following]),
        )
        if not last:
            rows, received = relayed(sent, kept, tick)
    return kept.reshape(1, z.micro, z.tok, z.width)


def solution(mesh):
    placed = (
        P(None, "expert", "hidden"),
        P("section", "hidden", None, "expert"),
        P("section", "expert", "hidden"),
        P("section", None, "expert", None),
        P("section", None, "expert", None),
    )
    return jax.shard_map(
        on_device,
        mesh=mesh,
        in_specs=placed,
        out_specs=P("section", None, "expert", "hidden"),
        check_vma=False,
    )
```

```python
import functools

import jax
import jax.numpy as jnp
from jax import lax
from jax.experimental import pallas as pl
from jax.experimental.pallas import tpu as pltpu
from jax.sharding import PartitionSpec as P

D = 7168
FFE = 1024
CAP = 3
EPS = 1e-06
EXTRA = 16
CUTS = 2
VMEM = pl.BlockSpec(memory_space=pltpu.VMEM)
HBM = pl.BlockSpec(memory_space=pltpu.HBM)
BF16 = jnp.bfloat16
F32 = jnp.float32
I32 = jnp.int32
ACROSS = (((1,), (1,)), ((), ()))
DOWN = (((0,), (0,)), ((), ()))


def padded(count, unit):
    return -(-count // unit) * unit


def dot(a, b, dims=(((1,), (0,)), ((), ()))):
    return lax.dot_general(a, b, dims, preferred_element_type=F32)


def one_hot(mask):
    return jnp.where(mask, F32(1.0), F32(0.0))


def divided(value, divisor):
    if divisor == 1:
        return value, jnp.zeros_like(value)
    quotient = lax.shift_right_logical(value * (2**20 // divisor + 1), 20)
    return quotient, value - quotient * divisor


class Sizes:
    def __init__(self, tokens, gate_up, peers, splits):
        self.peers, self.splits = peers, splits
        self.micro, self.tok, self.width = tokens.shape
        self.rows = self.micro * self.tok
        self.units_dev = gate_up.shape[3]
        self.units = min(FFE, self.units_dev)
        self.half = self.units // 2
        self.local = self.units_dev // self.units
        self.groups = 2 if self.local % 2 == 0 else 1
        self.members = self.local // self.groups
        self.slots = self.micro * CAP
        self.pay = padded(self.members * self.slots, 8)
        self.pieces = peers if peers <= 8 else 1
        self.pairs = self.groups - 1 if self.pieces == 4 else 0
        self.near = self.pieces // 2
        self.listed = sorted(range(self.pieces), key=lambda step: -step.bit_length())
        self.group_pay = peers * self.pay
        self.piece = self.group_pay // self.pieces
        self.all_pay = self.groups * self.group_pay
        self.all_piece = self.groups * self.piece
        self.each = padded(peers * self.slots, 8)
        self.group_each = self.members * self.each
        self.partial = (self.group_each + EXTRA, 2 * self.half)

    def order(self):
        shape = (self.group_each, self.group_pay)
        row = lax.broadcasted_iota(I32, (self.group_each, 1), 0)
        expert, rest = divided(row, self.each)
        step, slot = divided(rest, self.slots)
        target = jnp.where(step < self.peers, step * self.pay + expert * self.slots + slot, -1)
        return one_hot(lax.broadcasted_iota(I32, shape, 1) == target).astype(BF16)


def line_up(z, ref):
    total = None
    for batch in range(z.micro):
        shape = (z.tok, z.rows)
        place = lax.broadcasted_iota(I32, shape, 1) == lax.broadcasted_iota(I32, shape, 0) + batch * z.tok
        value = dot(ref[batch].astype(F32).astype(BF16), one_hot(place).astype(BF16))
        total = value if total is None else total + value
    return total


def slot_hits(z, routes_ref):
    row = lax.broadcasted_iota(I32, (z.all_pay, 1), 0)
    step, rest = divided(row, z.groups * z.pay)
    group, place = divided(rest, z.pay)
    member, inside = divided(place, z.slots)
    batch, rank = divided(inside, CAP)
    rank = jnp.where(member < z.members, rank, -1)
    owner = step ^ lax.axis_index("expert") if z.pieces > 1 else step
    if z.units_dev >= FFE:
        expert = owner * z.local + group * z.members + member
    else:
        expert = lax.shift_right_logical(owner, (FFE // z.units_dev).bit_length() - 1)
    routes = line_up(z, routes_ref)
    token = lax.broadcasted_iota(I32, (z.all_pay, z.rows), 1)
    start = batch * z.tok
    same = (token >= start) & (token < start + z.tok)
    expert = expert.astype(F32)
    first = (routes[0:1, :] == expert) & same
    second = (routes[1:2, :] == expert) & same
    chosen = one_hot(first | second)
    shape = (z.rows, z.rows)
    before = lax.broadcasted_iota(I32, shape, 0) < lax.broadcasted_iota(I32, shape, 1)
    count = dot(chosen.astype(BF16), one_hot(before).astype(BF16))
    hits = jnp.where(count == rank.astype(F32), chosen, F32(0.0))
    return hits, first, second


def send_rows(z, hits, rows, outs, steps):
    hits = [hits[step * z.all_piece:(step + 1) * z.all_piece] for step in steps]
    value = dot(jnp.concatenate(hits, axis=0).astype(BF16), rows)
    for index, out in enumerate(outs):
        out[...] = value[index * z.all_piece:(index + 1) * z.all_piece].astype(BF16)


def near_kernel(z, routes_ref, rows_ref, *outs):
    hits, _, _ = slot_hits(z, routes_ref)
    send_rows(z, hits, rows_ref[...], outs, range(z.near))


def group_rows(z, group, pieces):
    result = []
    for piece in pieces:
        value = piece[...].astype(F32)
        for step in range(z.peers // z.pieces):
            low = (step * z.groups + group) * z.pay
            result.append(value[low:low + z.pay])
    return jnp.concatenate(result, axis=0)


def pack_kernel(z, *refs):
    sources, outs = refs[:3], refs[3:-4]
    routes_ref, gates_ref, rows_ref, sems = refs[-4:]
    copies = [
        pltpu.make_async_copy(source, target, sems.at[index])
        for index, (source, target) in enumerate(zip(sources, refs[-4:-1]))
    ]
    for copy in copies:
        copy.start()
    copies[0].wait()
    hits, first, second = slot_hits(z, routes_ref)
    copies[1].wait()
    gates = line_up(z, gates_ref)
    weight = jnp.where(first, gates[0:1, :], F32(0.0)) + jnp.where(second, gates[1:2, :], F32(0.0))
    outs[-1][...] = (hits * weight).astype(BF16)
    copies[2].wait()
    send_rows(z, hits, rows_ref[...], outs[:-1], range(z.pieces))


def load_kernel(z, parts, gate_up, *refs):
    outs, sems = refs[:-1], refs[-1]
    flat = gate_up.reshape(2 * z.width, z.units_dev)
    depth = 2 * z.width // parts
    copies = []
    for expert in range(z.local):
        for part in range(parts):
            rows = pl.ds(part * depth, depth)
            copies.append(
                pltpu.make_async_copy(
                    flat.at[rows, pl.ds(expert * z.units, z.units)],
                    outs[expert].at[rows],
                    sems.at[expert * parts + part],
                )
            )
    for copy in copies:
        copy.start()
    for copy in copies:
        copy.wait()


def load_down_kernel(z, experts, down_proj, *refs):
    outs, sems = refs[:-1], refs[-1]
    copies = []
    for index, expert in enumerate(experts):
        rows = pl.ds(expert * z.units, z.units)
        copies.append(pltpu.make_async_copy(down_proj.at[0, rows, :], outs[index], sems.at[index]))
    for copy in copies:
        copy.start()
    for copy in copies:
        copy.wait()


def split_sums(sums, lanes):
    high = sums.astype(BF16).astype(F32)
    row = lax.broadcasted_iota(I32, sums.shape, 0)
    both = jnp.where(row == 0, high, jnp.where(row == 1, sums - high, F32(0.0)))
    if both.shape[1] < lanes:
        both = jnp.concatenate([both, jnp.zeros((EXTRA, lanes - both.shape[1]), F32)], axis=1)
    return both


def up_kernel(z, group, *refs):
    weights, refs = refs[:z.members], refs[z.members:]
    received, refs = refs[:z.pieces], refs[z.pieces:]
    received = [received[z.listed.index(step)] for step in range(z.pieces)]
    own, *sent, spread, staged = refs
    rows = dot(z.order(), group_rows(z, group, received).astype(BF16))
    squares = rows * rows
    high = squares.astype(BF16)
    low = (squares - high.astype(F32)).astype(BF16)
    ones = jnp.ones((EXTRA, z.width), BF16)
    sums = dot(ones, high, ACROSS) + dot(ones, low, ACROSS)
    rows = rows.astype(BF16)
    block = 128
    shape = (block, 2 * block)
    target = lax.broadcasted_iota(I32, shape, 1) - 2 * lax.broadcasted_iota(I32, shape, 0)
    placing = [one_hot(target == side).astype(BF16) for side in range(2)]
    for piece in range(z.width // block):
        columns = slice(piece * block, (piece + 1) * block)
        gate, up = dot(rows[:, columns], placing[0]), dot(rows[:, columns], placing[1])
        for expert in range(z.members):
            here = slice(expert * z.each, (expert + 1) * z.each)
            both = jnp.concatenate([gate[here], up[here]], axis=0).astype(BF16)
            spread[expert, :, 2 * piece * block:2 * (piece + 1) * block] = both
    totals = [dot(spread[expert], weights[expert][...]) for expert in range(z.members)]
    extra = split_sums(sums, 2 * z.half)
    for side in range(2):
        columns = slice(side * z.half, (side + 1) * z.half)
        gate = jnp.concatenate([total[:z.each, columns] for total in totals], axis=0)
        up = jnp.concatenate([total[z.each:, columns] for total in totals], axis=0)
        staged[side, :z.group_each, :] = jnp.concatenate([gate, up], axis=1)
        staged[side, z.group_each:, :] = extra
    core = lax.axis_index("hidden") & 1
    own[...] = staged[core]
    rows = z.partial[0] // CUTS
    value = staged[1 - core]
    for index, out in enumerate(sent):
        out[...] = value[index * rows:(index + 1) * rows].astype(BF16)


def joined(z, refs):
    total = refs[0][...].astype(F32)
    for ref in refs[1:]:
        total = total + ref[...].astype(F32)
    products, extra = total[:z.group_each], total[z.group_each:]
    row = lax.broadcasted_iota(I32, extra.shape, 0)
    sums = jnp.sum(jnp.where(row < 2, extra, F32(0.0)), axis=0, keepdims=True)
    return products, sums


def pair_kernel(z, own, *refs):
    *other, out = refs
    products, sums = joined(z, [own[...], jnp.concatenate([ref[...].astype(F32) for ref in other], axis=0)])
    sums = split_sums(jnp.broadcast_to(sums, (EXTRA, 2 * z.half)), 2 * z.half)
    out[...] = jnp.concatenate([products, sums], axis=0).astype(BF16)


def act_kernel(z, count, *refs):
    outs = refs[-count:]
    products, sums = joined(z, refs[:-count])
    shape = (z.group_each, z.group_each)
    diagonal = lax.broadcasted_iota(I32, shape, 0) == lax.broadcasted_iota(I32, shape, 1)
    sums = jnp.sum(jnp.where(diagonal, sums[:, :z.group_each], F32(0.0)), axis=1, keepdims=True)
    scale = lax.rsqrt(sums / D + EPS)
    gate = scale * products[:, :z.half]
    up = scale * products[:, z.half:]
    value = (gate / (F32(1.0) + jnp.exp(-gate)) * up).astype(BF16)
    rows = z.group_each // count
    for index, out in enumerate(outs):
        out[...] = value[index * rows:(index + 1) * rows]


def half_products(z, weights, units_refs, side):
    low = pl.multiple_of(side * z.half, z.half)
    units = jnp.concatenate([ref[...].astype(F32) for ref in units_refs], axis=0)
    results = []
    for expert in range(z.members):
        rows = units[expert * z.each:(expert + 1) * z.each].astype(BF16)
        results.append(dot(rows, weights[expert][pl.ds(low, z.half), :]))
    return jnp.concatenate(results, axis=0)


def own_down_kernel(z, *refs):
    weights, units_ref, out = refs[:z.members], refs[z.members:-1], refs[-1]
    out[...] = half_products(z, weights, units_ref, lax.axis_index("hidden") & 1)


def down_kernel(z, hands_on, *refs):
    weights, refs = refs[:z.members], refs[z.members:]
    units_ref, own_ref, outs = refs[:1], refs[1], refs[2:]
    if hands_on:
        outs[-1][...] = outs[0][...]
        outs = outs[1:-1]
    total = own_ref[...] + half_products(z, weights, units_ref, 1 - (lax.axis_index("hidden") & 1))
    value = dot(z.order(), total.astype(BF16), DOWN)
    low = 0
    for out in outs:
        out[...] = value[low:low + out.shape[0]].astype(BF16)
        low += out.shape[0]


def second_kernel(z, pair_ref, out):
    out[...] = pair_ref[...].astype(F32)[z.piece:].astype(BF16)


def combine_kernel(z, tick, last, weight_ref, rows_ref, kept_ref, *refs):
    count = z.groups * z.pieces
    returned, refs = [ref[...].astype(F32)[:z.piece] for ref in refs[:count]], refs[count:]
    stacked = []
    for piece in range(z.pieces):
        values = [returned[group * z.pieces + piece] for group in range(z.groups)]
        for step in range(z.peers // z.pieces):
            stacked += [value[step * z.pay:(step + 1) * z.pay] for value in values]
    stacked = jnp.concatenate(stacked, axis=0).astype(BF16)
    mixed = dot(weight_ref[...], stacked, DOWN)
    value = (rows_ref[...].astype(F32) + mixed).astype(BF16)
    if last:
        refs[0][...] = jnp.where(lax.axis_index("section") == tick, value, kept_ref[...])
        return
    routes_ref, out, outs = refs[0], refs[1], refs[2:]
    out[...] = jnp.where(lax.axis_index("section") == tick, value, kept_ref[...])
    hits, _, _ = slot_hits(z, routes_ref)
    send_rows(z, hits, value, outs, range(z.near, z.pieces))


def after_waits(waits, kernel, *refs):
    return kernel(*refs[waits:])


def call(kernel, sizes, megabytes, outs, in_specs, scratch, *args, waits=()):
    results = pl.pallas_call(
        functools.partial(after_waits, len(waits), functools.partial(kernel, *sizes)),
        out_shape=outs,
        in_specs=[VMEM] * len(waits) + in_specs,
        out_specs=[VMEM] * len(outs),
        scratch_shapes=scratch,
        compiler_params=pltpu.CompilerParams(vmem_limit_bytes=megabytes * 2**20),
    )(*waits, *args)
    return list(results)


def on_device(tokens, gate_up, down_proj, routes, gate_weights):
    sections = lax.axis_size("section")
    z = Sizes(tokens, gate_up, lax.axis_size("expert"), lax.axis_size("hidden"))
    parts = 2 if z.width % 256 == 0 else 1
    shape = jax.ShapeDtypeStruct
    pay = shape((z.piece, z.width), BF16)
    all_pay = shape((z.all_piece, z.width), BF16)
    merged = [pay, pay, shape((2 * z.piece, z.width), BF16)]
    whole = shape((z.rows, z.width), BF16)
    steps = sorted(range(z.peers), key=lambda step: -step.bit_length())

    def swap(value, step):
        pairs = [(i, i ^ step) for i in range(z.splits)]
        return lax.ppermute(value, "hidden", pairs)

    def exchanged(pieces):
        if z.pieces == 1:
            return [lax.all_to_all(pieces[0], "expert", split_axis=0, concat_axis=0, tiled=True)]
        result = list(pieces)
        for step in steps[:-1]:
            pairs = [(i, i ^ step) for i in range(z.peers)]
            result[step] = lax.ppermute(pieces[step], "expert", pairs)
        return result

    def across(value, step):
        return lax.ppermute(value, "expert", [(i, i ^ step) for i in range(z.peers)])

    def sent_back(pieces, group):
        if group >= z.pairs:
            return exchanged(pieces)
        own, near, far = pieces
        far = across(far, 2)
        second = call(second_kernel, (z,), 2, [pay], [VMEM], [], far)[0]
        return [own, across(near, 1), far, across(second, 1)]

    def within(value, step, section):
        low = section * z.peers
        pairs = [(low + i, low + (i ^ step)) for i in range(z.peers)]
        return lax.ppermute(value, ("section", "expert"), pairs)

    def relayed(pieces, kept, tick):
        hop = [(tick, tick + 1)]
        rows = lax.ppermute(kept, "section", hop)
        if z.pieces == 1:
            return rows, [lax.ppermute(exchanged(pieces)[0], "section", hop)]
        far = {}
        for step in steps:
            if step >= z.near:
                pairs = [(tick * z.peers + i, (tick + 1) * z.peers + (i ^ step)) for i in range(z.peers)]
                far[step] = lax.ppermute(pieces[step - z.near], ("section", "expert"), pairs)
        result = call(near_kernel, (z,), 4, [all_pay] * z.near, [VMEM] * 2, [], routes, rows)
        for step in range(1, z.near):
            result[step] = within(result[step], step, tick + 1)
        return rows, result + [far[step] for step in range(z.near, z.pieces)]

    def products(received, group, waits):
        own, *sent = call(
            up_kernel, (z, group), 6,
            [shape(z.partial, F32)] + [shape((z.partial[0] // CUTS, z.partial[1]), BF16)] * CUTS,
            [VMEM] * (z.members + z.pieces),
            [
                pltpu.VMEM((z.members, 2 * z.each, 2 * z.width), BF16),
                pltpu.VMEM((2,) + z.partial, F32),
            ],
            *wide[group * z.members:(group + 1) * z.members], *(received[step] for step in z.listed),
            waits=waits,
        )
        return own, [swap(value, 1) for value in sent]

    def pair_sums(own, other):
        pair = call(
            pair_kernel, (z,), 2, [shape(z.partial, BF16)], [VMEM] * (1 + CUTS), [], own, *other
        )[0]
        return [pair] + [swap(pair, step) for step in range(2, z.splits, 2)]

    def activated(pairs, waits):
        count = 1
        units = call(
            act_kernel, (z, count), 2,
            [shape((z.group_each // count, z.half), BF16)] * count, [VMEM] * len(pairs), [], *pairs, waits=waits,
        )
        return units, [swap(part, 1) for part in units]

    def down(halves, group, hand_on):
        own = call(
            own_down_kernel, (z,), 4, [shape((z.group_each, z.width), F32)],
            [VMEM] * (z.members + len(halves[0])), [], *tall[group * z.members:(group + 1) * z.members], *halves[0],
        )[0]
        return call(
            down_kernel, (z, len(hand_on)), 4,
            (merged if group < z.pairs else [pay] * z.pieces)
            + [shape(value.shape, value.dtype) for value in hand_on],
            [VMEM] * (z.members + 1 + len(halves[1]) + len(hand_on)), [],
            *tall[group * z.members:(group + 1) * z.members], *halves[1], own, *hand_on,
        )

    routes = routes[0].transpose(0, 2, 1)
    gates = gate_weights[0].transpose(0, 2, 1)
    rows = tokens.reshape(z.rows, z.width)
    kept = rows
    *sent, weight = call(
        pack_kernel, (z,), 3,
        [all_pay] * z.pieces + [shape((z.all_pay, z.rows), BF16)],
        [HBM] * 3,
        [
            pltpu.VMEM(routes.shape, routes.dtype),
            pltpu.VMEM(gates.shape, gates.dtype),
            pltpu.VMEM(rows.shape, rows.dtype),
            pltpu.SemaphoreType.DMA((3,)),
        ],
        *(pltpu.with_memory_space_constraint(value, pltpu.HBM) for value in (routes, gates, rows)),
    )
    received = exchanged(sent)
    gate_up = pltpu.with_memory_space_constraint(gate_up, pltpu.HBM)
    down_proj = pltpu.with_memory_space_constraint(down_proj, pltpu.HBM)
    wide = call(
        load_kernel, (z, parts), 1,
        [pltpu.VMEM((2 * z.width, z.units), BF16)] * z.local,
        [HBM], [pltpu.SemaphoreType.DMA((z.local * parts,))], gate_up, waits=[weight],
    )

    def load_down(experts, after):
        return call(
            load_down_kernel, (z, experts), 1,
            [pltpu.VMEM((z.units, z.width), BF16)] * len(experts),
            [HBM], [pltpu.SemaphoreType.DMA((len(experts),))], down_proj, waits=[after],
        )

    early = z.local if z.groups == 1 else z.members + z.members // 2
    tall = load_down(range(early), wide[-1])
    groups = range(z.groups)
    for tick in range(sections):
        last = tick == sections - 1
        sums, returned = [], []
        for group in groups:
            own, other = products(received, group, [sums[-1][0]] if group else tall[:1])
            sums.append(pair_sums(own, other))
            if group == 0:
                halves = activated(sums[0], [])
        for group in groups:
            if group and tick == 0:
                tall += load_down(range(early, z.local), outgoing[0])
            if group:
                halves = activated(sums[group], tall[-1:] if tick == 0 else outgoing[:1])
            hand_on = [routes] if tick == 0 and group == z.groups - 1 else []
            outgoing = down(halves, group, hand_on)
            if hand_on:
                pairs = [(i + 1, i) for i in range(sections - 1)]
                following = lax.ppermute(outgoing.pop(), "section", pairs)
            returned.append(sent_back(outgoing, group))
        returned = sum(returned, [])
        kept, *sent = call(
            combine_kernel, (z, tick, last), 4,
            [whole] if last else [whole] + [all_pay] * (z.pieces - z.near),
            [VMEM] * (3 + len(returned) + (not last)), [],
            weight, rows, kept, *returned, *([] if last else [following]),
        )
        if not last:
            rows, received = relayed(sent, kept, tick)
    return kept.reshape(1, z.micro, z.tok, z.width)


def solution(mesh):
    placed = (
        P(None, "expert", "hidden"),
        P("section", "hidden", None, "expert"),
        P("section", "expert", "hidden"),
        P("section", None, "expert", None),
        P("section", None, "expert", None),
    )
    return jax.shard_map(
        on_device,
        mesh=mesh,
        in_specs=placed,
        out_specs=P("section", None, "expert", "hidden"),
        check_vma=False,
    )
```

```python
import functools

import jax
import jax.numpy as jnp
from jax import lax
from jax.experimental import pallas as pl
from jax.experimental.pallas import tpu as pltpu
from jax.sharding import PartitionSpec as P

D = 7168
FFE = 1024
CAP = 3
EPS = 1e-06
EXTRA = 16
CUTS = 2
VMEM = pl.BlockSpec(memory_space=pltpu.VMEM)
HBM = pl.BlockSpec(memory_space=pltpu.HBM)
BF16 = jnp.bfloat16
F32 = jnp.float32
I32 = jnp.int32
ACROSS = (((1,), (1,)), ((), ()))
DOWN = (((0,), (0,)), ((), ()))


def padded(count, unit):
    return -(-count // unit) * unit


def dot(a, b, dims=(((1,), (0,)), ((), ()))):
    return lax.dot_general(a, b, dims, preferred_element_type=F32)


def one_hot(mask):
    return jnp.where(mask, F32(1.0), F32(0.0))


def divided(value, divisor):
    if divisor == 1:
        return value, jnp.zeros_like(value)
    quotient = lax.shift_right_logical(value * (2**20 // divisor + 1), 20)
    return quotient, value - quotient * divisor


class Sizes:
    def __init__(self, tokens, gate_up, peers, splits):
        self.peers, self.splits = peers, splits
        self.micro, self.tok, self.width = tokens.shape
        self.rows = self.micro * self.tok
        self.units_dev = gate_up.shape[3]
        self.units = min(FFE, self.units_dev)
        self.half = self.units // 2
        self.local = self.units_dev // self.units
        self.groups = 2 if self.local % 2 == 0 else 1
        self.members = self.local // self.groups
        self.slots = self.micro * CAP
        self.pay = padded(self.members * self.slots, 8)
        self.pieces = peers if peers <= 8 else 1
        self.pairs = self.groups - 1 if self.pieces == 4 else 0
        self.near = self.pieces // 2
        self.listed = sorted(range(self.pieces), key=lambda step: -step.bit_length())
        self.group_pay = peers * self.pay
        self.piece = self.group_pay // self.pieces
        self.all_pay = self.groups * self.group_pay
        self.all_piece = self.groups * self.piece
        self.each = padded(peers * self.slots, 8)
        self.group_each = self.members * self.each
        self.partial = (self.group_each + EXTRA, 2 * self.half)

    def order(self):
        shape = (self.group_each, self.group_pay)
        row = lax.broadcasted_iota(I32, (self.group_each, 1), 0)
        expert, rest = divided(row, self.each)
        step, slot = divided(rest, self.slots)
        target = jnp.where(step < self.peers, step * self.pay + expert * self.slots + slot, -1)
        return one_hot(lax.broadcasted_iota(I32, shape, 1) == target).astype(BF16)


def line_up(z, ref):
    total = None
    for batch in range(z.micro):
        shape = (z.tok, z.rows)
        place = lax.broadcasted_iota(I32, shape, 1) == lax.broadcasted_iota(I32, shape, 0) + batch * z.tok
        value = dot(ref[batch].astype(F32).astype(BF16), one_hot(place).astype(BF16))
        total = value if total is None else total + value
    return total


def slot_hits(z, routes_ref):
    row = lax.broadcasted_iota(I32, (z.all_pay, 1), 0)
    step, rest = divided(row, z.groups * z.pay)
    group, place = divided(rest, z.pay)
    member, inside = divided(place, z.slots)
    batch, rank = divided(inside, CAP)
    rank = jnp.where(member < z.members, rank, -1)
    owner = step ^ lax.axis_index("expert") if z.pieces > 1 else step
    if z.units_dev >= FFE:
        expert = owner * z.local + group * z.members + member
    else:
        expert = lax.shift_right_logical(owner, (FFE // z.units_dev).bit_length() - 1)
    routes = line_up(z, routes_ref)
    token = lax.broadcasted_iota(I32, (z.all_pay, z.rows), 1)
    start = batch * z.tok
    same = (token >= start) & (token < start + z.tok)
    expert = expert.astype(F32)
    first = (routes[0:1, :] == expert) & same
    second = (routes[1:2, :] == expert) & same
    chosen = one_hot(first | second)
    shape = (z.rows, z.rows)
    before = lax.broadcasted_iota(I32, shape, 0) < lax.broadcasted_iota(I32, shape, 1)
    count = dot(chosen.astype(BF16), one_hot(before).astype(BF16))
    hits = jnp.where(count == rank.astype(F32), chosen, F32(0.0))
    return hits, first, second


def send_rows(z, hits, rows, outs, steps):
    hits = [hits[step * z.all_piece:(step + 1) * z.all_piece] for step in steps]
    value = dot(jnp.concatenate(hits, axis=0).astype(BF16), rows)
    for index, out in enumerate(outs):
        out[...] = value[index * z.all_piece:(index + 1) * z.all_piece].astype(BF16)


def near_kernel(z, routes_ref, rows_ref, *outs):
    hits, _, _ = slot_hits(z, routes_ref)
    send_rows(z, hits, rows_ref[...], outs, range(z.near))


def group_rows(z, group, pieces):
    result = []
    for piece in pieces:
        value = piece[...].astype(F32)
        for step in range(z.peers // z.pieces):
            low = (step * z.groups + group) * z.pay
            result.append(value[low:low + z.pay])
    return jnp.concatenate(result, axis=0)


def pack_kernel(z, *refs):
    sources, outs = refs[:3], refs[3:-4]
    routes_ref, gates_ref, rows_ref, sems = refs[-4:]
    copies = [
        pltpu.make_async_copy(source, target, sems.at[index])
        for index, (source, target) in enumerate(zip(sources, refs[-4:-1]))
    ]
    for copy in copies:
        copy.start()
    copies[0].wait()
    hits, first, second = slot_hits(z, routes_ref)
    copies[1].wait()
    gates = line_up(z, gates_ref)
    weight = jnp.where(first, gates[0:1, :], F32(0.0)) + jnp.where(second, gates[1:2, :], F32(0.0))
    outs[-1][...] = (hits * weight).astype(BF16)
    copies[2].wait()
    send_rows(z, hits, rows_ref[...], outs[:-1], range(z.pieces))


def load_kernel(z, parts, gate_up, *refs):
    outs, sems = refs[:-1], refs[-1]
    flat = gate_up.reshape(2 * z.width, z.units_dev)
    depth = 2 * z.width // parts
    copies = []
    for expert in range(z.local):
        for part in range(parts):
            rows = pl.ds(part * depth, depth)
            copies.append(
                pltpu.make_async_copy(
                    flat.at[rows, pl.ds(expert * z.units, z.units)],
                    outs[expert].at[rows],
                    sems.at[expert * parts + part],
                )
            )
    for copy in copies:
        copy.start()
    for copy in copies:
        copy.wait()


def load_down_kernel(z, group, down_proj, *refs):
    outs, sems = refs[:-1], refs[-1]
    copies = []
    for index in range(z.members):
        rows = pl.ds((group * z.members + index) * z.units, z.units)
        copies.append(pltpu.make_async_copy(down_proj.at[0, rows, :], outs[index], sems.at[index]))
    for copy in copies:
        copy.start()
    for copy in copies:
        copy.wait()


def split_sums(sums, lanes):
    high = sums.astype(BF16).astype(F32)
    row = lax.broadcasted_iota(I32, sums.shape, 0)
    both = jnp.where(row == 0, high, jnp.where(row == 1, sums - high, F32(0.0)))
    if both.shape[1] < lanes:
        both = jnp.concatenate([both, jnp.zeros((EXTRA, lanes - both.shape[1]), F32)], axis=1)
    return both


def up_kernel(z, group, *refs):
    weights, refs = refs[:z.members], refs[z.members:]
    received, refs = refs[:z.pieces], refs[z.pieces:]
    received = [received[z.listed.index(step)] for step in range(z.pieces)]
    own, *sent, spread, staged = refs
    rows = dot(z.order(), group_rows(z, group, received).astype(BF16))
    squares = rows * rows
    high = squares.astype(BF16)
    low = (squares - high.astype(F32)).astype(BF16)
    ones = jnp.ones((EXTRA, z.width), BF16)
    sums = dot(ones, high, ACROSS) + dot(ones, low, ACROSS)
    rows = rows.astype(BF16)
    block = 128
    shape = (block, 2 * block)
    target = lax.broadcasted_iota(I32, shape, 1) - 2 * lax.broadcasted_iota(I32, shape, 0)
    placing = [one_hot(target == side).astype(BF16) for side in range(2)]
    for piece in range(z.width // block):
        columns = slice(piece * block, (piece + 1) * block)
        gate, up = dot(rows[:, columns], placing[0]), dot(rows[:, columns], placing[1])
        for expert in range(z.members):
            here = slice(expert * z.each, (expert + 1) * z.each)
            both = jnp.concatenate([gate[here], up[here]], axis=0).astype(BF16)
            spread[expert, :, 2 * piece * block:2 * (piece + 1) * block] = both
    totals = [dot(spread[expert], weights[expert][...]) for expert in range(z.members)]
    extra = split_sums(sums, 2 * z.half)
    for side in range(2):
        columns = slice(side * z.half, (side + 1) * z.half)
        gate = jnp.concatenate([total[:z.each, columns] for total in totals], axis=0)
        up = jnp.concatenate([total[z.each:, columns] for total in totals], axis=0)
        staged[side, :z.group_each, :] = jnp.concatenate([gate, up], axis=1)
        staged[side, z.group_each:, :] = extra
    core = lax.axis_index("hidden") & 1
    own[...] = staged[core]
    rows = z.partial[0] // CUTS
    value = staged[1 - core]
    for index, out in enumerate(sent):
        out[...] = value[index * rows:(index + 1) * rows].astype(BF16)


def joined(z, refs):
    total = refs[0][...].astype(F32)
    for ref in refs[1:]:
        total = total + ref[...].astype(F32)
    products, extra = total[:z.group_each], total[z.group_each:]
    row = lax.broadcasted_iota(I32, extra.shape, 0)
    sums = jnp.sum(jnp.where(row < 2, extra, F32(0.0)), axis=0, keepdims=True)
    return products, sums


def pair_kernel(z, own, *refs):
    *other, out = refs
    products, sums = joined(z, [own[...], jnp.concatenate([ref[...].astype(F32) for ref in other], axis=0)])
    sums = split_sums(jnp.broadcast_to(sums, (EXTRA // 2, 2 * z.half)), 2 * z.half)
    out[...] = jnp.concatenate([products, sums], axis=0).astype(BF16)


def act_kernel(z, count, *refs):
    outs = refs[-count:]
    products, sums = joined(z, refs[:-count])
    shape = (z.group_each, z.group_each)
    diagonal = lax.broadcasted_iota(I32, shape, 0) == lax.broadcasted_iota(I32, shape, 1)
    sums = jnp.sum(jnp.where(diagonal, sums[:, :z.group_each], F32(0.0)), axis=1, keepdims=True)
    scale = lax.rsqrt(sums / D + EPS)
    gate = scale * products[:, :z.half]
    up = scale * products[:, z.half:]
    value = (gate / (F32(1.0) + jnp.exp(-gate)) * up).astype(BF16)
    rows = z.group_each // count
    for index, out in enumerate(outs):
        out[...] = value[index * rows:(index + 1) * rows]


def half_products(z, weights, units_refs, side):
    low = pl.multiple_of(side * z.half, z.half)
    units = jnp.concatenate([ref[...].astype(F32) for ref in units_refs], axis=0)
    results = []
    for expert in range(z.members):
        rows = units[expert * z.each:(expert + 1) * z.each].astype(BF16)
        results.append(dot(rows, weights[expert][pl.ds(low, z.half), :]))
    return jnp.concatenate(results, axis=0)


def own_down_kernel(z, *refs):
    weights, units_ref, out = refs[:z.members], refs[z.members:-1], refs[-1]
    out[...] = half_products(z, weights, units_ref, lax.axis_index("hidden") & 1)


def down_kernel(z, hands_on, *refs):
    weights, refs = refs[:z.members], refs[z.members:]
    units_ref, own_ref, outs = refs[:1], refs[1], refs[2:]
    if hands_on:
        outs[-1][...] = outs[0][...]
        outs = outs[1:-1]
    total = own_ref[...] + half_products(z, weights, units_ref, 1 - (lax.axis_index("hidden") & 1))
    value = dot(z.order(), total.astype(BF16), DOWN)
    low = 0
    for out in outs:
        out[...] = value[low:low + out.shape[0]].astype(BF16)
        low += out.shape[0]


def second_kernel(z, pair_ref, out):
    out[...] = pair_ref[...].astype(F32)[z.piece:].astype(BF16)


def combine_kernel(z, tick, last, weight_ref, rows_ref, kept_ref, *refs):
    count = z.groups * z.pieces
    returned, refs = [ref[...].astype(F32)[:z.piece] for ref in refs[:count]], refs[count:]
    stacked = []
    for piece in range(z.pieces):
        values = [returned[group * z.pieces + piece] for group in range(z.groups)]
        for step in range(z.peers // z.pieces):
            stacked += [value[step * z.pay:(step + 1) * z.pay] for value in values]
    stacked = jnp.concatenate(stacked, axis=0).astype(BF16)
    mixed = dot(weight_ref[...], stacked, DOWN)
    value = (rows_ref[...].astype(F32) + mixed).astype(BF16)
    if last:
        refs[0][...] = jnp.where(lax.axis_index("section") == tick, value, kept_ref[...])
        return
    routes_ref, out, outs = refs[0], refs[1], refs[2:]
    out[...] = jnp.where(lax.axis_index("section") == tick, value, kept_ref[...])
    hits, _, _ = slot_hits(z, routes_ref)
    send_rows(z, hits, value, outs, range(z.near, z.pieces))


def after_waits(waits, kernel, *refs):
    return kernel(*refs[waits:])


def call(kernel, sizes, megabytes, outs, in_specs, scratch, *args, waits=()):
    results = pl.pallas_call(
        functools.partial(after_waits, len(waits), functools.partial(kernel, *sizes)),
        out_shape=outs,
        in_specs=[VMEM] * len(waits) + in_specs,
        out_specs=[VMEM] * len(outs),
        scratch_shapes=scratch,
        compiler_params=pltpu.CompilerParams(vmem_limit_bytes=megabytes * 2**20),
    )(*waits, *args)
    return list(results)


def on_device(tokens, gate_up, down_proj, routes, gate_weights):
    sections = lax.axis_size("section")
    z = Sizes(tokens, gate_up, lax.axis_size("expert"), lax.axis_size("hidden"))
    parts = 2 if z.width % 256 == 0 else 1
    shape = jax.ShapeDtypeStruct
    pay = shape((z.piece, z.width), BF16)
    all_pay = shape((z.all_piece, z.width), BF16)
    merged = [pay, pay, shape((2 * z.piece, z.width), BF16)]
    whole = shape((z.rows, z.width), BF16)
    steps = sorted(range(z.peers), key=lambda step: -step.bit_length())

    def swap(value, step):
        pairs = [(i, i ^ step) for i in range(z.splits)]
        return lax.ppermute(value, "hidden", pairs)

    def exchanged(pieces):
        if z.pieces == 1:
            return [lax.all_to_all(pieces[0], "expert", split_axis=0, concat_axis=0, tiled=True)]
        result = list(pieces)
        for step in steps[:-1]:
            pairs = [(i, i ^ step) for i in range(z.peers)]
            result[step] = lax.ppermute(pieces[step], "expert", pairs)
        return result

    def across(value, step):
        return lax.ppermute(value, "expert", [(i, i ^ step) for i in range(z.peers)])

    def sent_back(pieces, group):
        if group >= z.pairs:
            return exchanged(pieces)
        own, near, far = pieces
        far = across(far, 2)
        second = call(second_kernel, (z,), 2, [pay], [VMEM], [], far)[0]
        return [own, across(near, 1), far, across(second, 1)]

    def within(value, step, section):
        low = section * z.peers
        pairs = [(low + i, low + (i ^ step)) for i in range(z.peers)]
        return lax.ppermute(value, ("section", "expert"), pairs)

    def relayed(pieces, kept, tick):
        hop = [(tick, tick + 1)]
        rows = lax.ppermute(kept, "section", hop)
        if z.pieces == 1:
            return rows, [lax.ppermute(exchanged(pieces)[0], "section", hop)]
        far = {}
        for step in steps:
            if step >= z.near:
                pairs = [(tick * z.peers + i, (tick + 1) * z.peers + (i ^ step)) for i in range(z.peers)]
                far[step] = lax.ppermute(pieces[step - z.near], ("section", "expert"), pairs)
        result = call(near_kernel, (z,), 4, [all_pay] * z.near, [VMEM] * 2, [], routes, rows)
        for step in range(1, z.near):
            result[step] = within(result[step], step, tick + 1)
        return rows, result + [far[step] for step in range(z.near, z.pieces)]

    def products(received, group, waits):
        own, *sent = call(
            up_kernel, (z, group), 6,
            [shape(z.partial, F32)] + [shape((z.partial[0] // CUTS, z.partial[1]), BF16)] * CUTS,
            [VMEM] * (z.members + z.pieces),
            [
                pltpu.VMEM((z.members, 2 * z.each, 2 * z.width), BF16),
                pltpu.VMEM((2,) + z.partial, F32),
            ],
            *wide[group * z.members:(group + 1) * z.members], *(received[step] for step in z.listed),
            waits=waits,
        )
        return own, [swap(value, 1) for value in sent]

    def pair_sums(own, other):
        pair = call(
            pair_kernel, (z,), 2, [shape((z.group_each + EXTRA // 2, 2 * z.half), BF16)], [VMEM] * (1 + CUTS), [], own, *other
        )[0]
        return [pair] + [swap(pair, step) for step in range(2, z.splits, 2)]

    def activated(pairs, waits):
        count = 1
        units = call(
            act_kernel, (z, count), 2,
            [shape((z.group_each // count, z.half), BF16)] * count, [VMEM] * len(pairs), [], *pairs, waits=waits,
        )
        return units, [swap(part, 1) for part in units]

    def down(halves, group, hand_on):
        own = call(
            own_down_kernel, (z,), 4, [shape((z.group_each, z.width), F32)],
            [VMEM] * (z.members + len(halves[0])), [], *tall[group], *halves[0],
        )[0]
        return call(
            down_kernel, (z, len(hand_on)), 4,
            (merged if group < z.pairs else [pay] * z.pieces)
            + [shape(value.shape, value.dtype) for value in hand_on],
            [VMEM] * (z.members + 1 + len(halves[1]) + len(hand_on)), [],
            *tall[group], *halves[1], own, *hand_on,
        )

    routes = routes[0].transpose(0, 2, 1)
    gates = gate_weights[0].transpose(0, 2, 1)
    rows = tokens.reshape(z.rows, z.width)
    kept = rows
    *sent, weight = call(
        pack_kernel, (z,), 3,
        [all_pay] * z.pieces + [shape((z.all_pay, z.rows), BF16)],
        [HBM] * 3,
        [
            pltpu.VMEM(routes.shape, routes.dtype),
            pltpu.VMEM(gates.shape, gates.dtype),
            pltpu.VMEM(rows.shape, rows.dtype),
            pltpu.SemaphoreType.DMA((3,)),
        ],
        *(pltpu.with_memory_space_constraint(value, pltpu.HBM) for value in (routes, gates, rows)),
    )
    received = exchanged(sent)
    gate_up = pltpu.with_memory_space_constraint(gate_up, pltpu.HBM)
    down_proj = pltpu.with_memory_space_constraint(down_proj, pltpu.HBM)
    wide = call(
        load_kernel, (z, parts), 1,
        [pltpu.VMEM((2 * z.width, z.units), BF16)] * z.local,
        [HBM], [pltpu.SemaphoreType.DMA((z.local * parts,))], gate_up, waits=[weight],
    )

    def load_down(group, after):
        return call(
            load_down_kernel, (z, group), 1,
            [pltpu.VMEM((z.units, z.width), BF16)] * z.members,
            [HBM], [pltpu.SemaphoreType.DMA((z.members,))], down_proj, waits=[after],
        )

    tall = [load_down(0, wide[-1])]
    groups = range(z.groups)
    for tick in range(sections):
        last = tick == sections - 1
        sums, returned = [], []
        for group in groups:
            own, other = products(received, group, [sums[-1][0]] if group else tall[0][:1])
            sums.append(pair_sums(own, other))
            if group == 0:
                halves = activated(sums[0], [])
        for group in groups:
            if group and tick == 0:
                tall.append(load_down(group, outgoing[0]))
            if group:
                halves = activated(sums[group], tall[group][:1] if tick == 0 else outgoing[:1])
            hand_on = [routes] if tick == 0 and group == z.groups - 1 else []
            outgoing = down(halves, group, hand_on)
            if hand_on:
                pairs = [(i + 1, i) for i in range(sections - 1)]
                following = lax.ppermute(outgoing.pop(), "section", pairs)
            returned.append(sent_back(outgoing, group))
        returned = sum(returned, [])
        kept, *sent = call(
            combine_kernel, (z, tick, last), 4,
            [whole] if last else [whole] + [all_pay] * (z.pieces - z.near),
            [VMEM] * (3 + len(returned) + (not last)), [],
            weight, rows, kept, *returned, *([] if last else [following]),
        )
        if not last:
            rows, received = relayed(sent, kept, tick)
    return kept.reshape(1, z.micro, z.tok, z.width)


def solution(mesh):
    placed = (
        P(None, "expert", "hidden"),
        P("section", "hidden", None, "expert"),
        P("section", "expert", "hidden"),
        P("section", None, "expert", None),
        P("section", None, "expert", None),
    )
    return jax.shard_map(
        on_device,
        mesh=mesh,
        in_specs=placed,
        out_specs=P("section", None, "expert", "hidden"),
        check_vma=False,
    )
```

```python
import functools

import jax
import jax.numpy as jnp
from jax import lax
from jax.experimental import pallas as pl
from jax.experimental.pallas import tpu as pltpu
from jax.sharding import PartitionSpec as P

D = 7168
FFE = 1024
CAP = 3
EPS = 1e-06
EXTRA = 16
CUTS = 2
VMEM = pl.BlockSpec(memory_space=pltpu.VMEM)
HBM = pl.BlockSpec(memory_space=pltpu.HBM)
BF16 = jnp.bfloat16
F32 = jnp.float32
I32 = jnp.int32
ACROSS = (((1,), (1,)), ((), ()))
DOWN = (((0,), (0,)), ((), ()))


def padded(count, unit):
    return -(-count // unit) * unit


def dot(a, b, dims=(((1,), (0,)), ((), ()))):
    return lax.dot_general(a, b, dims, preferred_element_type=F32)


def one_hot(mask):
    return jnp.where(mask, F32(1.0), F32(0.0))


def divided(value, divisor):
    if divisor == 1:
        return value, jnp.zeros_like(value)
    quotient = lax.shift_right_logical(value * (2**20 // divisor + 1), 20)
    return quotient, value - quotient * divisor


class Sizes:
    def __init__(self, tokens, gate_up, peers, splits):
        self.peers, self.splits = peers, splits
        self.micro, self.tok, self.width = tokens.shape
        self.rows = self.micro * self.tok
        self.units_dev = gate_up.shape[3]
        self.units = min(FFE, self.units_dev)
        self.half = self.units // 2
        self.local = self.units_dev // self.units
        self.groups = 2 if self.local % 2 == 0 else 1
        self.members = self.local // self.groups
        self.slots = self.micro * CAP
        self.pay = padded(self.members * self.slots, 8)
        self.pieces = peers if peers <= 8 else 1
        self.pairs = self.groups - 1 if self.pieces == 4 else 0
        self.near = self.pieces // 2
        self.listed = sorted(range(self.pieces), key=lambda step: -step.bit_length())
        self.group_pay = peers * self.pay
        self.piece = self.group_pay // self.pieces
        self.all_pay = self.groups * self.group_pay
        self.all_piece = self.groups * self.piece
        self.each = padded(peers * self.slots, 8)
        self.group_each = self.members * self.each
        self.partial = (self.group_each + EXTRA, 2 * self.half)

    def order(self):
        shape = (self.group_each, self.group_pay)
        row = lax.broadcasted_iota(I32, (self.group_each, 1), 0)
        expert, rest = divided(row, self.each)
        step, slot = divided(rest, self.slots)
        target = jnp.where(step < self.peers, step * self.pay + expert * self.slots + slot, -1)
        return one_hot(lax.broadcasted_iota(I32, shape, 1) == target).astype(BF16)


def line_up(z, ref):
    total = None
    for batch in range(z.micro):
        shape = (z.tok, z.rows)
        place = lax.broadcasted_iota(I32, shape, 1) == lax.broadcasted_iota(I32, shape, 0) + batch * z.tok
        value = dot(ref[batch].astype(F32).astype(BF16), one_hot(place).astype(BF16))
        total = value if total is None else total + value
    return total


def slot_hits(z, routes_ref):
    row = lax.broadcasted_iota(I32, (z.all_pay, 1), 0)
    step, rest = divided(row, z.groups * z.pay)
    group, place = divided(rest, z.pay)
    member, inside = divided(place, z.slots)
    batch, rank = divided(inside, CAP)
    rank = jnp.where(member < z.members, rank, -1)
    owner = step ^ lax.axis_index("expert") if z.pieces > 1 else step
    if z.units_dev >= FFE:
        expert = owner * z.local + group * z.members + member
    else:
        expert = lax.shift_right_logical(owner, (FFE // z.units_dev).bit_length() - 1)
    routes = line_up(z, routes_ref)
    token = lax.broadcasted_iota(I32, (z.all_pay, z.rows), 1)
    start = batch * z.tok
    same = (token >= start) & (token < start + z.tok)
    expert = expert.astype(F32)
    first = (routes[0:1, :] == expert) & same
    second = (routes[1:2, :] == expert) & same
    chosen = one_hot(first | second)
    shape = (z.rows, z.rows)
    before = lax.broadcasted_iota(I32, shape, 0) < lax.broadcasted_iota(I32, shape, 1)
    count = dot(chosen.astype(BF16), one_hot(before).astype(BF16))
    hits = jnp.where(count == rank.astype(F32), chosen, F32(0.0))
    return hits, first, second


def send_rows(z, hits, rows, outs, steps):
    hits = [hits[step * z.all_piece:(step + 1) * z.all_piece] for step in steps]
    value = dot(jnp.concatenate(hits, axis=0).astype(BF16), rows)
    for index, out in enumerate(outs):
        out[...] = value[index * z.all_piece:(index + 1) * z.all_piece].astype(BF16)


def near_kernel(z, routes_ref, rows_ref, *outs):
    hits, _, _ = slot_hits(z, routes_ref)
    send_rows(z, hits, rows_ref[...], outs, range(z.near))


def group_rows(z, group, pieces):
    result = []
    for piece in pieces:
        value = piece[...].astype(F32)
        for step in range(z.peers // z.pieces):
            low = (step * z.groups + group) * z.pay
            result.append(value[low:low + z.pay])
    return jnp.concatenate(result, axis=0)


def pack_kernel(z, *refs):
    sources, outs = refs[:3], refs[3:-4]
    routes_ref, gates_ref, rows_ref, sems = refs[-4:]
    copies = [
        pltpu.make_async_copy(source, target, sems.at[index])
        for index, (source, target) in enumerate(zip(sources, refs[-4:-1]))
    ]
    for copy in copies:
        copy.start()
    copies[0].wait()
    hits, first, second = slot_hits(z, routes_ref)
    copies[1].wait()
    gates = line_up(z, gates_ref)
    weight = jnp.where(first, gates[0:1, :], F32(0.0)) + jnp.where(second, gates[1:2, :], F32(0.0))
    outs[-1][...] = (hits * weight).astype(BF16)
    copies[2].wait()
    send_rows(z, hits, rows_ref[...], outs[:-1], range(z.pieces))


def load_kernel(z, parts, experts, gate_up, *refs):
    outs, sems = refs[:-1], refs[-1]
    flat = gate_up.reshape(2 * z.width, z.units_dev)
    depth = 2 * z.width // parts
    copies = []
    for index, expert in enumerate(experts):
        for part in range(parts):
            rows = pl.ds(part * depth, depth)
            copies.append(
                pltpu.make_async_copy(
                    flat.at[rows, pl.ds(expert * z.units, z.units)],
                    outs[index].at[rows],
                    sems.at[index * parts + part],
                )
            )
    for copy in copies:
        copy.start()
    for copy in copies:
        copy.wait()


def load_down_kernel(z, group, down_proj, *refs):
    outs, sems = refs[:-1], refs[-1]
    copies = []
    for index in range(z.members):
        rows = pl.ds((group * z.members + index) * z.units, z.units)
        copies.append(pltpu.make_async_copy(down_proj.at[0, rows, :], outs[index], sems.at[index]))
    for copy in copies:
        copy.start()
    for copy in copies:
        copy.wait()


def split_sums(sums, lanes):
    high = sums.astype(BF16).astype(F32)
    row = lax.broadcasted_iota(I32, sums.shape, 0)
    both = jnp.where(row == 0, high, jnp.where(row == 1, sums - high, F32(0.0)))
    if both.shape[1] < lanes:
        both = jnp.concatenate([both, jnp.zeros((EXTRA, lanes - both.shape[1]), F32)], axis=1)
    return both


def up_kernel(z, group, *refs):
    weights, refs = refs[:z.members], refs[z.members:]
    received, refs = refs[:z.pieces], refs[z.pieces:]
    received = [received[z.listed.index(step)] for step in range(z.pieces)]
    own, *sent, spread, staged = refs
    rows = dot(z.order(), group_rows(z, group, received).astype(BF16))
    squares = rows * rows
    high = squares.astype(BF16)
    low = (squares - high.astype(F32)).astype(BF16)
    ones = jnp.ones((EXTRA, z.width), BF16)
    sums = dot(ones, high, ACROSS) + dot(ones, low, ACROSS)
    rows = rows.astype(BF16)
    block = 128
    shape = (block, 2 * block)
    target = lax.broadcasted_iota(I32, shape, 1) - 2 * lax.broadcasted_iota(I32, shape, 0)
    placing = [one_hot(target == side).astype(BF16) for side in range(2)]
    for piece in range(z.width // block):
        columns = slice(piece * block, (piece + 1) * block)
        gate, up = dot(rows[:, columns], placing[0]), dot(rows[:, columns], placing[1])
        for expert in range(z.members):
            here = slice(expert * z.each, (expert + 1) * z.each)
            both = jnp.concatenate([gate[here], up[here]], axis=0).astype(BF16)
            spread[expert, :, 2 * piece * block:2 * (piece + 1) * block] = both
    totals = [dot(spread[expert], weights[expert][...]) for expert in range(z.members)]
    extra = split_sums(sums, 2 * z.half)
    for side in range(2):
        columns = slice(side * z.half, (side + 1) * z.half)
        gate = jnp.concatenate([total[:z.each, columns] for total in totals], axis=0)
        up = jnp.concatenate([total[z.each:, columns] for total in totals], axis=0)
        staged[side, :z.group_each, :] = jnp.concatenate([gate, up], axis=1)
        staged[side, z.group_each:, :] = extra
    core = lax.axis_index("hidden") & 1
    own[...] = staged[core]
    rows = z.partial[0] // CUTS
    value = staged[1 - core]
    for index, out in enumerate(sent):
        out[...] = value[index * rows:(index + 1) * rows].astype(BF16)


def joined(z, refs):
    total = refs[0][...].astype(F32)
    for ref in refs[1:]:
        total = total + ref[...].astype(F32)
    products, extra = total[:z.group_each], total[z.group_each:]
    row = lax.broadcasted_iota(I32, extra.shape, 0)
    sums = jnp.sum(jnp.where(row < 2, extra, F32(0.0)), axis=0, keepdims=True)
    return products, sums


def pair_kernel(z, own, *refs):
    *other, out = refs
    products, sums = joined(z, [own[...], jnp.concatenate([ref[...].astype(F32) for ref in other], axis=0)])
    sums = split_sums(jnp.broadcast_to(sums, (EXTRA // 2, 2 * z.half)), 2 * z.half)
    out[...] = jnp.concatenate([products, sums], axis=0).astype(BF16)


def act_kernel(z, count, *refs):
    outs = refs[-count:]
    products, sums = joined(z, refs[:-count])
    shape = (z.group_each, z.group_each)
    diagonal = lax.broadcasted_iota(I32, shape, 0) == lax.broadcasted_iota(I32, shape, 1)
    sums = jnp.sum(jnp.where(diagonal, sums[:, :z.group_each], F32(0.0)), axis=1, keepdims=True)
    scale = lax.rsqrt(sums / D + EPS)
    gate = scale * products[:, :z.half]
    up = scale * products[:, z.half:]
    value = (gate / (F32(1.0) + jnp.exp(-gate)) * up).astype(BF16)
    rows = z.group_each // count
    for index, out in enumerate(outs):
        out[...] = value[index * rows:(index + 1) * rows]


def half_products(z, weights, units_refs, side):
    low = pl.multiple_of(side * z.half, z.half)
    units = jnp.concatenate([ref[...].astype(F32) for ref in units_refs], axis=0)
    results = []
    for expert in range(z.members):
        rows = units[expert * z.each:(expert + 1) * z.each].astype(BF16)
        results.append(dot(rows, weights[expert][pl.ds(low, z.half), :]))
    return jnp.concatenate(results, axis=0)


def own_down_kernel(z, *refs):
    weights, units_ref, out = refs[:z.members], refs[z.members:-1], refs[-1]
    out[...] = half_products(z, weights, units_ref, lax.axis_index("hidden") & 1)


def down_kernel(z, hands_on, *refs):
    weights, refs = refs[:z.members], refs[z.members:]
    units_ref, own_ref, outs = refs[:1], refs[1], refs[2:]
    if hands_on:
        outs[-1][...] = outs[0][...]
        outs = outs[1:-1]
    total = own_ref[...] + half_products(z, weights, units_ref, 1 - (lax.axis_index("hidden") & 1))
    value = dot(z.order(), total.astype(BF16), DOWN)
    low = 0
    for out in outs:
        out[...] = value[low:low + out.shape[0]].astype(BF16)
        low += out.shape[0]


def second_kernel(z, pair_ref, out):
    out[...] = pair_ref[...].astype(F32)[z.piece:].astype(BF16)


def combine_kernel(z, tick, last, weight_ref, rows_ref, kept_ref, *refs):
    count = z.groups * z.pieces
    returned, refs = [ref[...].astype(F32)[:z.piece] for ref in refs[:count]], refs[count:]
    stacked = []
    for piece in range(z.pieces):
        values = [returned[group * z.pieces + piece] for group in range(z.groups)]
        for step in range(z.peers // z.pieces):
            stacked += [value[step * z.pay:(step + 1) * z.pay] for value in values]
    stacked = jnp.concatenate(stacked, axis=0).astype(BF16)
    mixed = dot(weight_ref[...], stacked, DOWN)
    value = (rows_ref[...].astype(F32) + mixed).astype(BF16)
    if last:
        refs[0][...] = jnp.where(lax.axis_index("section") == tick, value, kept_ref[...])
        return
    routes_ref, out, outs = refs[0], refs[1], refs[2:]
    out[...] = jnp.where(lax.axis_index("section") == tick, value, kept_ref[...])
    hits, _, _ = slot_hits(z, routes_ref)
    send_rows(z, hits, value, outs, range(z.near, z.pieces))


def after_waits(waits, kernel, *refs):
    return kernel(*refs[waits:])


def call(kernel, sizes, megabytes, outs, in_specs, scratch, *args, waits=()):
    results = pl.pallas_call(
        functools.partial(after_waits, len(waits), functools.partial(kernel, *sizes)),
        out_shape=outs,
        in_specs=[VMEM] * len(waits) + in_specs,
        out_specs=[VMEM] * len(outs),
        scratch_shapes=scratch,
        compiler_params=pltpu.CompilerParams(vmem_limit_bytes=megabytes * 2**20),
    )(*waits, *args)
    return list(results)


def on_device(tokens, gate_up, down_proj, routes, gate_weights):
    sections = lax.axis_size("section")
    z = Sizes(tokens, gate_up, lax.axis_size("expert"), lax.axis_size("hidden"))
    parts = 2 if z.width % 256 == 0 else 1
    shape = jax.ShapeDtypeStruct
    pay = shape((z.piece, z.width), BF16)
    all_pay = shape((z.all_piece, z.width), BF16)
    merged = [pay, pay, shape((2 * z.piece, z.width), BF16)]
    whole = shape((z.rows, z.width), BF16)
    steps = sorted(range(z.peers), key=lambda step: -step.bit_length())

    def swap(value, step):
        pairs = [(i, i ^ step) for i in range(z.splits)]
        return lax.ppermute(value, "hidden", pairs)

    def exchanged(pieces):
        if z.pieces == 1:
            return [lax.all_to_all(pieces[0], "expert", split_axis=0, concat_axis=0, tiled=True)]
        result = list(pieces)
        for step in steps[:-1]:
            pairs = [(i, i ^ step) for i in range(z.peers)]
            result[step] = lax.ppermute(pieces[step], "expert", pairs)
        return result

    def across(value, step):
        return lax.ppermute(value, "expert", [(i, i ^ step) for i in range(z.peers)])

    def sent_back(pieces, group):
        if group >= z.pairs:
            return exchanged(pieces)
        own, near, far = pieces
        far = across(far, 2)
        second = call(second_kernel, (z,), 2, [pay], [VMEM], [], far)[0]
        return [own, across(near, 1), far, across(second, 1)]

    def within(value, step, section):
        low = section * z.peers
        pairs = [(low + i, low + (i ^ step)) for i in range(z.peers)]
        return lax.ppermute(value, ("section", "expert"), pairs)

    def relayed(pieces, kept, tick):
        hop = [(tick, tick + 1)]
        rows = lax.ppermute(kept, "section", hop)
        if z.pieces == 1:
            return rows, [lax.ppermute(exchanged(pieces)[0], "section", hop)]
        far = {}
        for step in steps:
            if step >= z.near:
                pairs = [(tick * z.peers + i, (tick + 1) * z.peers + (i ^ step)) for i in range(z.peers)]
                far[step] = lax.ppermute(pieces[step - z.near], ("section", "expert"), pairs)
        result = call(near_kernel, (z,), 4, [all_pay] * z.near, [VMEM] * 2, [], routes, rows)
        for step in range(1, z.near):
            result[step] = within(result[step], step, tick + 1)
        return rows, result + [far[step] for step in range(z.near, z.pieces)]

    def products(received, group, waits):
        own, *sent = call(
            up_kernel, (z, group), 6,
            [shape(z.partial, F32)] + [shape((z.partial[0] // CUTS, z.partial[1]), BF16)] * CUTS,
            [VMEM] * (z.members + z.pieces),
            [
                pltpu.VMEM((z.members, 2 * z.each, 2 * z.width), BF16),
                pltpu.VMEM((2,) + z.partial, F32),
            ],
            *wide[group * z.members:(group + 1) * z.members], *(received[step] for step in z.listed),
            waits=waits,
        )
        return own, [swap(value, 1) for value in sent]

    def pair_sums(own, other):
        pair = call(
            pair_kernel, (z,), 2, [shape((z.group_each + EXTRA // 2, 2 * z.half), BF16)], [VMEM] * (1 + CUTS), [], own, *other
        )[0]
        return [pair] + [swap(pair, step) for step in range(2, z.splits, 2)]

    def activated(pairs, waits):
        count = 1
        units = call(
            act_kernel, (z, count), 2,
            [shape((z.group_each // count, z.half), BF16)] * count, [VMEM] * len(pairs), [], *pairs, waits=waits,
        )
        return units, [swap(part, 1) for part in units]

    def down(halves, group, hand_on):
        own = call(
            own_down_kernel, (z,), 4, [shape((z.group_each, z.width), F32)],
            [VMEM] * (z.members + len(halves[0])), [], *tall[group], *halves[0],
        )[0]
        return call(
            down_kernel, (z, len(hand_on)), 4,
            (merged if group < z.pairs else [pay] * z.pieces)
            + [shape(value.shape, value.dtype) for value in hand_on],
            [VMEM] * (z.members + 1 + len(halves[1]) + len(hand_on)), [],
            *tall[group], *halves[1], own, *hand_on,
        )

    routes = routes[0].transpose(0, 2, 1)
    gates = gate_weights[0].transpose(0, 2, 1)
    rows = tokens.reshape(z.rows, z.width)
    kept = rows
    *sent, weight = call(
        pack_kernel, (z,), 3,
        [all_pay] * z.pieces + [shape((z.all_pay, z.rows), BF16)],
        [HBM] * 3,
        [
            pltpu.VMEM(routes.shape, routes.dtype),
            pltpu.VMEM(gates.shape, gates.dtype),
            pltpu.VMEM(rows.shape, rows.dtype),
            pltpu.SemaphoreType.DMA((3,)),
        ],
        *(pltpu.with_memory_space_constraint(value, pltpu.HBM) for value in (routes, gates, rows)),
    )
    received = exchanged(sent)
    gate_up = pltpu.with_memory_space_constraint(gate_up, pltpu.HBM)
    down_proj = pltpu.with_memory_space_constraint(down_proj, pltpu.HBM)
    def load(experts, after):
        return call(
            load_kernel, (z, parts, experts), 1,
            [pltpu.VMEM((2 * z.width, z.units), BF16)] * len(experts),
            [HBM], [pltpu.SemaphoreType.DMA((len(experts) * parts,))], gate_up, waits=[after],
        )

    wide = load(range(z.local), weight)

    def load_down(group, after):
        return call(
            load_down_kernel, (z, group), 1,
            [pltpu.VMEM((z.units, z.width), BF16)] * z.members,
            [HBM], [pltpu.SemaphoreType.DMA((z.members,))], down_proj, waits=[after],
        )

    tall = [load_down(0, wide[-1])]
    groups = range(z.groups)
    for tick in range(sections):
        last = tick == sections - 1
        sums, returned = [], []
        for group in groups:
            own, other = products(received, group, [sums[-1][0]] if group else tall[0][:1])
            sums.append(pair_sums(own, other))
            if group == 0:
                halves = activated(sums[0], [])
        for group in groups:
            if group and tick == 0:
                tall.append(load_down(group, outgoing[0]))
            if group:
                halves = activated(sums[group], tall[group][:1] if tick == 0 else outgoing[:1])
            hand_on = [routes] if tick == 0 and group == z.groups - 1 else []
            outgoing = down(halves, group, hand_on)
            if hand_on:
                pairs = [(i + 1, i) for i in range(sections - 1)]
                following = lax.ppermute(outgoing.pop(), "section", pairs)
            returned.append(sent_back(outgoing, group))
        returned = sum(returned, [])
        kept, *sent = call(
            combine_kernel, (z, tick, last), 4,
            [whole] if last else [whole] + [all_pay] * (z.pieces - z.near),
            [VMEM] * (3 + len(returned) + (not last)), [],
            weight, rows, kept, *returned, *([] if last else [following]),
        )
        if not last:
            rows, received = relayed(sent, kept, tick)
            wide[0:1] = load(range(0, 1), kept)
    return kept.reshape(1, z.micro, z.tok, z.width)


def solution(mesh):
    placed = (
        P(None, "expert", "hidden"),
        P("section", "hidden", None, "expert"),
        P("section", "expert", "hidden"),
        P("section", None, "expert", None),
        P("section", None, "expert", None),
    )
    return jax.shard_map(
        on_device,
        mesh=mesh,
        in_specs=placed,
        out_specs=P("section", None, "expert", "hidden"),
        check_vma=False,
    )
```

```python
import functools

import jax
import jax.numpy as jnp
from jax import lax
from jax.experimental import pallas as pl
from jax.experimental.pallas import tpu as pltpu
from jax.sharding import PartitionSpec as P

D = 7168
FFE = 1024
CAP = 3
EPS = 1e-06
EXTRA = 16
CUTS = 2
VMEM = pl.BlockSpec(memory_space=pltpu.VMEM)
HBM = pl.BlockSpec(memory_space=pltpu.HBM)
BF16 = jnp.bfloat16
F32 = jnp.float32
I32 = jnp.int32
ACROSS = (((1,), (1,)), ((), ()))
DOWN = (((0,), (0,)), ((), ()))


def padded(count, unit):
    return -(-count // unit) * unit


def dot(a, b, dims=(((1,), (0,)), ((), ()))):
    return lax.dot_general(a, b, dims, preferred_element_type=F32)


def one_hot(mask):
    return jnp.where(mask, F32(1.0), F32(0.0))


def divided(value, divisor):
    if divisor == 1:
        return value, jnp.zeros_like(value)
    quotient = lax.shift_right_logical(value * (2**20 // divisor + 1), 20)
    return quotient, value - quotient * divisor


class Sizes:
    def __init__(self, tokens, gate_up, peers, splits):
        self.peers, self.splits = peers, splits
        self.micro, self.tok, self.width = tokens.shape
        self.rows = self.micro * self.tok
        self.units_dev = gate_up.shape[3]
        self.units = min(FFE, self.units_dev)
        self.half = self.units // 2
        self.local = self.units_dev // self.units
        self.groups = 2 if self.local % 2 == 0 else 1
        self.members = self.local // self.groups
        self.slots = self.micro * CAP
        self.pay = padded(self.members * self.slots, 8)
        self.pieces = peers if peers <= 8 else 1
        self.pairs = self.groups - 1 if self.pieces == 4 else 0
        self.near = self.pieces // 2
        self.listed = sorted(range(self.pieces), key=lambda step: -step.bit_length())
        self.group_pay = peers * self.pay
        self.piece = self.group_pay // self.pieces
        self.all_pay = self.groups * self.group_pay
        self.all_piece = self.groups * self.piece
        self.each = padded(peers * self.slots, 8)
        self.group_each = self.members * self.each
        self.partial = (self.group_each + EXTRA, 2 * self.half)

    def order(self):
        shape = (self.group_each, self.group_pay)
        row = lax.broadcasted_iota(I32, (self.group_each, 1), 0)
        expert, rest = divided(row, self.each)
        step, slot = divided(rest, self.slots)
        target = jnp.where(step < self.peers, step * self.pay + expert * self.slots + slot, -1)
        return one_hot(lax.broadcasted_iota(I32, shape, 1) == target).astype(BF16)


def line_up(z, ref):
    total = None
    for batch in range(z.micro):
        shape = (z.tok, z.rows)
        place = lax.broadcasted_iota(I32, shape, 1) == lax.broadcasted_iota(I32, shape, 0) + batch * z.tok
        value = dot(ref[batch].astype(F32).astype(BF16), one_hot(place).astype(BF16))
        total = value if total is None else total + value
    return total


def slot_hits(z, routes_ref):
    row = lax.broadcasted_iota(I32, (z.all_pay, 1), 0)
    step, rest = divided(row, z.groups * z.pay)
    group, place = divided(rest, z.pay)
    member, inside = divided(place, z.slots)
    batch, rank = divided(inside, CAP)
    rank = jnp.where(member < z.members, rank, -1)
    owner = step ^ lax.axis_index("expert") if z.pieces > 1 else step
    if z.units_dev >= FFE:
        expert = owner * z.local + group * z.members + member
    else:
        expert = lax.shift_right_logical(owner, (FFE // z.units_dev).bit_length() - 1)
    routes = line_up(z, routes_ref)
    token = lax.broadcasted_iota(I32, (z.all_pay, z.rows), 1)
    start = batch * z.tok
    same = (token >= start) & (token < start + z.tok)
    expert = expert.astype(F32)
    first = (routes[0:1, :] == expert) & same
    second = (routes[1:2, :] == expert) & same
    chosen = one_hot(first | second)
    shape = (z.rows, z.rows)
    before = lax.broadcasted_iota(I32, shape, 0) < lax.broadcasted_iota(I32, shape, 1)
    count = dot(chosen.astype(BF16), one_hot(before).astype(BF16))
    hits = jnp.where(count == rank.astype(F32), chosen, F32(0.0))
    return hits, first, second


def send_rows(z, hits, rows, outs, steps):
    hits = [hits[step * z.all_piece:(step + 1) * z.all_piece] for step in steps]
    value = dot(jnp.concatenate(hits, axis=0).astype(BF16), rows)
    for index, out in enumerate(outs):
        out[...] = value[index * z.all_piece:(index + 1) * z.all_piece].astype(BF16)


def near_kernel(z, routes_ref, rows_ref, *outs):
    hits, _, _ = slot_hits(z, routes_ref)
    send_rows(z, hits, rows_ref[...], outs, range(z.near))


def group_rows(z, group, pieces):
    result = []
    for piece in pieces:
        value = piece[...].astype(F32)
        for step in range(z.peers // z.pieces):
            low = (step * z.groups + group) * z.pay
            result.append(value[low:low + z.pay])
    return jnp.concatenate(result, axis=0)


def pack_kernel(z, *refs):
    sources, outs = refs[:3], refs[3:-4]
    routes_ref, gates_ref, rows_ref, sems = refs[-4:]
    copies = [
        pltpu.make_async_copy(source, target, sems.at[index])
        for index, (source, target) in enumerate(zip(sources, refs[-4:-1]))
    ]
    for copy in copies:
        copy.start()
    copies[0].wait()
    hits, first, second = slot_hits(z, routes_ref)
    copies[1].wait()
    gates = line_up(z, gates_ref)
    weight = jnp.where(first, gates[0:1, :], F32(0.0)) + jnp.where(second, gates[1:2, :], F32(0.0))
    outs[-1][...] = (hits * weight).astype(BF16)
    copies[2].wait()
    send_rows(z, hits, rows_ref[...], outs[:-1], range(z.pieces))


def load_kernel(z, parts, experts, gate_up, *refs):
    outs, sems = refs[:-1], refs[-1]
    flat = gate_up.reshape(2 * z.width, z.units_dev)
    depth = 2 * z.width // parts
    copies = []
    for index, expert in enumerate(experts):
        for part in range(parts):
            rows = pl.ds(part * depth, depth)
            copies.append(
                pltpu.make_async_copy(
                    flat.at[rows, pl.ds(expert * z.units, z.units)],
                    outs[index].at[rows],
                    sems.at[index * parts + part],
                )
            )
    for copy in copies:
        copy.start()
    for copy in copies:
        copy.wait()


def load_down_kernel(z, group, down_proj, *refs):
    outs, sems = refs[:-1], refs[-1]
    copies = []
    for index in range(z.members):
        rows = pl.ds((group * z.members + index) * z.units, z.units)
        copies.append(pltpu.make_async_copy(down_proj.at[0, rows, :], outs[index], sems.at[index]))
    for copy in copies:
        copy.start()
    for copy in copies:
        copy.wait()


def split_sums(sums, lanes):
    high = sums.astype(BF16).astype(F32)
    row = lax.broadcasted_iota(I32, sums.shape, 0)
    both = jnp.where(row == 0, high, jnp.where(row == 1, sums - high, F32(0.0)))
    if both.shape[1] < lanes:
        both = jnp.concatenate([both, jnp.zeros((EXTRA, lanes - both.shape[1]), F32)], axis=1)
    return both


def up_kernel(z, group, *refs):
    weights, refs = refs[:z.members], refs[z.members:]
    received, refs = refs[:z.pieces], refs[z.pieces:]
    received = [received[z.listed.index(step)] for step in range(z.pieces)]
    own, *sent, spread = refs
    rows = dot(z.order(), group_rows(z, group, received).astype(BF16))
    squares = rows * rows
    high = squares.astype(BF16)
    low = (squares - high.astype(F32)).astype(BF16)
    ones = jnp.ones((EXTRA, z.width), BF16)
    sums = dot(ones, high, ACROSS) + dot(ones, low, ACROSS)
    rows = rows.astype(BF16)
    block = 128
    shape = (block, 2 * block)
    target = lax.broadcasted_iota(I32, shape, 1) - 2 * lax.broadcasted_iota(I32, shape, 0)
    placing = [one_hot(target == side).astype(BF16) for side in range(2)]
    for piece in range(z.width // block):
        columns = slice(piece * block, (piece + 1) * block)
        gate, up = dot(rows[:, columns], placing[0]), dot(rows[:, columns], placing[1])
        for expert in range(z.members):
            here = slice(expert * z.each, (expert + 1) * z.each)
            both = jnp.concatenate([gate[here], up[here]], axis=0).astype(BF16)
            spread[expert, :, 2 * piece * block:2 * (piece + 1) * block] = both
    totals = [dot(spread[expert], weights[expert][...]) for expert in range(z.members)]
    extra = split_sums(sums, 2 * z.half)
    sides = []
    for side in range(2):
        columns = slice(side * z.half, (side + 1) * z.half)
        gate = jnp.concatenate([total[:z.each, columns] for total in totals], axis=0)
        up = jnp.concatenate([total[z.each:, columns] for total in totals], axis=0)
        sides.append(jnp.concatenate([jnp.concatenate([gate, up], axis=1), extra], axis=0))
    first = (lax.axis_index("hidden") & 1) == 0
    own[...] = jnp.where(first, sides[0], sides[1])
    value, rows = jnp.where(first, sides[1], sides[0]), z.partial[0] // CUTS
    for index, out in enumerate(sent):
        out[...] = value[index * rows:(index + 1) * rows].astype(BF16)


def joined(z, refs):
    total = refs[0][...].astype(F32)
    for ref in refs[1:]:
        total = total + ref[...].astype(F32)
    products, extra = total[:z.group_each], total[z.group_each:]
    row = lax.broadcasted_iota(I32, extra.shape, 0)
    sums = jnp.sum(jnp.where(row < 2, extra, F32(0.0)), axis=0, keepdims=True)
    return products, sums


def pair_kernel(z, own, *refs):
    *other, out = refs
    products, sums = joined(z, [own[...], jnp.concatenate([ref[...].astype(F32) for ref in other], axis=0)])
    sums = split_sums(jnp.broadcast_to(sums, (EXTRA // 2, 2 * z.half)), 2 * z.half)
    out[...] = jnp.concatenate([products, sums], axis=0).astype(BF16)


def act_kernel(z, count, *refs):
    outs = refs[-count:]
    products, sums = joined(z, refs[:-count])
    shape = (z.group_each, z.group_each)
    diagonal = lax.broadcasted_iota(I32, shape, 0) == lax.broadcasted_iota(I32, shape, 1)
    sums = jnp.sum(jnp.where(diagonal, sums[:, :z.group_each], F32(0.0)), axis=1, keepdims=True)
    scale = lax.rsqrt(sums / D + EPS)
    gate = scale * products[:, :z.half]
    up = scale * products[:, z.half:]
    value = (gate / (F32(1.0) + jnp.exp(-gate)) * up).astype(BF16)
    rows = z.group_each // count
    for index, out in enumerate(outs):
        out[...] = value[index * rows:(index + 1) * rows]


def half_products(z, weights, units_refs, side):
    low = pl.multiple_of(side * z.half, z.half)
    units = jnp.concatenate([ref[...].astype(F32) for ref in units_refs], axis=0)
    results = []
    for expert in range(z.members):
        rows = units[expert * z.each:(expert + 1) * z.each].astype(BF16)
        results.append(dot(rows, weights[expert][pl.ds(low, z.half), :]))
    return jnp.concatenate(results, axis=0)


def own_down_kernel(z, *refs):
    weights, units_ref, out = refs[:z.members], refs[z.members:-1], refs[-1]
    out[...] = half_products(z, weights, units_ref, lax.axis_index("hidden") & 1)


def down_kernel(z, hands_on, *refs):
    weights, refs = refs[:z.members], refs[z.members:]
    units_ref, own_ref, outs = refs[:1], refs[1], refs[2:]
    if hands_on:
        outs[-1][...] = outs[0][...]
        outs = outs[1:-1]
    total = own_ref[...] + half_products(z, weights, units_ref, 1 - (lax.axis_index("hidden") & 1))
    value = dot(z.order(), total.astype(BF16), DOWN)
    low = 0
    for out in outs:
        out[...] = value[low:low + out.shape[0]].astype(BF16)
        low += out.shape[0]


def second_kernel(z, pair_ref, out):
    out[...] = pair_ref[...].astype(F32)[z.piece:].astype(BF16)


def combine_kernel(z, tick, last, weight_ref, rows_ref, kept_ref, *refs):
    count = z.groups * z.pieces
    returned, refs = [ref[...].astype(F32)[:z.piece] for ref in refs[:count]], refs[count:]
    stacked = []
    for piece in range(z.pieces):
        values = [returned[group * z.pieces + piece] for group in range(z.groups)]
        for step in range(z.peers // z.pieces):
            stacked += [value[step * z.pay:(step + 1) * z.pay] for value in values]
    stacked = jnp.concatenate(stacked, axis=0).astype(BF16)
    mixed = dot(weight_ref[...], stacked, DOWN)
    value = (rows_ref[...].astype(F32) + mixed).astype(BF16)
    if last:
        refs[0][...] = jnp.where(lax.axis_index("section") == tick, value, kept_ref[...])
        return
    routes_ref, out, outs = refs[0], refs[1], refs[2:]
    out[...] = jnp.where(lax.axis_index("section") == tick, value, kept_ref[...])
    hits, _, _ = slot_hits(z, routes_ref)
    send_rows(z, hits, value, outs, range(z.near, z.pieces))


def after_waits(waits, kernel, *refs):
    return kernel(*refs[waits:])


def call(kernel, sizes, megabytes, outs, in_specs, scratch, *args, waits=()):
    results = pl.pallas_call(
        functools.partial(after_waits, len(waits), functools.partial(kernel, *sizes)),
        out_shape=outs,
        in_specs=[VMEM] * len(waits) + in_specs,
        out_specs=[VMEM] * len(outs),
        scratch_shapes=scratch,
        compiler_params=pltpu.CompilerParams(vmem_limit_bytes=megabytes * 2**20),
    )(*waits, *args)
    return list(results)


def on_device(tokens, gate_up, down_proj, routes, gate_weights):
    sections = lax.axis_size("section")
    z = Sizes(tokens, gate_up, lax.axis_size("expert"), lax.axis_size("hidden"))
    parts = 2 if z.width % 256 == 0 else 1
    shape = jax.ShapeDtypeStruct
    pay = shape((z.piece, z.width), BF16)
    all_pay = shape((z.all_piece, z.width), BF16)
    merged = [pay, pay, shape((2 * z.piece, z.width), BF16)]
    whole = shape((z.rows, z.width), BF16)
    steps = sorted(range(z.peers), key=lambda step: -step.bit_length())

    def swap(value, step):
        pairs = [(i, i ^ step) for i in range(z.splits)]
        return lax.ppermute(value, "hidden", pairs)

    def exchanged(pieces):
        if z.pieces == 1:
            return [lax.all_to_all(pieces[0], "expert", split_axis=0, concat_axis=0, tiled=True)]
        result = list(pieces)
        for step in steps[:-1]:
            pairs = [(i, i ^ step) for i in range(z.peers)]
            result[step] = lax.ppermute(pieces[step], "expert", pairs)
        return result

    def across(value, step):
        return lax.ppermute(value, "expert", [(i, i ^ step) for i in range(z.peers)])

    def sent_back(pieces, group):
        if group >= z.pairs:
            return exchanged(pieces)
        own, near, far = pieces
        far = across(far, 2)
        second = call(second_kernel, (z,), 2, [pay], [VMEM], [], far)[0]
        return [own, across(near, 1), far, across(second, 1)]

    def within(value, step, section):
        low = section * z.peers
        pairs = [(low + i, low + (i ^ step)) for i in range(z.peers)]
        return lax.ppermute(value, ("section", "expert"), pairs)

    def relayed(pieces, kept, tick):
        hop = [(tick, tick + 1)]
        rows = lax.ppermute(kept, "section", hop)
        if z.pieces == 1:
            return rows, [lax.ppermute(exchanged(pieces)[0], "section", hop)]
        far = {}
        for step in steps:
            if step >= z.near:
                pairs = [(tick * z.peers + i, (tick + 1) * z.peers + (i ^ step)) for i in range(z.peers)]
                far[step] = lax.ppermute(pieces[step - z.near], ("section", "expert"), pairs)
        result = call(near_kernel, (z,), 4, [all_pay] * z.near, [VMEM] * 2, [], routes, rows)
        for step in range(1, z.near):
            result[step] = within(result[step], step, tick + 1)
        return rows, result + [far[step] for step in range(z.near, z.pieces)]

    def products(received, group, waits):
        own, *sent = call(
            up_kernel, (z, group), 6,
            [shape(z.partial, F32)] + [shape((z.partial[0] // CUTS, z.partial[1]), BF16)] * CUTS,
            [VMEM] * (z.members + z.pieces),
            [
                pltpu.VMEM((z.members, 2 * z.each, 2 * z.width), BF16),
            ],
            *wide[group * z.members:(group + 1) * z.members], *(received[step] for step in z.listed),
            waits=waits,
        )
        return own, [swap(value, 1) for value in sent]

    def pair_sums(own, other):
        pair = call(
            pair_kernel, (z,), 2, [shape((z.group_each + EXTRA // 2, 2 * z.half), BF16)], [VMEM] * (1 + CUTS), [], own, *other
        )[0]
        return [pair] + [swap(pair, step) for step in range(2, z.splits, 2)]

    def activated(pairs, waits):
        count = 1
        units = call(
            act_kernel, (z, count), 2,
            [shape((z.group_each // count, z.half), BF16)] * count, [VMEM] * len(pairs), [], *pairs, waits=waits,
        )
        return units, [swap(part, 1) for part in units]

    def down(halves, group, hand_on):
        own = call(
            own_down_kernel, (z,), 4, [shape((z.group_each, z.width), F32)],
            [VMEM] * (z.members + len(halves[0])), [], *tall[group], *halves[0],
        )[0]
        return call(
            down_kernel, (z, len(hand_on)), 4,
            (merged if group < z.pairs else [pay] * z.pieces)
            + [shape(value.shape, value.dtype) for value in hand_on],
            [VMEM] * (z.members + 1 + len(halves[1]) + len(hand_on)), [],
            *tall[group], *halves[1], own, *hand_on,
        )

    routes = routes[0].transpose(0, 2, 1)
    gates = gate_weights[0].transpose(0, 2, 1)
    rows = tokens.reshape(z.rows, z.width)
    kept = rows
    *sent, weight = call(
        pack_kernel, (z,), 3,
        [all_pay] * z.pieces + [shape((z.all_pay, z.rows), BF16)],
        [HBM] * 3,
        [
            pltpu.VMEM(routes.shape, routes.dtype),
            pltpu.VMEM(gates.shape, gates.dtype),
            pltpu.VMEM(rows.shape, rows.dtype),
            pltpu.SemaphoreType.DMA((3,)),
        ],
        *(pltpu.with_memory_space_constraint(value, pltpu.HBM) for value in (routes, gates, rows)),
    )
    received = exchanged(sent)
    gate_up = pltpu.with_memory_space_constraint(gate_up, pltpu.HBM)
    down_proj = pltpu.with_memory_space_constraint(down_proj, pltpu.HBM)
    def load(experts, after):
        return call(
            load_kernel, (z, parts, experts), 1,
            [pltpu.VMEM((2 * z.width, z.units), BF16)] * len(experts),
            [HBM], [pltpu.SemaphoreType.DMA((len(experts) * parts,))], gate_up, waits=[after],
        )

    wide = load(range(z.local), weight)

    def load_down(group, after):
        return call(
            load_down_kernel, (z, group), 1,
            [pltpu.VMEM((z.units, z.width), BF16)] * z.members,
            [HBM], [pltpu.SemaphoreType.DMA((z.members,))], down_proj, waits=[after],
        )

    tall = [load_down(0, wide[-1])]
    groups = range(z.groups)
    for tick in range(sections):
        last = tick == sections - 1
        sums, returned = [], []
        for group in groups:
            own, other = products(received, group, [sums[-1][0]] if group else tall[0][:1])
            sums.append(pair_sums(own, other))
            if group == 0:
                halves = activated(sums[0], [])
        for group in groups:
            if group and tick == 0:
                tall.append(load_down(group, outgoing[0]))
            if group:
                halves = activated(sums[group], tall[group][:1] if tick == 0 else outgoing[:1])
            hand_on = [routes] if tick == 0 and group == z.groups - 1 else []
            outgoing = down(halves, group, hand_on)
            if hand_on:
                pairs = [(i + 1, i) for i in range(sections - 1)]
                following = lax.ppermute(outgoing.pop(), "section", pairs)
            returned.append(sent_back(outgoing, group))
        returned = sum(returned, [])
        kept, *sent = call(
            combine_kernel, (z, tick, last), 4,
            [whole] if last else [whole] + [all_pay] * (z.pieces - z.near),
            [VMEM] * (3 + len(returned) + (not last)), [],
            weight, rows, kept, *returned, *([] if last else [following]),
        )
        if not last:
            rows, received = relayed(sent, kept, tick)
            wide[0:1] = load(range(0, 1), kept)
    return kept.reshape(1, z.micro, z.tok, z.width)


def solution(mesh):
    placed = (
        P(None, "expert", "hidden"),
        P("section", "hidden", None, "expert"),
        P("section", "expert", "hidden"),
        P("section", None, "expert", None),
        P("section", None, "expert", None),
    )
    return jax.shard_map(
        on_device,
        mesh=mesh,
        in_specs=placed,
        out_specs=P("section", None, "expert", "hidden"),
        check_vma=False,
    )
```
